32 devices in a mesh: dp: 8 (over z, y), mp: 4 (over x, core).
Axes of the slice: x: 2, y: 2, z: 4, core: 2. Of those that a mesh axis runs over, the one named last changes fastest.
Arguments:
- tokens: bfloat16 [8192, 2048], P(('dp', 'mp')), may hold values from -6 to 6
- cotangent: bfloat16 [8192, 2048], P(('dp', 'mp')), may hold values from -6 to 6
- qkv_weight: float32 [3, 2048, 2048], P(None, 'dp', 'mp'), may hold values from -0.1875 to 0.1875
- qkv_first: float32 [3, 2048, 2048], P(None, 'dp', 'mp'), may hold values from -64 to 64
- qkv_second: float32 [3, 2048, 2048], P(None, 'dp', 'mp'), may hold values from 4.096 to 65.536
- dense_weight: float32 [2048, 2048], P('mp', 'dp'), may hold values from -0.5 to 0.5
- dense_first: float32 [2048, 2048], P('mp', 'dp'), may hold values from -16 to 16
- dense_second: float32 [2048, 2048], P('mp', 'dp'), may hold values from 0.36864 to 5.89824
- up_weight: float32 [2048, 8192], P('dp', 'mp'), may hold values from -0.125 to 0.125
- up_first: float32 [2048, 8192], P('dp', 'mp'), may hold values from -16 to 16
- up_second: float32 [2048, 8192], P('dp', 'mp'), may hold values from 0.24576 to 4.096
- down_weight: float32 [8192, 2048], P('mp', 'dp'), may hold values from -0.0625 to 0.0625
- down_first: float32 [8192, 2048], P('mp', 'dp'), may hold values from -32 to 32
- down_second: float32 [8192, 2048], P('mp', 'dp'), may hold values from 1.47456 to 23.7568
- head_bias: float32 [3, 2048], P(None, 'mp'), may hold values from -0.625 to 0.625
- head_first: float32 [3, 2048], P(None, 'mp'), may hold values from -48 to 48
- head_second: float32 [3, 2048], P(None, 'mp'), may hold values from 2.62144 to 41.7792
- hidden_bias: float32 [8192], P('mp'), may hold values from -0.625 to 0.625
- hidden_first: float32 [8192], P('mp'), may hold values from -16 to 16
- hidden_second: float32 [8192], P('mp'), may hold values from 0.24576 to 4.096
- outer_params: float32 [4, 2048], replicated, may hold values from -0.4 to 1.5, as said below
- outer_first: float32 [4, 2048], replicated, may hold values from -96 to 96
- outer_second: float32 [4, 2048], replicated, may hold values from 9.0112 to 147.456
Outputs:
- layer_out: bfloat16 [8192, 2048], P(('dp', 'mp'))
- input_grad: float32 [8192, 2048], P(('dp', 'mp'))
- new_qkv: float32 [3, 2048, 2048], P(None, 'dp', 'mp')
- new_qkv_first: float32 [3, 2048, 2048], P(None, 'dp', 'mp')
- new_qkv_second: float32 [3, 2048, 2048], P(None, 'dp', 'mp')
- new_dense: float32 [2048, 2048], P('mp', 'dp')
- new_dense_first: float32 [2048, 2048], P('mp', 'dp')
- new_dense_second: float32 [2048, 2048], P('mp', 'dp')
- new_up: float32 [2048, 8192], P('dp', 'mp')
- new_up_first: float32 [2048, 8192], P('dp', 'mp')
- new_up_second: float32 [2048, 8192], P('dp', 'mp')
- new_down: float32 [8192, 2048], P('mp', 'dp')
- new_down_first: float32 [8192, 2048], P('mp', 'dp')
- new_down_second: float32 [8192, 2048], P('mp', 'dp')
- new_head_bias: float32 [3, 2048], P(None, 'mp')
- new_head_first: float32 [3, 2048], P(None, 'mp')
- new_head_second: float32 [3, 2048], P(None, 'mp')
- new_hidden_bias: float32 [8192], P('mp')
- new_hidden_first: float32 [8192], P('mp')
- new_hidden_second: float32 [8192], P('mp')
- new_outer: float32 [4, 2048], replicated
- new_outer_first: float32 [4, 2048], replicated
- new_outer_second: float32 [4, 2048], replicated
The draws below stay inside these ranges and needn't reach their ends.
Inputs may be any that keep to these rules, and one draw needn't show every extreme that they name: `outer_params`: row 0, the norm's gain, lies between 0.5 and 1.5; rows 1 to 3 lie between -0.4 and 0.4.
All inputs are finite; a program needn't handle non-finite values.
Results may differ from the reference program's by a relative error of at most 0.0045.
The reference program's roundings to bfloat16 on the way count: a program that leaves them out, or rounds other values in their place, can miss the bound.
Values may be sent and summed in bfloat16 or wider, within the bound.
A program may use at most 136 MiB of HBM per device.

```python
import math
import jax
import jax.numpy as jnp
from jax import lax

D = 2048
HEADS = 32
FF = 8192
HEAD = 64
ROT = 32
SEQ = 1024
TOKENS = 8192
STEP = 10
N_DP = 8


def draw_outer_params(key, part):
    key = jax.random.fold_in(key, 7)
    gain_key, bias_key = jax.random.split(key)
    gain_row = 1.0 + 0.15 * jnp.clip(jax.random.normal(gain_key, (1, D), jnp.float32), -3.0, 3.0)
    bias_rows = 0.1 * jnp.clip(jax.random.normal(bias_key, (3, D), jnp.float32), -4.0, 4.0)
    return jnp.concatenate([gain_row, bias_rows], axis=0)


def spiked(array, key, source, target, shards_of, factor):
    def block_of(position):
        return (jnp.arange(array.shape[position]) // (array.shape[position] // shards_of)).reshape((-1,) + (1,) * (array.ndim - 1 - position))

    first = jax.random.permutation(key, shards_of)[block_of(target)]
    far = (block_of(target) + shards_of // 2) % shards_of
    return jnp.where((block_of(source) == first) | (block_of(source) == far), factor * array, array)


def block_scale(key, extent, cuts, low, high):
    gain, own = 1.0, jax.random.fold_in(key, 6)
    for position, blocks in cuts:
        draws = jnp.exp(jax.random.uniform(jax.random.fold_in(own, position), (blocks,), jnp.float32, low / len(cuts), high / len(cuts)))
        gain = gain * jnp.repeat(draws, extent[position] // blocks).reshape([-1 if axis == position else 1 for axis in range(len(extent))])
    return gain


def normal_values(key, dims, spread, most, cuts=(), kind=jnp.bfloat16):
    values = spread * jax.random.normal(key, dims, jnp.float32)
    if cuts:
        values = values * block_scale(key, dims, cuts, -0.22, 0.18)
    return jnp.clip(values, -most, most).astype(kind)


def heavy_noise(stream_key, extent, width, most, cuts, heavy, kind=jnp.bfloat16):
    values = width * jax.random.normal(stream_key, extent, jnp.float32)
    if cuts:
        values = values * block_scale(stream_key, extent, cuts, -0.22, 0.18)
    return jnp.clip(spiked(values, jax.random.fold_in(stream_key, 3), *heavy), -most, most).astype(kind)


def setup_inputs(seed: int = 0) -> dict:
    splits = jax.random.split(jax.random.key(seed), 24)
    return {
        "tokens": heavy_noise(splits[0], (TOKENS, D), 1.0, 6.0, ((0, 32),), (0, 1, 32, 2.75)),
        "cotangent": heavy_noise(splits[1], (TOKENS, D), 1.0, 6.0, ((0, 32),), (0, 1, 32, 2.75)),
        "qkv_weight": normal_values(splits[2], (3, D, D), (D // 2) ** -0.5, 0.1875, ((1, 8), (2, 4)), jnp.float32),
        "qkv_first": normal_values(splits[3], (3, D, D), (0.11 * TOKENS ** 0.5), 64.0, ((1, 8), (2, 4)), jnp.float32),
        "qkv_second": jnp.clip(jnp.exp(math.log(65.536) - 2.7725887 * jax.random.uniform(splits[4], (3, D, D), jnp.float32) ** block_scale(splits[4], (3, D, D), ((1, 8), (2, 4)), -0.2, 0.2)), 4.096, 65.536),
        "dense_weight": normal_values(splits[5], (D, D), (D // 16) ** -0.5, 0.5, ((0, 4), (1, 8)), jnp.float32),
        "dense_first": normal_values(splits[6], (D, D), (0.033 * TOKENS ** 0.5), 16.0, ((0, 4), (1, 8)), jnp.float32),
        "dense_second": jnp.clip(jnp.exp(math.log(5.89824) - 2.7725887 * jax.random.uniform(splits[7], (D, D), jnp.float32) ** block_scale(splits[7], (D, D), ((0, 4), (1, 8)), -0.2, 0.2)), 0.36864, 5.89824),
        "up_weight": normal_values(splits[8], (D, FF), D ** -0.5, 0.125, ((0, 8), (1, 4)), jnp.float32),
        "up_first": normal_values(splits[9], (D, FF), (0.028 * TOKENS ** 0.5), 16.0, ((0, 8), (1, 4)), jnp.float32),
        "up_second": jnp.clip(jnp.exp(math.log(4.096) - 2.8134108 * jax.random.uniform(splits[10], (D, FF), jnp.float32) ** block_scale(splits[10], (D, FF), ((0, 8), (1, 4)), -0.2, 0.2)), 0.24576, 4.096),
        "down_weight": normal_values(splits[11], (FF, D), FF ** -0.5, 0.0625, ((0, 4), (1, 8)), jnp.float32),
        "down_first": normal_values(splits[12], (FF, D), (0.066 * TOKENS ** 0.5), 32.0, ((0, 4), (1, 8)), jnp.float32),
        "down_second": jnp.clip(jnp.exp(math.log(23.7568) - 2.779509 * jax.random.uniform(splits[13], (FF, D), jnp.float32) ** block_scale(splits[13], (FF, D), ((0, 4), (1, 8)), -0.2, 0.2)), 1.47456, 23.7568),
        "head_bias": normal_values(splits[14], (3, D), 0.1, 0.625, ((1, 4),), jnp.float32),
        "head_first": normal_values(splits[15], (3, D), (0.09 * TOKENS ** 0.5), 48.0, ((1, 4),), jnp.float32),
        "head_second": jnp.clip(jnp.exp(math.log(41.7792) - 2.7686749 * jax.random.uniform(splits[16], (3, D), jnp.float32) ** block_scale(splits[16], (3, D), ((1, 4),), -0.2, 0.2)), 2.62144, 41.7792),
        "hidden_bias": normal_values(splits[17], (FF,), 0.1, 0.625, ((0, 4),), jnp.float32),
        "hidden_first": normal_values(splits[18], (FF,), (0.028 * TOKENS ** 0.5), 16.0, ((0, 4),), jnp.float32),
        "hidden_second": jnp.clip(jnp.exp(math.log(4.096) - 2.8134108 * jax.random.uniform(splits[19], (FF,), jnp.float32) ** block_scale(splits[19], (FF,), ((0, 4),), -0.2, 0.2)), 0.24576, 4.096),
        "outer_params": draw_outer_params(jax.random.fold_in(splits[23], 71), 0),
        "outer_first": normal_values(splits[21], (4, D), (0.17 * TOKENS ** 0.5), 96.0, (), jnp.float32),
        "outer_second": jnp.clip(jnp.exp(jax.random.uniform(splits[22], (4, D), jnp.float32, math.log(9.0112), math.log(147.456))), 9.0112, 147.456),
    }


PRECISE = lax.Precision.HIGHEST
BETA_ONE = 0.9
BETA_TWO = 0.999
ADAM_EPS = 1e-08
MATRIX_DECAY = 0.1
VECTOR_RATE = 0.1

@jax.custom_vjp
def low(v):
    return lax.optimization_barrier(v.astype(jnp.bfloat16)).astype(jnp.float32)

@jax.custom_vjp
def low_back(v):
    return v

def low_keep(v):
    return (low(v), None)

def low_pass(kept, grad):
    return (grad,)

def back_keep(v):
    return (v, None)

def back_low(kept, grad):
    return (low(grad),)
low.defvjp(low_keep, low_pass)
low_back.defvjp(back_keep, back_low)

def normalize(inputs, scales, offsets):
    average = lax.optimization_barrier(jnp.mean(inputs, axis=-1, keepdims=True))
    centred = inputs - average
    variance = lax.optimization_barrier(jnp.mean(centred * centred, axis=-1, keepdims=True))
    return centred * lax.rsqrt(variance + 1e-05) * scales + offsets

def rotation(positions):
    exponent = jnp.arange(ROT // 2, dtype=jnp.float32) * (2.0 / ROT)
    inverse = jnp.exp(-math.log(10000.0) * exponent)
    angles = positions[:, None] * inverse[None, :]
    return (jnp.cos(angles)[:, None, :], jnp.sin(angles)[:, None, :])

def rotate(pieces, cos_table, sin_table):
    first_half = pieces[..., :ROT // 2]
    second_half = pieces[..., ROT // 2:ROT]
    return jnp.concatenate([first_half * cos_table - second_half * sin_table, second_half * cos_table + first_half * sin_table, pieces[..., ROT:]], axis=-1)

def attend(seq_qkv):
    queries = seq_qkv[0]
    key_rows = seq_qkv[1]
    values = seq_qkv[2]
    scores = low_back(jnp.einsum('qhd,khd->hqk', queries, key_rows, precision=PRECISE) * HEAD ** (-0.5))
    positions = jnp.arange(SEQ)
    allowed = positions[None, :] <= positions[:, None]
    scores = jnp.where(allowed[None], scores, -1e+30)
    weights = jax.nn.softmax(scores, axis=-1)
    return jnp.einsum('hqk,khd->qhd', low(weights), values, precision=PRECISE)

def forward(tokens, qkv_weight, dense_weight, up_weight, down_weight, head_bias, hidden_bias, outer_params):
    normed = low(normalize(tokens, outer_params[0], outer_params[1]))
    projected = jnp.einsum('sd,tde->tse', normed, low(qkv_weight), precision=PRECISE) + head_bias[:, None, :]
    separated = low_back(projected).reshape(3, TOKENS, HEADS, HEAD)
    cos_table, sin_table = rotation((jnp.arange(TOKENS) % SEQ).astype(jnp.float32))
    turned = low(jnp.concatenate([rotate(separated[:2], cos_table, sin_table), separated[2:]], axis=0))
    per_seq = jnp.moveaxis(turned.reshape(3, N_DP, SEQ, HEADS, HEAD), 1, 0)
    mixed = lax.map(jax.checkpoint(attend), per_seq).reshape(TOKENS, D)
    mixed = low(low_back(mixed))
    hidden = low_back(jnp.dot(normed, low(up_weight), precision=PRECISE) + hidden_bias)
    activated = low(jax.nn.gelu(hidden, approximate=True))
    branch = jnp.dot(mixed, low(dense_weight), precision=PRECISE) + jnp.dot(activated, low(down_weight), precision=PRECISE)
    return tokens + branch + outer_params[2] + outer_params[3]

def adam_update(weight, moment_one, moment_two, gradient, step_rate, decay_rate):
    first_new = BETA_ONE * moment_one + (1.0 - BETA_ONE) * gradient
    second_new = BETA_TWO * moment_two + (1.0 - BETA_TWO) * gradient * gradient
    normalized = first_new / (1.0 - BETA_ONE ** STEP) / (jnp.sqrt(second_new / (1.0 - BETA_TWO ** STEP)) + ADAM_EPS)
    return (weight - step_rate * (normalized + decay_rate * weight), first_new, second_new)

def reference(tokens, cotangent, qkv_weight, qkv_first, qkv_second, dense_weight, dense_first, dense_second, up_weight, up_first, up_second, down_weight, down_first, down_second, head_bias, head_first, head_second, hidden_bias, hidden_first, hidden_second, outer_params, outer_first, outer_second):
    result, pullback = jax.vjp(forward, tokens.astype(jnp.float32), qkv_weight, dense_weight, up_weight, down_weight, head_bias, hidden_bias, outer_params)
    input_grad, qkv_grad, dense_grad, up_grad, down_grad, head_grad, hidden_grad, outer_grad = pullback(cotangent.astype(jnp.float32))
    new_qkv, new_qkv_first, new_qkv_second = adam_update(qkv_weight, qkv_first, qkv_second, qkv_grad, (D // 2) ** (-0.5), MATRIX_DECAY)
    new_dense, new_dense_first, new_dense_second = adam_update(dense_weight, dense_first, dense_second, dense_grad, (D // 16) ** (-0.5), MATRIX_DECAY)
    new_up, new_up_first, new_up_second = adam_update(up_weight, up_first, up_second, up_grad, D ** (-0.5), MATRIX_DECAY)
    new_down, new_down_first, new_down_second = adam_update(down_weight, down_first, down_second, down_grad, FF ** (-0.5), MATRIX_DECAY)
    new_head_bias, new_head_first, new_head_second = adam_update(head_bias, head_first, head_second, head_grad, VECTOR_RATE, 0.0)
    new_hidden_bias, new_hidden_first, new_hidden_second = adam_update(hidden_bias, hidden_first, hidden_second, hidden_grad, VECTOR_RATE, 0.0)
    new_outer, new_outer_first, new_outer_second = adam_update(outer_params, outer_first, outer_second, outer_grad, VECTOR_RATE, 0.0)
    return (result.astype(jnp.bfloat16), input_grad, new_qkv, new_qkv_first, new_qkv_second, new_dense, new_dense_first, new_dense_second, new_up, new_up_first, new_up_second, new_down, new_down_first, new_down_second, new_head_bias, new_head_first, new_head_second, new_hidden_bias, new_hidden_first, new_hidden_second, new_outer, new_outer_first, new_outer_second)
```

```python
import functools
import math

import jax
import jax.numpy as jnp
import numpy as np
from jax import lax
from jax.experimental import pallas as pl
from jax.experimental.pallas import tpu as pltpu
from jax.sharding import Mesh
from jax.sharding import PartitionSpec as P

HEAD = 64
ROT = 32
STEP = 10

BETA_ONE = 0.9
BETA_TWO = 0.999
ADAM_EPS = 1e-08
MATRIX_DECAY = 0.1
VECTOR_RATE = 0.1

F32 = jnp.float32
BF16 = jnp.bfloat16
MESH = pl.DeviceIdType.MESH
ANY = pl.BlockSpec(memory_space=pl.ANY)
VMEM_LIMIT = 52 * 1024 * 1024


def gather_kernel(n_zh, n_ref, c_ref, *refs):
    halves = refs[:8]
    n_all, c_all = refs[8:10]
    full = refs[10:14]
    w_send, w_recv, y_send, y_recv, a_send, a_recv, local_sem = refs[14:]
    zh, zp, y = lax.axis_index("zh"), lax.axis_index("zp"), lax.axis_index("y")
    x, c = lax.axis_index("x"), lax.axis_index("c")
    mp = x * 2 + c
    steps = [(s, f) for s in range(n_zh) for f in (0, 1)]

    def block_of(s, f):
        return lax.rem(zh - s + n_zh, n_zh) * 4 + (zp ^ f) * 2 + y

    def target(s, f):
        return {"zh": lax.rem(zh + s, n_zh), "zp": zp ^ f}

    barrier = pltpu.get_barrier_semaphore()
    partners = [target(s, f) for s, f in steps[1:]] + [{"y": 1 - y}, {"x": 1 - x}, {"c": 1 - c}]
    for partner in partners:
        pl.semaphore_signal(barrier, inc=1, device_id=partner, device_id_type=MESH)
    pl.semaphore_wait(barrier, len(partners))

    def remote(src, dst, send, recv, to):
        return pltpu.make_async_remote_copy(
            src_ref=src, dst_ref=dst, send_sem=send, recv_sem=recv, device_id=to, device_id_type=MESH
        )

    me = block_of(0, 0)
    locals_ = [
        pltpu.make_async_copy(n_ref, n_all.at[zp, mp], local_sem.at[0]),
        pltpu.make_async_copy(c_ref, c_all.at[zp, mp], local_sem.at[1]),
    ]
    for w in range(4):
        locals_.append(pltpu.make_async_copy(halves[2 * w], full[w].at[me], local_sem.at[2 + w]))
    started = []

    def go(copy):
        copy.start()
        started.append(copy)
        return copy

    def z_copy(w, i):
        s, f = steps[i]
        return remote(halves[2 * w + f], full[w].at[me], w_send.at[w, i], w_recv.at[w, i], target(s, f))

    def y_copy(w, i):
        s, f = steps[i]
        src = halves[2 * w] if i == 0 else full[w].at[block_of(s, f)]
        return remote(src, full[w].at[block_of(s, f)], y_send.at[w, i], y_recv.at[w, i], {"y": 1 - y})

    def act_copy(k, stage, part):
        own, every = ((n_ref, n_all), (c_ref, c_all))[k]
        if stage == 0:
            return remote(own, every.at[zp, mp], a_send.at[k, 0], a_recv.at[k, 0], {"zp": 1 - zp})
        row = zp ^ (part % 2)
        column = mp if part < 2 else (1 - x) * 2 + c
        src = own if part == 0 else every.at[row, column]
        slot = 1 + part if stage == 1 else 3 + part
        to = {"x": 1 - x} if stage == 1 else {"c": 1 - c}
        return remote(src, every.at[row, column], a_send.at[k, slot], a_recv.at[k, slot], to)

    for k in (0, 1):
        go(act_copy(k, 0, 0))
        go(act_copy(k, 1, 0))
    for w in (0, 1):
        for i in range(1, len(steps)):
            go(z_copy(w, i))
        go(y_copy(w, 0))
    for copy in locals_:
        copy.start()
    for k in (0, 1):
        go(act_copy(k, 2, 0))

    for k in (0, 1):
        act_copy(k, 0, 0).wait_recv()
        go(act_copy(k, 1, 1))
        go(act_copy(k, 2, 1))
    for w in range(4):
        for i in range(1, len(steps)):
            z_copy(w, i).wait_recv()
            go(y_copy(w, i))
        if w + 2 < 4:
            for i in range(1, len(steps)):
                go(z_copy(w + 2, i))
            go(y_copy(w + 2, 0))
        if w < 2:
            for part in (0, 1):
                act_copy(w, 1, part).wait_recv()
                go(act_copy(w, 2, 2 + part))
    for k in (0, 1):
        for part in range(4):
            act_copy(k, 2, part).wait_recv()
    for w in range(4):
        for i in range(len(steps)):
            y_copy(w, i).wait_recv()
    for copy in started:
        copy.wait_send()
    for copy in locals_:
        copy.wait()


def gather(n_zh, normed, cotangent, halves):
    rows, width = normed.shape
    dp = 4 * n_zh
    outs = [jax.ShapeDtypeStruct((2, 4, rows, width), BF16)] * 2
    outs += [jax.ShapeDtypeStruct((dp,) + halves[2 * w].shape, BF16) for w in range(4)]
    count = 2 * n_zh
    dma = pltpu.SemaphoreType.DMA
    return pl.pallas_call(
        functools.partial(gather_kernel, n_zh),
        out_shape=outs,
        in_specs=[ANY] * 10,
        out_specs=[ANY] * 6,
        scratch_shapes=[
            dma((4, count)),
            dma((4, count)),
            dma((4, count)),
            dma((4, count)),
            dma((2, 7)),
            dma((2, 7)),
            dma((6,)),
        ],
        compiler_params=pltpu.CompilerParams(collective_id=0, has_side_effects=True),
    )(normed, cotangent, *halves)


def mlp_kernel(n_ref, c_ref, up_ref, down_ref, bias_ref, act_ref, grad_ref, sum_ref):
    chunk = 256
    rows = n_ref[...]
    back = c_ref[...]

    @pl.when(pl.program_id(0) == 0)
    def _():
        sum_ref[...] = jnp.zeros_like(sum_ref)

    for j in range(up_ref.shape[1] // chunk):
        cols = pl.ds(j * chunk, chunk)
        hidden = jnp.dot(rows, up_ref[:, cols], preferred_element_type=F32) + bias_ref[:, cols]
        grad = jnp.dot(back, down_ref[:, cols], preferred_element_type=F32)
        k0 = math.sqrt(2.0 / math.pi)
        square = hidden * hidden
        tanh = jnp.tanh(k0 * (hidden * (1.0 + 0.044715 * square)))
        act_ref[:, cols] = (0.5 * hidden * (1.0 + tanh)).astype(BF16)
        slope = 0.5 * (1.0 + tanh) + 0.5 * hidden * (1.0 - tanh * tanh) * (
            k0 * (1.0 + 3.0 * 0.044715 * square)
        )
        low = (grad * slope).astype(BF16)
        grad_ref[:, cols] = low
        sum_ref[:, cols] += jnp.sum(low.astype(F32), axis=0, keepdims=True)


def mlp(normed, back, up, down_t, bias):
    tokens, width = normed.shape
    units = up.shape[1]
    tile = 512
    rows = pl.BlockSpec((tile, width), lambda i: (i, 0))
    whole = pl.BlockSpec((width, units), lambda i: (0, 0))
    one = pl.BlockSpec((1, units), lambda i: (0, 0))
    out = pl.BlockSpec((tile, units), lambda i: (i, 0))
    return pl.pallas_call(
        mlp_kernel,
        grid=(tokens // tile,),
        out_shape=[
            jax.ShapeDtypeStruct((tokens, units), BF16),
            jax.ShapeDtypeStruct((tokens, units), BF16),
            jax.ShapeDtypeStruct((1, units), F32),
        ],
        in_specs=[rows, rows, whole, whole, one],
        out_specs=[out, out, one],
        compiler_params=pltpu.CompilerParams(vmem_limit_bytes=VMEM_LIMIT),
        cost_estimate=pl.CostEstimate(
            flops=4 * tokens * width * units,
            bytes_accessed=4 * width * (tokens + units) + 4 * tokens * units,
            transcendentals=tokens * units,
        ),
    )(normed, back, up, down_t, bias)


def turn(values, cos, sin_up, sin_down):
    lanes = values.shape[-1]
    after = pltpu.roll(values, lanes - ROT // 2, 1)
    before = pltpu.roll(values, ROT // 2, 1)
    return values * cos + after * sin_up + before * sin_down


def attention_kernel(
    proj_ref, bias_ref, grad_ref, cos_ref, up_ref, down_ref,
    mixed_ref, out_ref, sum_ref,
    q_s, k_s, v_s, dq_s, dk_s, dv_s, s_s, p_s,
):
    seq = proj_ref.shape[1]
    width = proj_ref.shape[2] // 3
    lanes = 2 * HEAD
    block = 256
    count = seq // block
    scale = HEAD ** (-0.5)
    cos, sin_up, sin_down = cos_ref[...], up_ref[...], down_ref[...]
    first = lax.broadcasted_iota(jnp.int32, (1, lanes), 1) < HEAD
    diagonal = lax.broadcasted_iota(jnp.int32, (block, block), 0) <= lax.broadcasted_iota(
        jnp.int32, (block, block), 1
    )
    tn = (((0,), (0,)), ((), ()))
    nt = (((1,), (1,)), ((), ()))

    def pair(hp, carry):
        def cols(t):
            return pl.ds(pl.multiple_of(t * width + hp * lanes, lanes), lanes)

        here = pl.ds(pl.multiple_of(hp * lanes, lanes), lanes)

        def load(t):
            return proj_ref[0, :, cols(t)] + bias_ref[:, cols(t)]

        q_s[...] = turn(load(0), cos, sin_up, sin_down).astype(BF16)
        k_s[...] = turn(load(1), cos, sin_up, sin_down).astype(BF16)
        v_s[...] = load(2).astype(BF16)
        dk_s[...] = jnp.zeros_like(dk_s)
        dv_s[...] = jnp.zeros_like(dv_s)
        for qb in range(count):
            rows = pl.ds(qb * block, block)
            q_rows = q_s[rows, :] * jnp.asarray(scale, BF16)
            g_rows = grad_ref[0, rows, here]
            mixed_halves, dq_halves = [], []
            for h in (0, 1):
                mine = first if h == 0 else jnp.logical_not(first)
                q_one = jnp.where(mine, q_rows, jnp.zeros_like(q_rows))
                g_one = jnp.where(mine, g_rows, jnp.zeros_like(g_rows))
                top = None
                for j in range(qb + 1):
                    scores = lax.dot_general(
                        k_s[pl.ds(j * block, block), :], q_one, nt, preferred_element_type=F32
                    )
                    if j == qb:
                        scores = jnp.where(diagonal, scores, -1e30)
                    s_s[h, j] = scores
                    peak = jnp.max(scores, axis=0, keepdims=True)
                    top = peak if top is None else jnp.maximum(top, peak)
                total = None
                for j in range(qb + 1):
                    e = jnp.exp(s_s[h, j] - top)
                    s_s[h, j] = e
                    part = jnp.sum(e, axis=0, keepdims=True)
                    total = part if total is None else total + part
                inverse = 1.0 / total
                mixed, inner = None, None
                for j in range(qb + 1):
                    keys = pl.ds(j * block, block)
                    probs = s_s[h, j] * inverse
                    low = probs.astype(BF16)
                    part = lax.dot_general(low, v_s[keys, :], tn, preferred_element_type=F32)
                    mixed = part if mixed is None else mixed + part
                    dv_s[h, keys, :] += jnp.dot(low, g_rows, preferred_element_type=F32)
                    grad_probs = lax.dot_general(v_s[keys, :], g_one, nt, preferred_element_type=F32)
                    s_s[h, j] = probs
                    p_s[h, j] = grad_probs
                    part = jnp.sum(probs * grad_probs, axis=0, keepdims=True)
                    inner = part if inner is None else inner + part
                dq = None
                for j in range(qb + 1):
                    keys = pl.ds(j * block, block)
                    grad_scores = (s_s[h, j] * (p_s[h, j] - inner)).astype(BF16)
                    part = lax.dot_general(grad_scores, k_s[keys, :], tn, preferred_element_type=F32)
                    dq = part if dq is None else dq + part
                    dk_s[h, keys, :] += jnp.dot(grad_scores, q_rows, preferred_element_type=F32)
                mixed_halves.append(mixed)
                dq_halves.append(dq)
            mixed_ref[0, rows, here] = jnp.where(first, *mixed_halves).astype(BF16)
            dq_s[rows, :] = jnp.where(first, *dq_halves) * scale
        gq = turn(dq_s[...], cos, -sin_up, -sin_down).astype(BF16)
        gk = turn(jnp.where(first, dk_s[0], dk_s[1]), cos, -sin_up, -sin_down).astype(BF16)
        gv = jnp.where(first, dv_s[0], dv_s[1]).astype(BF16)
        for t, g in enumerate((gq, gk, gv)):
            out_ref[0, :, cols(t)] = g
            sum_ref[0, :, cols(t)] = jnp.sum(g.astype(F32), axis=0, keepdims=True)
        return carry

    lax.fori_loop(0, width // lanes, pair, 0)


def attention(proj, bias, grad_mixed, tables):
    seqs, seq, triple = proj.shape
    width = triple // 3
    lanes = 2 * HEAD
    block = 256
    table = pl.BlockSpec((seq, lanes), lambda i: (0, 0))
    return pl.pallas_call(
        attention_kernel,
        grid=(seqs,),
        out_shape=[
            jax.ShapeDtypeStruct((seqs, seq, width), BF16),
            jax.ShapeDtypeStruct((seqs, seq, triple), BF16),
            jax.ShapeDtypeStruct((seqs, 1, triple), F32),
        ],
        in_specs=[
            pl.BlockSpec((1, seq, triple), lambda i: (i, 0, 0)),
            pl.BlockSpec((1, triple), lambda i: (0, 0)),
            pl.BlockSpec((1, seq, width), lambda i: (i, 0, 0)),
            table,
            table,
            table,
        ],
        out_specs=[
            pl.BlockSpec((1, seq, width), lambda i: (i, 0, 0)),
            pl.BlockSpec((1, seq, triple), lambda i: (i, 0, 0)),
            pl.BlockSpec((1, 1, triple), lambda i: (i, 0, 0)),
        ],
        scratch_shapes=[
            pltpu.VMEM((seq, lanes), BF16),
            pltpu.VMEM((seq, lanes), BF16),
            pltpu.VMEM((seq, lanes), BF16),
            pltpu.VMEM((seq, lanes), F32),
            pltpu.VMEM((2, seq, lanes), F32),
            pltpu.VMEM((2, seq, lanes), F32),
            pltpu.VMEM((2, seq // block, block, block), F32),
            pltpu.VMEM((2, seq // block, block, block), F32),
        ],
        compiler_params=pltpu.CompilerParams(vmem_limit_bytes=VMEM_LIMIT),
        cost_estimate=pl.CostEstimate(
            flops=40 * seqs * seq * seq * width, bytes_accessed=20 * seqs * seq * width, transcendentals=0
        ),
    )(proj, bias, grad_mixed, *tables)


def rotation_tables(seq):
    lane = np.arange(2 * HEAD) % HEAD
    exponent = (lane % (ROT // 2)).astype(np.float32) * np.float32(2.0 / ROT)
    inverse = jnp.exp(-math.log(10000.0) * jnp.asarray(exponent))
    angles = jnp.arange(seq, dtype=F32)[:, None] * inverse[None, :]
    cos, sin = jnp.cos(angles), jnp.sin(angles)
    turned = jnp.asarray(lane < ROT)[None, :]
    low = jnp.asarray(lane < ROT // 2)[None, :]
    zero = jnp.zeros_like(sin)
    return (
        jnp.where(turned, cos, 1.0),
        jnp.where(low, -sin, zero),
        jnp.where(turned & ~low, sin, zero),
    )


def normalize(inputs, scales, offsets):
    average = jnp.mean(inputs, axis=-1, keepdims=True)
    centred = inputs - average
    variance = jnp.mean(centred * centred, axis=-1, keepdims=True)
    return centred * lax.rsqrt(variance + 1e-05) * scales + offsets


def adam_update(weight, moment_one, moment_two, gradient, step_rate, decay_rate):
    first_new = BETA_ONE * moment_one + (1.0 - BETA_ONE) * gradient
    second_new = BETA_TWO * moment_two + (1.0 - BETA_TWO) * gradient * gradient
    normalized = (
        first_new
        / (1.0 - BETA_ONE**STEP)
        / (jnp.sqrt(second_new / (1.0 - BETA_TWO**STEP)) + ADAM_EPS)
    )
    return (weight - step_rate * (normalized + decay_rate * weight), first_new, second_new)


def flip(value, name):
    return lax.ppermute(value, name, [(0, 1), (1, 0)])


def pick(value, index, axis):
    return lax.dynamic_index_in_dim(value, index, axis, keepdims=False)


def z_send(value, n_zh, s, f):
    pairs = [
        (h * 2 + p, (h + s) % n_zh * 2 + (p ^ f)) for h in range(n_zh) for p in range(2)
    ]
    return lax.ppermute(value, ("zh", "zp"), pairs)


def reduce_weight(partial, n_zh):
    zh, zp, y = lax.axis_index("zh"), lax.axis_index("zp"), lax.axis_index("y")
    blocks = partial.reshape(n_zh, 2, 2, -1, partial.shape[1])
    got = flip(pick(blocks, 1 - y, 2), "y")
    summed = (pick(blocks, y, 2).astype(F32) + got.astype(F32)).astype(BF16)

    def block(s, f):
        return pick(pick(summed, lax.rem(zh + s, n_zh), 0), zp ^ f, 0)

    mine = block(0, 0).astype(F32)
    theirs = z_send(block(0, 1), n_zh, 0, 1).astype(F32)
    for s in range(1, n_zh):
        mine = mine + z_send(block(s, 0), n_zh, s, 0).astype(F32)
        theirs = theirs + z_send(block(s, 1), n_zh, s, 1).astype(F32)
    low = jnp.where(zp == 0, mine, theirs)
    high = jnp.where(zp == 0, theirs, mine)
    return jnp.stack([low, high], axis=1)


def reduce_rows(partial, tok_rows):
    zp, x, c = lax.axis_index("zp"), lax.axis_index("x"), lax.axis_index("c")
    value = partial.reshape(2, 2, 2, tok_rows, partial.shape[1])
    value = pick(value, c, 2) + flip(pick(value, 1 - c, 2).astype(BF16), "c").astype(F32)
    value = pick(value, x, 1) + flip(pick(value, 1 - x, 1).astype(BF16), "x").astype(F32)
    return pick(value, zp, 0) + flip(pick(value, 1 - zp, 0).astype(BF16), "zp").astype(F32)


def sum_over(value, n_zh, names):
    for name in names:
        if name == "zh":
            step = 1
            while step < n_zh:
                value = value + lax.ppermute(value, "zh", [(i, i ^ step) for i in range(n_zh)])
                step *= 2
        else:
            value = value + flip(value, name)
    return value


def local(
    n_zh,
    tokens, cotangent,
    qkv_weight, qkv_first, qkv_second,
    dense_weight, dense_first, dense_second,
    up_weight, up_first, up_second,
    down_weight, down_first, down_second,
    head_bias, head_first, head_second,
    hidden_bias, hidden_first, hidden_second,
    outer_params, outer_first, outer_second,
):
    zp = lax.axis_index("zp")
    tok_rows, width = tokens.shape
    seq_rows = tok_rows * 4
    bw = qkv_weight.shape[1]
    local_width = qkv_weight.shape[2]
    half_width = local_width // 2
    half_units = up_weight.shape[1] // 2

    tokens_wide = tokens.astype(F32)
    normed, norm_back = jax.vjp(normalize, tokens_wide, outer_params[0], outer_params[1])

    qkv_rows = jnp.moveaxis(qkv_weight, 0, 1).reshape(bw, 3, 2, half_width)
    qkv_rows = jnp.moveaxis(qkv_rows, 2, 1).reshape(bw, 2, 3 * half_width).astype(BF16)
    dense_rows = dense_weight.T.reshape(bw, 2, half_width).astype(BF16)
    up_rows = up_weight.reshape(bw, 2, half_units).astype(BF16)
    down_rows = down_weight.T.reshape(bw, 2, half_units).astype(BF16)
    halves = []
    for rows in (up_rows, down_rows, qkv_rows, dense_rows):
        halves += [pick(rows, zp, 1), pick(rows, 1 - zp, 1)]
    n_all, c_all, up, down_t, qkv, dense_t = gather(
        n_zh, normed.astype(BF16), cotangent, halves
    )
    n_all = n_all.reshape(2 * seq_rows, width)
    c_all = c_all.reshape(2 * seq_rows, width)
    up, down_t, qkv, dense_t = (w.reshape(width, w.shape[2]) for w in (up, down_t, qkv, dense_t))

    bias_half = pick(hidden_bias.reshape(2, 1, half_units), zp, 0)
    act, grad_hidden, hidden_part = mlp(n_all, c_all, up, down_t, bias_half)
    tn = (((0,), (0,)), ((), ()))
    nt = (((1,), (1,)), ((), ()))

    def weight_grad(left, right):
        return lax.dot_general(left, right, tn, preferred_element_type=F32).astype(BF16)

    down_sum = reduce_weight(weight_grad(c_all, act), n_zh)
    up_sum = reduce_weight(weight_grad(n_all, grad_hidden), n_zh)

    proj = jnp.dot(n_all, qkv, preferred_element_type=F32).reshape(2, seq_rows, 3 * half_width)
    grad_mixed = (
        jnp.dot(c_all, dense_t, preferred_element_type=F32)
        .astype(BF16)
        .reshape(2, seq_rows, half_width)
    )
    head_half = pick(head_bias.reshape(3, 2, half_width), zp, 1).reshape(1, 3 * half_width)
    mixed, grad_proj, head_part = attention(
        proj, head_half, grad_mixed, rotation_tables(seq_rows)
    )
    mixed = mixed.reshape(2 * seq_rows, half_width)
    grad_proj = grad_proj.reshape(2 * seq_rows, 3 * half_width)
    dense_sum = reduce_weight(weight_grad(c_all, mixed), n_zh)
    qkv_sum = reduce_weight(weight_grad(n_all, grad_proj), n_zh)

    grad_normed = reduce_rows(
        lax.dot_general(grad_hidden, up, nt, preferred_element_type=F32)
        + lax.dot_general(grad_proj, qkv, nt, preferred_element_type=F32),
        tok_rows,
    )
    branch = reduce_rows(
        lax.dot_general(act, down_t, nt, preferred_element_type=F32)
        + lax.dot_general(mixed, dense_t, nt, preferred_element_type=F32),
        tok_rows,
    )
    layer_out = (tokens_wide + branch + outer_params[2] + outer_params[3]).astype(BF16)

    input_part, gain_grad, shift_grad = norm_back(grad_normed)
    back_wide = cotangent.astype(F32)
    input_grad = back_wide + input_part
    out_bias_grad = jnp.sum(back_wide, axis=0)

    vectors = jnp.concatenate(
        [hidden_part.reshape(half_units), jnp.sum(head_part, axis=0).reshape(3 * half_width)]
    )
    both = jnp.where(
        jnp.arange(2)[:, None] == zp, vectors[None, :], jnp.zeros_like(vectors)[None, :]
    )
    both = sum_over(both, n_zh, ("zp", "y", "zh"))
    hidden_sum = both[:, :half_units].reshape(2 * half_units)
    head_sum = jnp.moveaxis(both[:, half_units:].reshape(2, 3, half_width), 0, 1).reshape(
        3, local_width
    )
    outer_sum = sum_over(
        jnp.stack([gain_grad, shift_grad, out_bias_grad]), n_zh, ("c", "x", "y", "zp", "zh")
    )
    outer_sum = jnp.concatenate([outer_sum, outer_sum[2:]], axis=0)

    model = width
    qkv_sum = qkv_sum.reshape(bw, 2, 3, half_width)
    qkv_sum = jnp.moveaxis(qkv_sum, 2, 0).reshape(3, bw, local_width)
    dense_sum = dense_sum.reshape(bw, local_width).T
    up_sum = up_sum.reshape(bw, 2 * half_units)
    down_sum = down_sum.reshape(bw, 2 * half_units).T
    new_qkv = adam_update(
        qkv_weight, qkv_first, qkv_second, qkv_sum, (model // 2) ** (-0.5), MATRIX_DECAY
    )
    new_dense = adam_update(
        dense_weight, dense_first, dense_second, dense_sum, (model // 16) ** (-0.5), MATRIX_DECAY
    )
    new_up = adam_update(up_weight, up_first, up_second, up_sum, model ** (-0.5), MATRIX_DECAY)
    new_down = adam_update(
        down_weight, down_first, down_second, down_sum, (4 * model) ** (-0.5), MATRIX_DECAY
    )
    new_head = adam_update(head_bias, head_first, head_second, head_sum, VECTOR_RATE, 0.0)
    new_hidden = adam_update(
        hidden_bias, hidden_first, hidden_second, hidden_sum, VECTOR_RATE, 0.0
    )
    new_outer = adam_update(outer_params, outer_first, outer_second, outer_sum, VECTOR_RATE, 0.0)
    return (
        layer_out,
        input_grad,
        *new_qkv,
        *new_dense,
        *new_up,
        *new_down,
        *new_head,
        *new_hidden,
        *new_outer,
    )


def solution(mesh):
    n_zh = mesh.shape["dp"] // 4
    split = Mesh(mesh.devices.reshape(n_zh, 2, 2, 2, 2), ("zh", "zp", "y", "x", "c"))
    dp, mp = ("zh", "zp", "y"), ("x", "c")
    rows = P(dp + mp, None)
    qkv, dense, up, down = P(None, dp, mp), P(mp, dp), P(dp, mp), P(mp, dp)
    rest = (qkv,) * 3 + (dense,) * 3 + (up,) * 3 + (down,) * 3
    rest += (P(None, mp),) * 3 + (P(mp),) * 3 + (P(),) * 3
    return jax.shard_map(
        functools.partial(local, n_zh),
        mesh=split,
        in_specs=(rows, rows) + rest,
        out_specs=(rows, rows) + rest,
        check_vma=False,
    )
```

```python
import functools
import math

import jax
import jax.numpy as jnp
import numpy as np
from jax import lax
from jax.experimental import pallas as pl
from jax.experimental.pallas import tpu as pltpu
from jax.sharding import Mesh
from jax.sharding import PartitionSpec as P

HEAD = 64
ROT = 32
STEP = 10

BETA_ONE = 0.9
BETA_TWO = 0.999
ADAM_EPS = 1e-08
MATRIX_DECAY = 0.1
VECTOR_RATE = 0.1

F32 = jnp.float32
BF16 = jnp.bfloat16
MESH = pl.DeviceIdType.MESH
ANY = pl.BlockSpec(memory_space=pl.ANY)
VMEM_LIMIT = 63 * 1024 * 1024


CHUNK = 256
TILE_SLOTS = 4
NT = (((1,), (1,)), ((), ()))
TN = (((0,), (0,)), ((), ()))


def at(index, size):
    return pl.ds(pl.multiple_of(index * size, size), size)


def block_kernel(
    n_zh,
    n_in, c_in, down_own, down_other, up_own, up_other, dense_own, dense_other, qkv_own, qkv_other,
    hidden_bias, head_bias, cos_ref, sin_ref,
    z_mlp, z_dense, z_qkv, y_mlp, y_dense, y_qkv, rows_in, grad_out, branch_out, hidden_sum, head_sum,
    rows2, mlp_w, dense_w, qkv_w, units2, heads3, heads1,
    dq_s, dk_s, dv_s, s_s, p_s,
    y_stage, z_stage, qkv_stage, dense_stage, tile_stage, load_s, wide_s, turned_s,
    w_send, w_recv, fwd_send, fwd_recv, a_send, a_recv, local_sem,
    ym_send, ym_recv, zm_send, zm_recv, yd_send, yd_recv, zd_send, zd_recv,
    yq_send, yq_recv, zq_send, zq_recv, tile_send, tile_recv, load_sem, wide_sem,
):
    zh, zp, y = lax.axis_index("zh"), lax.axis_index("zp"), lax.axis_index("y")
    x, c = lax.axis_index("x"), lax.axis_index("c")
    mp = x * 2 + c
    n = 2 * n_zh
    tok_rows, width = n_in.shape
    bw = up_own.shape[0]
    units = up_own.shape[1]
    half_width = dense_own.shape[1]
    seq = 4 * tok_rows
    half = width // 2
    lanes = 2 * HEAD
    count = seq // CHUNK
    scale = HEAD ** (-0.5)

    def step(i):
        back = n - 1 - i
        if isinstance(back, int):
            return back // 2, back % 2
        return lax.div(back, 2), lax.rem(back, 2)

    def source_block(i):
        s, f = step(i)
        return lax.rem(zh - s + n_zh, n_zh) * 4 + (zp ^ f) * 2 + y

    def target(i):
        s, f = step(i)
        return {"zh": lax.rem(zh + s, n_zh), "zp": zp ^ f}

    def target_block(i):
        s, f = step(i)
        return lax.rem(zh + s, n_zh) * 4 + (zp ^ f) * 2

    to_y, to_x, to_c, to_zp = {"y": 1 - y}, {"x": 1 - x}, {"c": 1 - c}, {"zp": 1 - zp}
    barrier = pltpu.get_barrier_semaphore()
    partners = [target(i) for i in range(n - 1)] + [to_y, to_x, to_c]
    for partner in partners:
        pl.semaphore_signal(barrier, inc=1, device_id=partner, device_id_type=MESH)
    pl.semaphore_wait(barrier, len(partners))

    def remote(src, dst, send, recv, to):
        return pltpu.make_async_remote_copy(
            src_ref=src, dst_ref=dst, send_sem=send, recv_sem=recv, device_id=to, device_id_type=MESH
        )


    me = source_block(n - 1)
    halves = ((down_own, down_other), (up_own, up_other), (dense_own, dense_other), (qkv_own, qkv_other))

    def place(w, b):
        if w < 2:
            return mlp_w.at[w, at(b, bw), :]
        return (dense_w, qkv_w)[w - 2].at[at(b, bw), :]

    started = []

    def go(copy):
        copy.start()
        started.append(copy)

    def z_copy(w, i):
        return remote(halves[w][step(i)[1]], place(w, me), w_send.at[w, i], w_recv.at[w, i], target(i))

    def y_copy(w, i):
        b = source_block(i)
        src = halves[w][0] if i == n - 1 else place(w, b)
        return remote(src, place(w, b), fwd_send.at[w, i], fwd_recv.at[w, i], to_y)

    own_rows = (c_in, n_in)

    def act_copy(k, stage, part):
        if stage == 0:
            slot, to, row, column = 0, to_zp, zp, mp
        else:
            row = zp ^ (part % 2)
            column = mp if part < 2 else (1 - x) * 2 + c
            slot, to = (1 + part, to_x) if stage == 1 else (3 + part, to_c)
        spot = rows2.at[k, at(row * 4 + column, tok_rows), :]
        src = own_rows[k] if stage == 0 or part == 0 else spot
        return remote(src, spot, a_send.at[k, slot], a_recv.at[k, slot], to)

    def locals_():
        copies = [
            pltpu.make_async_copy(own_rows[k], rows2.at[k, at(zp * 4 + mp, tok_rows), :], local_sem.at[k])
            for k in (0, 1)
        ]
        return copies + [
            pltpu.make_async_copy(halves[w][0], place(w, me), local_sem.at[2 + w]) for w in range(4)
        ]

    go(act_copy(1, 0, 0))
    go(act_copy(1, 1, 0))
    for i in range(n - 1):
        go(z_copy(1, i))
    go(y_copy(1, n - 1))
    go(act_copy(0, 0, 0))
    go(act_copy(0, 1, 0))
    for i in range(n - 1):
        go(z_copy(0, i))
    go(y_copy(0, n - 1))
    go(act_copy(1, 2, 0))
    go(act_copy(0, 2, 0))
    for w in (3, 2):
        for i in range(n - 1):
            go(z_copy(w, i))
    for copy in locals_():
        copy.start()

    def pass_on(k, stage, part):
        act_copy(k, stage, part).wait_recv()
        if stage == 0:
            go(act_copy(k, 1, 1))
            go(act_copy(k, 2, 1))
        else:
            go(act_copy(k, 2, 2 + part))

    def forward(w, i):
        z_copy(w, i).wait_recv()
        go(y_copy(w, i))

    pass_on(1, 0, 0)
    for i in range(n - 1):
        forward(1, i)
    pass_on(1, 1, 0)
    pass_on(0, 0, 0)
    pass_on(1, 1, 1)
    for i in range(n - 1):
        forward(0, i)
    pass_on(0, 1, 0)
    pass_on(0, 1, 1)
    go(y_copy(3, n - 1))
    go(y_copy(2, n - 1))
    for copy in locals_():
        copy.wait()
    for k in (1, 0):
        for part in range(4):
            act_copy(k, 2, part).wait_recv()
    for w in (1, 0):
        for i in range(n):
            y_copy(w, i).wait_recv()


    hidden_sum[...] = jnp.zeros_like(hidden_sum)
    events = [(w, i) for w in (3, 2) for i in range(n - 1)]
    tiles = 2 * seq // CHUNK

    def mlp_tile(r, carry):
        rows = at(r, CHUNK)
        for j in range(units // CHUNK):
            cols = pl.ds(j * CHUNK, CHUNK)
            hidden = jnp.dot(rows2[1, rows, :], mlp_w[1, :, cols], preferred_element_type=F32)
            hidden = hidden + hidden_bias[:, cols]
            grad = jnp.dot(rows2[0, rows, :], mlp_w[0, :, cols], preferred_element_type=F32)
            k0 = math.sqrt(2.0 / math.pi)
            square = hidden * hidden
            tanh = jnp.tanh(k0 * (hidden * (1.0 + 0.044715 * square)))
            units2[0, rows, cols] = (0.5 * hidden * (1.0 + tanh)).astype(BF16)
            slope = 0.5 * (1.0 + tanh) + 0.5 * hidden * (1.0 - tanh * tanh) * (
                k0 * (1.0 + 3.0 * 0.044715 * square)
            )
            low = (grad * slope).astype(BF16)
            units2[1, rows, cols] = low
            hidden_sum[:, cols] += jnp.sum(low.astype(F32), axis=0, keepdims=True)
        for r_at in range(tiles):
            mine = [e for k, e in enumerate(events) if min(k + 1, tiles - 1) == r_at]
            if mine:
                @pl.when(r == r_at)
                def _():
                    for w, i in mine:
                        z_copy(w, i).wait_recv()
                        y_copy(w, i).start()
        return carry

    lax.fori_loop(0, tiles, mlp_tile, 0)
    started.extend(y_copy(w, i) for w, i in events)


    def weight_grad(left, right, b, put):
        wide = max(bw, 128)
        turned = turned_s.at[pl.ds(0, wide), :]
        if bw == wide:
            turned[...] = left[:, at(b, bw)].T
        else:
            turned[...] = left[:, at(lax.div(b, wide // bw), wide)].T
        for j in range(right.shape[1] // CHUNK):
            cols = pl.ds(j * CHUNK, CHUNK)
            value = jnp.dot(turned[...], right[:, cols], preferred_element_type=F32)
            if bw < wide:
                spot = lax.rem(b, wide // bw)
                value = sum(
                    jnp.where(spot == k, value[k * bw : (k + 1) * bw], 0.0) for k in range(wide // bw)
                )
            put(cols, value)

    def mlp_grad(w, b, put):
        weight_grad(rows2.at[w], units2.at[w], b, put)

    def ym_copy(k):
        w, i = lax.div(k, n), lax.rem(k, n)
        return remote(y_stage.at[k], y_mlp.at[w, i], ym_send.at[k], ym_recv.at[k], to_y)

    def ym_step(k, carry):
        w, i = lax.div(k, n), lax.rem(k, n)

        def put(cols, value):
            y_stage[k, :, cols] = value.astype(BF16)

        mlp_grad(w, target_block(i) + 1 - y, put)
        ym_copy(k).start()
        return carry

    lax.fori_loop(0, 2 * n, ym_step, 0)

    def zm_copy(k):
        w, i = lax.div(k, n), lax.rem(k, n)
        return remote(z_stage.at[i], z_mlp.at[w, i], zm_send.at[i], zm_recv.at[k], target(i))

    def zm_local(k):
        w, i = lax.div(k, n), lax.rem(k, n)
        return pltpu.make_async_copy(z_stage.at[i], z_mlp.at[w, i], zm_send.at[i])

    def zm_step(k, carry):
        w, i = lax.div(k, n), lax.rem(k, n)
        ym_copy(k).wait_recv()
        load = pltpu.make_async_copy(y_mlp.at[w, i], load_s.at[0, pl.ds(0, bw), :], load_sem.at[0])
        load.start()

        @pl.when((k >= n) & (i < n - 1))
        def _():
            zm_copy(k - n).wait_send()

        @pl.when((k >= n) & (i == n - 1))
        def _():
            zm_local(k - n).wait()

        load.wait()

        def put(cols, value):
            z_stage[i, :, cols] = (value + load_s[0, pl.ds(0, bw), cols].astype(F32)).astype(BF16)

        mlp_grad(w, target_block(i) + y, put)

        @pl.when(i < n - 1)
        def _():
            zm_copy(k).start()

        @pl.when(i == n - 1)
        def _():
            zm_local(k).start()

        return carry


    for w in (3, 2):
        for i in range(n):
            y_copy(w, i).wait_recv()
    low_lane = lax.broadcasted_iota(jnp.int32, (1, lanes), 1) % HEAD < ROT // 2

    def turn(values, rows, sign):
        after = pltpu.roll(values, lanes - ROT // 2, 1)
        before = pltpu.roll(values, ROT // 2, 1)
        return values * cos_ref[rows, :] + jnp.where(low_lane, after, before) * (sign * sin_ref[rows, :])

    def proj_tile(r, carry):
        rows = at(r, CHUNK)
        where = at(lax.rem(r, count), CHUNK)
        for t in range(3):
            cols = pl.ds(t * half_width, half_width)
            proj = jnp.dot(rows2[1, rows, :], qkv_w[:, cols], preferred_element_type=F32) + head_bias[:, cols]
            for g in range(half_width // lanes):
                part = proj[:, g * lanes : (g + 1) * lanes]
                if t < 2:
                    part = turn(part, where, 1.0)
                heads3[rows, pl.ds(t * half_width + g * lanes, lanes)] = part.astype(BF16)
        heads1[rows, :] = jnp.dot(rows2[0, rows, :], dense_w[...], preferred_element_type=F32).astype(BF16)
        return carry

    lax.fori_loop(0, tiles, proj_tile, 0)


    first = lax.broadcasted_iota(jnp.int32, (1, lanes), 1) < HEAD
    pairs = half_width // lanes

    def attend(it, carry):
        base = lax.div(it, pairs) * count
        hp = lax.rem(it, pairs)

        def cols(t):
            return at(t * pairs + hp, lanes)

        here = at(hp, lanes)
        dk_s[...] = jnp.zeros_like(dk_s)
        dv_s[...] = jnp.zeros_like(dv_s)
        diagonal = lax.broadcasted_iota(jnp.int32, (CHUNK, CHUNK), 0) <= lax.broadcasted_iota(
            jnp.int32, (CHUNK, CHUNK), 1
        )
        for qb in range(count):
            rows = at(base + qb, CHUNK)
            q_rows = heads3[rows, cols(0)] * jnp.asarray(scale, BF16)
            g_rows = heads1[rows, here]
            mixed_halves, dq_halves = [], []
            for h in (0, 1):
                mine = first if h == 0 else jnp.logical_not(first)
                q_one = jnp.where(mine, q_rows, jnp.zeros_like(q_rows))
                g_one = jnp.where(mine, g_rows, jnp.zeros_like(g_rows))
                top = None
                for j in range(qb + 1):
                    keys = heads3[at(base + j, CHUNK), cols(1)]
                    scores = lax.dot_general(keys, q_one, NT, preferred_element_type=F32)
                    if j == qb:
                        scores = jnp.where(diagonal, scores, -1e30)
                    s_s[j] = scores
                    peak = jnp.max(scores, axis=0, keepdims=True)
                    top = peak if top is None else jnp.maximum(top, peak)
                total = None
                for j in range(qb + 1):
                    e = jnp.exp(s_s[j] - top)
                    s_s[j] = e
                    part = jnp.sum(e, axis=0, keepdims=True)
                    total = part if total is None else total + part
                inverse = 1.0 / total
                mixed, inner = None, None
                for j in range(qb + 1):
                    values = heads3[at(base + j, CHUNK), cols(2)]
                    probs = s_s[j] * inverse
                    low = probs.astype(BF16)
                    part = lax.dot_general(low, values, TN, preferred_element_type=F32)
                    mixed = part if mixed is None else mixed + part
                    dv_s[h, pl.ds(j * CHUNK, CHUNK), :] += jnp.dot(low, g_rows, preferred_element_type=F32)
                    grad_probs = lax.dot_general(values, g_one, NT, preferred_element_type=F32)
                    s_s[j] = probs
                    p_s[j] = grad_probs
                    part = jnp.sum(probs * grad_probs, axis=0, keepdims=True)
                    inner = part if inner is None else inner + part
                dq = None
                for j in range(qb + 1):
                    keys = heads3[at(base + j, CHUNK), cols(1)]
                    grad_scores = (s_s[j] * (p_s[j] - inner)).astype(BF16)
                    part = lax.dot_general(grad_scores, keys, TN, preferred_element_type=F32)
                    dq = part if dq is None else dq + part
                    dk_s[h, pl.ds(j * CHUNK, CHUNK), :] += jnp.dot(
                        grad_scores, q_rows, preferred_element_type=F32
                    )
                mixed_halves.append(mixed)
                dq_halves.append(dq)
            heads1[rows, here] = jnp.where(first, *mixed_halves).astype(BF16)
            dq_s[pl.ds(qb * CHUNK, CHUNK), :] = jnp.where(first, *dq_halves) * scale
        for qb in range(count):
            rows = pl.ds(qb * CHUNK, CHUNK)
            gq = turn(dq_s[rows, :], rows, -1.0)
            gk = turn(jnp.where(first, dk_s[0, rows, :], dk_s[1, rows, :]), rows, -1.0)
            gv = jnp.where(first, dv_s[0, rows, :], dv_s[1, rows, :])
            for t, g in enumerate((gq, gk, gv)):
                low = g.astype(BF16)
                heads3[at(base + qb, CHUNK), cols(t)] = low
                head_sum[:, cols(t)] += jnp.sum(low.astype(F32), axis=0, keepdims=True)
        per = n // 4
        lax.fori_loop(it * per, (it + 1) * per, zm_step, 0)
        return carry

    head_sum[...] = jnp.zeros_like(head_sum)
    lax.fori_loop(0, 2 * pairs, attend, 0)


    def small(left, right, y_buf, z_buf, stage, ys, yr, zs, zr):
        cols = stage.shape[2]

        def y_copy_(i):
            return remote(stage.at[i], y_buf.at[i], ys.at[i], yr.at[i], to_y)

        def z_copy_(i):
            return remote(stage.at[i], z_buf.at[i], zs.at[i], zr.at[i], target(i))

        def z_local(i):
            return pltpu.make_async_copy(stage.at[i], z_buf.at[i], zs.at[i])

        def y_step(i, carry):
            def put(at_cols, value):
                stage[i, :, at_cols] = value.astype(BF16)

            weight_grad(left, right, target_block(i) + 1 - y, put)
            y_copy_(i).start()
            return carry

        def z_step(i, carry):
            y_copy_(i).wait_recv()
            spot = load_s.at[0, pl.ds(0, bw), pl.ds(0, cols)]
            load = pltpu.make_async_copy(y_buf.at[i], spot, load_sem.at[0])
            load.start()
            y_copy_(i).wait_send()
            load.wait()

            def put(at_cols, value):
                stage[i, :, at_cols] = (value + spot[:, at_cols].astype(F32)).astype(BF16)

            weight_grad(left, right, target_block(i) + y, put)

            @pl.when(i < n - 1)
            def _():
                z_copy_(i).start()

            @pl.when(i == n - 1)
            def _():
                z_local(i).start()

            return carry

        def finish(i, carry):
            @pl.when(i < n - 1)
            def _():
                z_copy_(i).wait_send()
                z_copy_(i).wait_recv()

            @pl.when(i == n - 1)
            def _():
                z_local(i).wait()

            return carry

        return y_step, z_step, finish

    dense_steps = small(
        rows2.at[0], heads1, y_dense, z_dense, dense_stage, yd_send, yd_recv, zd_send, zd_recv
    )
    qkv_steps = small(
        rows2.at[1], heads3, y_qkv, z_qkv, qkv_stage, yq_send, yq_recv, zq_send, zq_recv
    )


    def tile_copy(kind, slot, index, to):
        return remote(
            tile_stage.at[slot], rows_in.at[kind, index], tile_send.at[slot],
            tile_recv.at[kind, index], to,
        )

    def row_tiles(kind, stage, base, total):
        left, left_w = units2.at[1 - kind], mlp_w.at[1 - kind]
        right, right_w = ((heads3, qkv_w), (heads1, dense_w))[kind]

        def one(t, carry):
            h = lax.rem(t, 2)
            if stage == 0:
                zq, xq = lax.div(t, 4), lax.rem(lax.div(t, 2), 2)
                block, come, to, index = zq * 4 + xq * 2 + 1 - c, (), to_c, t
            elif stage == 1:
                zq = lax.div(t, 2)
                block, to, index = zq * 4 + (1 - x) * 2 + c, to_x, 8 + t
                come = (zq * 4 + (1 - x) * 2 + h,)
            elif stage == 2:
                block, to, index = (1 - zp) * 4 + x * 2 + c, to_zp, 12 + h
                come = ((1 - zp) * 4 + x * 2 + h, 8 + (1 - zp) * 2 + h)
            else:
                block, to, index = zp * 4 + x * 2 + c, None, None
                come = (zp * 4 + x * 2 + h, 8 + zp * 2 + h, 12 + h)
            loads = []
            for slot, (spot, back) in enumerate(zip(come, (to_c, to_x, to_zp))):
                tile_copy(kind, 0, spot, back).wait_recv()
                loads.append(
                    pltpu.make_async_copy(rows_in.at[kind, spot], load_s.at[slot], load_sem.at[slot])
                )
                loads[-1].start()
            for load in loads:
                load.wait()
            rows = at(block, tok_rows)
            if stage < 3:
                slot = lax.rem(base + t, TILE_SLOTS)

                @pl.when(base + t >= TILE_SLOTS)
                def _():
                    tile_copy(kind, slot, index, to).wait_send()

            for j in range(half // CHUNK):
                cols = pl.ds(j * CHUNK, CHUNK)
                model = at(h * (half // CHUNK) + j, CHUNK)
                value = lax.dot_general(left[rows, :], left_w[model, :], NT, preferred_element_type=F32)
                value += lax.dot_general(right[rows, :], right_w[model, :], NT, preferred_element_type=F32)
                for k in range(len(loads)):
                    value += load_s[k, :, cols].astype(F32)
                if stage < 3:
                    tile_stage[slot, :, cols] = value.astype(BF16)
                else:
                    wide_s[:, cols] = value
            if stage < 3:
                tile_copy(kind, slot, index, to).start()
            else:
                out = (grad_out, branch_out)[kind]
                copy = pltpu.make_async_copy(wide_s, out.at[:, at(h, half)], wide_sem)
                copy.start()
                copy.wait()
            return carry

        lax.fori_loop(0, total, one, 0)

    lax.fori_loop(0, n, dense_steps[0], 0)
    lax.fori_loop(0, n, qkv_steps[0], 0)
    per = n // 4
    lax.fori_loop(n, n + per, zm_step, 0)
    row_tiles(0, 0, 0, 8)
    lax.fori_loop(n + per, n + 2 * per, zm_step, 0)
    row_tiles(1, 0, 8, 8)
    lax.fori_loop(n + 2 * per, n + 3 * per, zm_step, 0)
    row_tiles(0, 1, 16, 4)
    lax.fori_loop(n + 3 * per, 2 * n, zm_step, 0)
    row_tiles(1, 1, 20, 4)
    lax.fori_loop(0, n, dense_steps[1], 0)
    row_tiles(0, 2, 24, 2)
    lax.fori_loop(0, n, qkv_steps[1], 0)
    row_tiles(1, 2, 26, 2)
    row_tiles(0, 3, 0, 2)
    row_tiles(1, 3, 0, 2)


    for copy in started:
        copy.wait_send()

    def finish_y(k, carry):
        ym_copy(k).wait_send()
        return carry

    def finish_z(k, carry):
        i = lax.rem(k, n)

        @pl.when(i < n - 1)
        def _():
            zm_copy(k).wait_recv()

        @pl.when((k >= n) & (i < n - 1))
        def _():
            zm_copy(k).wait_send()

        @pl.when((k >= n) & (i == n - 1))
        def _():
            zm_local(k).wait()

        return carry

    lax.fori_loop(0, 2 * n, finish_y, 0)
    lax.fori_loop(0, 2 * n, finish_z, 0)
    for slot in range(TILE_SLOTS):
        tile_copy(0, slot, 0, to_c).wait_send()
    lax.fori_loop(0, n, dense_steps[2], 0)
    lax.fori_loop(0, n, qkv_steps[2], 0)


def block(n_zh, normed, cotangent, halves, hidden_bias, head_bias, tables):
    tok_rows, width = normed.shape
    n = 2 * n_zh
    dp = 2 * n
    bw = width // dp
    units = halves[2].shape[1]
    half_width = halves[4].shape[1]
    triple = 3 * half_width
    seq = 4 * tok_rows
    count = seq // CHUNK
    shape = jax.ShapeDtypeStruct
    vmem = pl.BlockSpec(memory_space=pltpu.VMEM)
    dma = pltpu.SemaphoreType.DMA
    outs = [
        shape((2, n, bw, units), BF16),
        shape((n, bw, half_width), BF16),
        shape((n, bw, triple), BF16),
        shape((2, n, bw, units), BF16),
        shape((n, bw, half_width), BF16),
        shape((n, bw, triple), BF16),
        shape((2, 14, tok_rows, width // 2), BF16),
        shape((tok_rows, width), F32),
        shape((tok_rows, width), F32),
        shape((1, units), F32),
        shape((1, triple), F32),
    ]
    scratch = [
        pltpu.VMEM((2, 2 * seq, width), BF16),
        pltpu.VMEM((2, width, units), BF16),
        pltpu.VMEM((width, half_width), BF16),
        pltpu.VMEM((width, triple), BF16),
        pltpu.VMEM((2, 2 * seq, units), BF16),
        pltpu.VMEM((2 * seq, triple), BF16),
        pltpu.VMEM((2 * seq, half_width), BF16),
        pltpu.VMEM((seq, 2 * HEAD), F32),
        pltpu.VMEM((2, seq, 2 * HEAD), F32),
        pltpu.VMEM((2, seq, 2 * HEAD), F32),
        pltpu.VMEM((count, CHUNK, CHUNK), F32),
        pltpu.VMEM((count, CHUNK, CHUNK), F32),
        pltpu.VMEM((2 * n, bw, units), BF16),
        pltpu.VMEM((n, bw, units), BF16),
        pltpu.VMEM((n, bw, triple), BF16),
        pltpu.VMEM((n, bw, half_width), BF16),
        pltpu.VMEM((TILE_SLOTS, tok_rows, width // 2), BF16),
        pltpu.VMEM((3, tok_rows, width // 2), BF16),
        pltpu.VMEM((tok_rows, width // 2), F32),
        pltpu.VMEM((max(bw, 128), 2 * seq), BF16),
        dma((4, n)), dma((4, n)), dma((4, n)), dma((4, n)), dma((2, 7)), dma((2, 7)), dma((6,)),
        dma((2 * n,)), dma((2 * n,)), dma((n,)), dma((2 * n,)),
        dma((n,)), dma((n,)), dma((n,)), dma((n,)),
        dma((n,)), dma((n,)), dma((n,)), dma((n,)),
        dma((TILE_SLOTS,)), dma((2, 14)), dma((3,)), dma,
    ]
    return pl.pallas_call(
        functools.partial(block_kernel, n_zh),
        out_shape=outs,
        in_specs=[ANY] * 10 + [vmem] * 4,
        out_specs=[ANY] * 9 + [vmem] * 2,
        scratch_shapes=scratch,
        compiler_params=pltpu.CompilerParams(
            collective_id=0, has_side_effects=True, vmem_limit_bytes=VMEM_LIMIT
        ),
    )(normed, cotangent, *halves, hidden_bias, head_bias, *tables)


def rotation_tables(seq):
    lane = np.arange(2 * HEAD) % HEAD
    exponent = (lane % (ROT // 2)).astype(np.float32) * np.float32(2.0 / ROT)
    inverse = jnp.exp(-math.log(10000.0) * jnp.asarray(exponent))
    angles = jnp.arange(seq, dtype=F32)[:, None] * inverse[None, :]
    cos, sin = jnp.cos(angles), jnp.sin(angles)
    turned = jnp.asarray(lane < ROT)[None, :]
    low = jnp.asarray(lane < ROT // 2)[None, :]
    return jnp.where(turned, cos, 1.0), jnp.where(turned, jnp.where(low, -sin, sin), 0.0)


def normalize(inputs, scales, offsets):
    average = jnp.mean(inputs, axis=-1, keepdims=True)
    centred = inputs - average
    variance = jnp.mean(centred * centred, axis=-1, keepdims=True)
    return centred * lax.rsqrt(variance + 1e-05) * scales + offsets


def adam_update(weight, moment_one, moment_two, gradient, step_rate, decay_rate):
    first_new = BETA_ONE * moment_one + (1.0 - BETA_ONE) * gradient
    second_new = BETA_TWO * moment_two + (1.0 - BETA_TWO) * gradient * gradient
    normalized = (
        first_new
        / (1.0 - BETA_ONE**STEP)
        / (jnp.sqrt(second_new / (1.0 - BETA_TWO**STEP)) + ADAM_EPS)
    )
    return (weight - step_rate * (normalized + decay_rate * weight), first_new, second_new)


def flip(value, name):
    return lax.ppermute(value, name, [(0, 1), (1, 0)])


def pick(value, index, axis):
    return lax.dynamic_index_in_dim(value, index, axis, keepdims=False)


def owner_sum(parts, n_zh):
    zp = lax.axis_index("zp")
    wide = parts.astype(F32)
    mine = sum(wide[2 * n_zh - 1 - 2 * s] for s in range(n_zh))
    theirs = sum(wide[2 * n_zh - 2 - 2 * s] for s in range(n_zh))
    low = jnp.where(zp == 0, mine, theirs)
    high = jnp.where(zp == 0, theirs, mine)
    return jnp.stack([low, high], axis=1)


def sum_over(value, n_zh, names):
    for name in names:
        if name == "zh":
            step = 1
            while step < n_zh:
                value = value + lax.ppermute(value, "zh", [(i, i ^ step) for i in range(n_zh)])
                step *= 2
        else:
            value = value + flip(value, name)
    return value


def local(
    n_zh,
    tokens, cotangent,
    qkv_weight, qkv_first, qkv_second,
    dense_weight, dense_first, dense_second,
    up_weight, up_first, up_second,
    down_weight, down_first, down_second,
    head_bias, head_first, head_second,
    hidden_bias, hidden_first, hidden_second,
    outer_params, outer_first, outer_second,
):
    zp = lax.axis_index("zp")
    tok_rows, width = tokens.shape
    seq_rows = tok_rows * 4
    bw = qkv_weight.shape[1]
    local_width = qkv_weight.shape[2]
    half_width = local_width // 2
    half_units = up_weight.shape[1] // 2

    tokens_wide = tokens.astype(F32)
    normed, norm_back = jax.vjp(normalize, tokens_wide, outer_params[0], outer_params[1])

    qkv_rows = jnp.moveaxis(qkv_weight, 0, 1).reshape(bw, 3, 2, half_width)
    qkv_rows = jnp.moveaxis(qkv_rows, 2, 1).reshape(bw, 2, 3 * half_width).astype(BF16)
    dense_rows = dense_weight.T.reshape(bw, 2, half_width).astype(BF16)
    up_rows = up_weight.reshape(bw, 2, half_units).astype(BF16)
    down_rows = down_weight.T.reshape(bw, 2, half_units).astype(BF16)
    halves = []
    for rows in (down_rows, up_rows, dense_rows, qkv_rows):
        halves += [pick(rows, zp, 1), pick(rows, 1 - zp, 1)]
    bias_half = pick(hidden_bias.reshape(2, 1, half_units), zp, 0)
    head_half = pick(head_bias.reshape(3, 2, half_width), zp, 1).reshape(1, 3 * half_width)
    outs = block(
        n_zh, normed.astype(BF16), cotangent, halves, bias_half, head_half, rotation_tables(seq_rows)
    )
    z_mlp, z_dense, z_qkv = outs[:3]
    grad_normed, branch, hidden_part, head_part = outs[7:]
    down_sum = owner_sum(z_mlp[0], n_zh)
    up_sum = owner_sum(z_mlp[1], n_zh)
    dense_sum = owner_sum(z_dense, n_zh)
    qkv_sum = owner_sum(z_qkv, n_zh)
    layer_out = (tokens_wide + branch + outer_params[2] + outer_params[3]).astype(BF16)

    input_part, gain_grad, shift_grad = norm_back(grad_normed)
    back_wide = cotangent.astype(F32)
    input_grad = back_wide + input_part
    out_bias_grad = jnp.sum(back_wide, axis=0)

    vectors = jnp.concatenate(
        [hidden_part.reshape(half_units), head_part.reshape(3 * half_width)]
    )
    both = jnp.where(
        jnp.arange(2)[:, None] == zp, vectors[None, :], jnp.zeros_like(vectors)[None, :]
    )
    both = sum_over(both, n_zh, ("zp", "y", "zh"))
    hidden_sum = both[:, :half_units].reshape(2 * half_units)
    head_sum = jnp.moveaxis(both[:, half_units:].reshape(2, 3, half_width), 0, 1).reshape(
        3, local_width
    )
    outer_sum = sum_over(
        jnp.stack([gain_grad, shift_grad, out_bias_grad]), n_zh, ("c", "x", "y", "zp", "zh")
    )
    outer_sum = jnp.concatenate([outer_sum, outer_sum[2:]], axis=0)

    model = width
    qkv_sum = qkv_sum.reshape(bw, 2, 3, half_width)
    qkv_sum = jnp.moveaxis(qkv_sum, 2, 0).reshape(3, bw, local_width)
    dense_sum = dense_sum.reshape(bw, local_width).T
    up_sum = up_sum.reshape(bw, 2 * half_units)
    down_sum = down_sum.reshape(bw, 2 * half_units).T
    new_qkv = adam_update(
        qkv_weight, qkv_first, qkv_second, qkv_sum, (model // 2) ** (-0.5), MATRIX_DECAY
    )
    new_dense = adam_update(
        dense_weight, dense_first, dense_second, dense_sum, (model // 16) ** (-0.5), MATRIX_DECAY
    )
    new_up = adam_update(up_weight, up_first, up_second, up_sum, model ** (-0.5), MATRIX_DECAY)
    new_down = adam_update(
        down_weight, down_first, down_second, down_sum, (4 * model) ** (-0.5), MATRIX_DECAY
    )
    new_head = adam_update(head_bias, head_first, head_second, head_sum, VECTOR_RATE, 0.0)
    new_hidden = adam_update(
        hidden_bias, hidden_first, hidden_second, hidden_sum, VECTOR_RATE, 0.0
    )
    new_outer = adam_update(outer_params, outer_first, outer_second, outer_sum, VECTOR_RATE, 0.0)
    return (
        layer_out,
        input_grad,
        *new_qkv,
        *new_dense,
        *new_up,
        *new_down,
        *new_head,
        *new_hidden,
        *new_outer,
    )


def solution(mesh):
    n_zh = mesh.shape["dp"] // 4
    split = Mesh(mesh.devices.reshape(n_zh, 2, 2, 2, 2), ("zh", "zp", "y", "x", "c"))
    dp, mp = ("zh", "zp", "y"), ("x", "c")
    rows = P(dp + mp, None)
    qkv, dense, up, down = P(None, dp, mp), P(mp, dp), P(dp, mp), P(mp, dp)
    rest = (qkv,) * 3 + (dense,) * 3 + (up,) * 3 + (down,) * 3
    rest += (P(None, mp),) * 3 + (P(mp),) * 3 + (P(),) * 3
    return jax.shard_map(
        functools.partial(local, n_zh),
        mesh=split,
        in_specs=(rows, rows) + rest,
        out_specs=(rows, rows) + rest,
        check_vma=False,
    )
```

```python
import functools
import math

import jax
import jax.numpy as jnp
import numpy as np
from jax import lax
from jax.experimental import pallas as pl
from jax.experimental.pallas import tpu as pltpu
from jax.sharding import Mesh
from jax.sharding import PartitionSpec as P

HEAD = 64
ROT = 32
STEP = 10

BETA_ONE = 0.9
BETA_TWO = 0.999
ADAM_EPS = 1e-08
MATRIX_DECAY = 0.1
VECTOR_RATE = 0.1

F32 = jnp.float32
BF16 = jnp.bfloat16
MESH = pl.DeviceIdType.MESH
ANY = pl.BlockSpec(memory_space=pl.ANY)
VMEM_LIMIT = 63 * 1024 * 1024


CHUNK = 256
RING = 2
NT = (((1,), (1,)), ((), ()))
TN = (((0,), (0,)), ((), ()))


def at(index, size):
    return pl.ds(pl.multiple_of(index * size, size), size)


def block_kernel(
    n_zh,
    tok_in, c_in, down_in, up_in, dense_in, qkv_in,
    outer_ref, hidden_bias, head_bias, cos_ref, sin_ref,
    z_mlp, z_dense, z_qkv, y_mlp, y_dense, y_qkv, rows_in, grad_out, branch_out, sums_ref,
    rows2, mlp_w, dense_w, qkv_w, units2, heads3, heads1,
    dq_s, dk_s, dv_s, s_s, p_s, tok_s, stat_s, hidden_sum, head_sum, vec_s, vec_in,
    y_stage, z_stage, qkv_stage, dense_stage, tile_stage, load_s, turned_s,
    w_send, w_recv, fwd_send, fwd_recv, a_send, a_recv, local_sem,
    ym_send, ym_recv, zm_send, zm_recv, yd_send, yd_recv, zd_send, zd_recv,
    yq_send, yq_recv, zq_send, zq_recv, tile_send, tile_recv, x_send, load_sem, wide_sem, vec_send, vec_recv,
):
    zh, zp, y = lax.axis_index("zh"), lax.axis_index("zp"), lax.axis_index("y")
    x, c = lax.axis_index("x"), lax.axis_index("c")
    mp = x * 2 + c
    n = 2 * n_zh
    tok_rows, width = tok_in.shape
    _, bw, units = up_in.shape
    half_width = dense_in.shape[2]
    seq = 4 * tok_rows
    half = width // 2
    lanes = 2 * HEAD
    count = seq // CHUNK
    scale = HEAD ** (-0.5)

    def step(i):
        back = n - 1 - i
        if isinstance(back, int):
            return back // 2, back % 2
        return lax.div(back, 2), lax.rem(back, 2)

    def source_block(i):
        s, f = step(i)
        return lax.rem(zh - s + n_zh, n_zh) * 4 + (zp ^ f) * 2 + y

    def target(i):
        s, f = step(i)
        return {"zh": lax.rem(zh + s, n_zh), "zp": zp ^ f}

    def target_block(i):
        s, f = step(i)
        return lax.rem(zh + s, n_zh) * 4 + (zp ^ f) * 2

    to_y, to_x, to_c, to_zp = {"y": 1 - y}, {"x": 1 - x}, {"c": 1 - c}, {"zp": 1 - zp}
    barrier = pltpu.get_barrier_semaphore()
    partners = [target(i) for i in range(n - 1)] + [to_y, to_x, to_c]
    for partner in partners:
        pl.semaphore_signal(barrier, inc=1, device_id=partner, device_id_type=MESH)
    own = at(zp * 4 + mp, tok_rows)
    tok_load = pltpu.make_async_copy(tok_in, tok_s, load_sem.at[0])
    tok_load.start()
    pl.semaphore_wait(barrier, len(partners))

    def remote(src, dst, send, recv, to):
        return pltpu.make_async_remote_copy(
            src_ref=src, dst_ref=dst, send_sem=send, recv_sem=recv, device_id=to, device_id_type=MESH
        )


    me = source_block(n - 1)
    halves = (down_in, up_in, dense_in, qkv_in)

    pieces = (4, 4, 2, 4) if n_zh == 2 else (1, 1, 1, 1)

    def place(w, b, k=0, m=1):
        spot = at(b * m + k, bw // m)
        if w < 2:
            return mlp_w.at[w, spot, :]
        return (dense_w, qkv_w)[w - 2].at[spot, :]

    started = []

    def go(copy):
        copy.start()
        started.append(copy)

    def z_copy(w, i, k):
        m = pieces[w]
        src = halves[w].at[zp ^ step(i)[1], pl.ds(k * (bw // m), bw // m), :]
        return remote(src, place(w, me, k, m), w_send.at[w, i, k], w_recv.at[w, i, k], target(i))

    def y_copy(w, i, k=0):
        b = source_block(i)
        if i == n - 1:
            return remote(halves[w].at[zp], place(w, b), fwd_send.at[w, i, 0], fwd_recv.at[w, i, 0], to_y)
        spot = place(w, b, k, pieces[w])
        return remote(spot, spot, fwd_send.at[w, i, k], fwd_recv.at[w, i, k], to_y)

    def y_arrived(w):
        for i in range(n - 1):
            for k in range(pieces[w]):
                y_copy(w, i, k).wait_recv()
        y_copy(w, n - 1).wait_recv()

    own_rows = (c_in, rows2.at[1, own, :])

    def act_copy(k, stage, part):
        if stage == 0:
            slot, to, row, column = 0, to_zp, zp, mp
        else:
            row = zp ^ (part % 2)
            column = mp if part < 2 else (1 - x) * 2 + c
            slot, to = (1 + part, to_x) if stage == 1 else (3 + part, to_c)
        spot = rows2.at[k, at(row * 4 + column, tok_rows), :]
        src = own_rows[k] if stage == 0 or part == 0 else spot
        return remote(src, spot, a_send.at[k, slot], a_recv.at[k, slot], to)

    def locals_():
        return [pltpu.make_async_copy(c_in, rows2.at[0, own, :], local_sem.at[0])] + [
            pltpu.make_async_copy(halves[w].at[zp], place(w, me), local_sem.at[1 + w]) for w in range(4)
        ]

    def pass_on(k, stage, part):
        act_copy(k, stage, part).wait_recv()
        if stage == 0:
            go(act_copy(k, 1, 1))
            go(act_copy(k, 2, 1))
        else:
            go(act_copy(k, 2, 2 + part))

    inner = zh != zp if n_zh == 2 else zh < 0
    outer = jnp.logical_not(inner)

    def send_step(w, i, k):
        if i == 0:
            pl.when(outer)(z_copy(w, i, k).start)
        else:
            z_copy(w, i, k).start()

    def forward(w, i, k):
        z_copy(w, i, k).wait_recv()
        y_copy(w, i, k).start()

    def forward_step(w, i, k):
        if i == 0:
            pl.when(outer)(lambda: forward(w, i, k))
        else:
            forward(w, i, k)

    order = [(w, k) for w in (1, 0, 3, 2) for k in range(pieces[w])]
    later = list(range(n - 2, -1, -1))
    go(act_copy(0, 1, 0))
    tok_load.wait()
    for j in range(tok_rows // 64):
        rows = pl.ds(j * 64, 64)
        values = tok_s[rows, :].astype(F32)
        mean = jnp.mean(values, axis=-1, keepdims=True)
        centred = values - mean
        inverse = lax.rsqrt(jnp.mean(centred * centred, axis=-1, keepdims=True) + 1e-05)
        stat_s[0, rows, :] = mean
        stat_s[1, rows, :] = inverse
        normed = centred * inverse * outer_ref[0:1, :] + outer_ref[1:2, :]
        rows2[1, at((zp * 4 + mp) * (tok_rows // 64) + j, 64), :] = normed.astype(BF16)
    go(act_copy(1, 0, 0))
    go(act_copy(0, 0, 0))
    go(act_copy(1, 1, 0))
    go(act_copy(1, 2, 0))
    go(act_copy(0, 2, 0))
    for w in (1, 0, 3, 2):
        go(y_copy(w, n - 1))

    @pl.when(inner)
    def _():
        for w, k in order:
            z_copy(w, 0, k).start()

    for copy in locals_():
        copy.start()
    pass_on(1, 0, 0)
    pl.when(inner)(lambda: forward(1, 0, 0))
    pass_on(0, 0, 0)
    for w, k in order:
        for i in later:
            send_step(w, i, k)

    @pl.when(inner)
    def _():
        for w, k in order[1:]:
            forward(w, 0, k)

    pass_on(1, 1, 0)
    pass_on(0, 1, 0)
    for w, extra in ((1, 1), (0, 0)):
        for k in range(pieces[w]):
            for i in later:
                forward_step(w, i, k)
        pass_on(extra, 1, 1)
    for copy in locals_():
        copy.wait()
    for k in (1, 0):
        for part in range(4):
            act_copy(k, 2, part).wait_recv()
    y_arrived(1)
    y_arrived(0)


    hidden_sum[...] = jnp.zeros_like(hidden_sum)
    events = [(w, i, k) for w in (3, 2) for k in range(pieces[w]) for i in later]
    tiles = 2 * seq // CHUNK

    def mlp_tile(r, carry):
        rows = at(r, CHUNK)
        for j in range(units // CHUNK):
            cols = pl.ds(j * CHUNK, CHUNK)
            hidden = jnp.dot(rows2[1, rows, :], mlp_w[1, :, cols], preferred_element_type=F32)
            hidden = hidden + hidden_bias[:, cols]
            grad = jnp.dot(rows2[0, rows, :], mlp_w[0, :, cols], preferred_element_type=F32)
            k0 = math.sqrt(2.0 / math.pi)
            square = hidden * hidden
            tanh = jnp.tanh(k0 * (hidden * (1.0 + 0.044715 * square)))
            units2[0, rows, cols] = (0.5 * hidden * (1.0 + tanh)).astype(BF16)
            slope = 0.5 * (1.0 + tanh) + 0.5 * hidden * (1.0 - tanh * tanh) * (
                k0 * (1.0 + 3.0 * 0.044715 * square)
            )
            low = (grad * slope).astype(BF16)
            units2[1, rows, cols] = low
            hidden_sum[:, cols] += jnp.sum(low.astype(F32), axis=0, keepdims=True)
        for r_at in range(tiles):
            mine = [e for k, e in enumerate(events) if k * (tiles - 2) // len(events) == r_at]
            if mine:
                @pl.when(r == r_at)
                def _():
                    for event in mine:
                        forward_step(*event)
        return carry

    lax.fori_loop(0, tiles, mlp_tile, 0)
    for w in range(4):
        for i in range(n - 1):
            for k in range(pieces[w]):
                started.extend([z_copy(w, i, k), y_copy(w, i, k)])


    def weight_grad(left, right, b, put):
        wide = max(bw, 128)
        turned = turned_s.at[pl.ds(0, wide), :]
        if bw == wide:
            turned[...] = left[:, at(b, bw)].T
        else:
            turned[...] = left[:, at(lax.div(b, wide // bw), wide)].T
        for j in range(right.shape[1] // CHUNK):
            cols = pl.ds(j * CHUNK, CHUNK)
            value = jnp.dot(turned[...], right[:, cols], preferred_element_type=F32)
            if bw < wide:
                spot = lax.rem(b, wide // bw)
                value = sum(
                    jnp.where(spot == k, value[k * bw : (k + 1) * bw], 0.0) for k in range(wide // bw)
                )
            put(cols, value)

    def mlp_grad(w, b, put):
        weight_grad(rows2.at[w], units2.at[w], b, put)

    def ym_copy(k):
        w, i = lax.div(k, n), lax.rem(k, n)
        return remote(y_stage.at[at(k, bw), :], y_mlp.at[w, i], ym_send.at[k], ym_recv.at[k], to_y)

    def ym_step(k, carry):
        w, i = lax.div(k, n), lax.rem(k, n)

        def put(cols, value):
            y_stage[at(k, bw), cols] = value.astype(BF16)

        mlp_grad(w, target_block(i) + 1 - y, put)
        ym_copy(k).start()
        return carry

    lax.fori_loop(0, 2 * n, ym_step, 0)

    def zm_copy(k):
        w, i = lax.div(k, n), lax.rem(k, n)
        return remote(z_stage.at[i], z_mlp.at[w, i], zm_send.at[i], zm_recv.at[k], target(i))

    def zm_local(k):
        w, i = lax.div(k, n), lax.rem(k, n)
        return pltpu.make_async_copy(z_stage.at[i], z_mlp.at[w, i], zm_send.at[i])

    def zm_step(k, carry):
        w, i = lax.div(k, n), lax.rem(k, n)
        ym_copy(k).wait_recv()
        load = pltpu.make_async_copy(y_mlp.at[w, i], load_s.at[0, pl.ds(0, bw), :], load_sem.at[0])
        load.start()

        @pl.when((k >= n) & (i < n - 1))
        def _():
            zm_copy(k - n).wait_send()

        @pl.when((k >= n) & (i == n - 1))
        def _():
            zm_local(k - n).wait()

        load.wait()

        def put(cols, value):
            z_stage[i, :, cols] = (value + load_s[0, pl.ds(0, bw), cols].astype(F32)).astype(BF16)

        mlp_grad(w, target_block(i) + y, put)

        @pl.when(i < n - 1)
        def _():
            zm_copy(k).start()

        @pl.when(i == n - 1)
        def _():
            zm_local(k).start()

        return carry


    y_arrived(3)
    y_arrived(2)
    low_lane = lax.broadcasted_iota(jnp.int32, (1, lanes), 1) % HEAD < ROT // 2

    def turn(values, rows, sign):
        after = pltpu.roll(values, lanes - ROT // 2, 1)
        before = pltpu.roll(values, ROT // 2, 1)
        return values * cos_ref[rows, :] + jnp.where(low_lane, after, before) * (sign * sin_ref[rows, :])

    def proj_tile(r, carry):
        rows = at(r, CHUNK)
        where = at(lax.rem(r, count), CHUNK)
        for t in range(3):
            cols = pl.ds(t * half_width, half_width)
            proj = jnp.dot(rows2[1, rows, :], qkv_w[:, cols], preferred_element_type=F32) + head_bias[:, cols]
            for g in range(half_width // lanes):
                part = proj[:, g * lanes : (g + 1) * lanes]
                if t < 2:
                    part = turn(part, where, 1.0)
                heads3[rows, pl.ds(t * half_width + g * lanes, lanes)] = part.astype(BF16)
        heads1[rows, :] = jnp.dot(rows2[0, rows, :], dense_w[...], preferred_element_type=F32).astype(BF16)
        return carry

    lax.fori_loop(0, tiles, proj_tile, 0)


    first = lax.broadcasted_iota(jnp.int32, (1, lanes), 1) < HEAD
    pairs = half_width // lanes

    def attend(it, carry):
        base = lax.div(it, pairs) * count
        hp = lax.rem(it, pairs)

        def cols(t):
            return at(t * pairs + hp, lanes)

        here = at(hp, lanes)
        dk_s[...] = jnp.zeros_like(dk_s)
        dv_s[...] = jnp.zeros_like(dv_s)
        diagonal = lax.broadcasted_iota(jnp.int32, (CHUNK, CHUNK), 0) <= lax.broadcasted_iota(
            jnp.int32, (CHUNK, CHUNK), 1
        )
        for qb in range(count):
            rows = at(base + qb, CHUNK)
            q_rows = heads3[rows, cols(0)] * jnp.asarray(scale, BF16)
            g_rows = heads1[rows, here]
            mixed_halves, dq_halves = [], []
            for h in (0, 1):
                mine = first if h == 0 else jnp.logical_not(first)
                q_one = jnp.where(mine, q_rows, jnp.zeros_like(q_rows))
                g_one = jnp.where(mine, g_rows, jnp.zeros_like(g_rows))
                top = None
                for j in range(qb + 1):
                    keys = heads3[at(base + j, CHUNK), cols(1)]
                    scores = lax.dot_general(keys, q_one, NT, preferred_element_type=F32)
                    if j == qb:
                        scores = jnp.where(diagonal, scores, -1e30)
                    s_s[j] = scores
                    peak = jnp.max(scores, axis=0, keepdims=True)
                    top = peak if top is None else jnp.maximum(top, peak)
                total = None
                for j in range(qb + 1):
                    e = jnp.exp(s_s[j] - top)
                    s_s[j] = e
                    part = jnp.sum(e, axis=0, keepdims=True)
                    total = part if total is None else total + part
                inverse = 1.0 / total
                mixed, inner = None, None
                for j in range(qb + 1):
                    values = heads3[at(base + j, CHUNK), cols(2)]
                    probs = s_s[j] * inverse
                    low = probs.astype(BF16)
                    part = lax.dot_general(low, values, TN, preferred_element_type=F32)
                    mixed = part if mixed is None else mixed + part
                    dv_s[h, pl.ds(j * CHUNK, CHUNK), :] += jnp.dot(low, g_rows, preferred_element_type=F32)
                    grad_probs = lax.dot_general(values, g_one, NT, preferred_element_type=F32)
                    s_s[j] = probs
                    p_s[j] = grad_probs
                    part = jnp.sum(probs * grad_probs, axis=0, keepdims=True)
                    inner = part if inner is None else inner + part
                dq = None
                for j in range(qb + 1):
                    keys = heads3[at(base + j, CHUNK), cols(1)]
                    grad_scores = (s_s[j] * (p_s[j] - inner)).astype(BF16)
                    part = lax.dot_general(grad_scores, keys, TN, preferred_element_type=F32)
                    dq = part if dq is None else dq + part
                    dk_s[h, pl.ds(j * CHUNK, CHUNK), :] += jnp.dot(
                        grad_scores, q_rows, preferred_element_type=F32
                    )
                mixed_halves.append(mixed)
                dq_halves.append(dq)
            heads1[rows, here] = jnp.where(first, *mixed_halves).astype(BF16)
            dq_s[pl.ds(qb * CHUNK, CHUNK), :] = jnp.where(first, *dq_halves) * scale
        for qb in range(count):
            rows = pl.ds(qb * CHUNK, CHUNK)
            gq = turn(dq_s[rows, :], rows, -1.0)
            gk = turn(jnp.where(first, dk_s[0, rows, :], dk_s[1, rows, :]), rows, -1.0)
            gv = jnp.where(first, dv_s[0, rows, :], dv_s[1, rows, :])
            for t, g in enumerate((gq, gk, gv)):
                low = g.astype(BF16)
                heads3[at(base + qb, CHUNK), cols(t)] = low
                head_sum[:, cols(t)] += jnp.sum(low.astype(F32), axis=0, keepdims=True)
        per = n // 4
        lax.fori_loop(it * per, (it + 1) * per, zm_step, 0)
        return carry

    head_sum[...] = jnp.zeros_like(head_sum)
    lax.fori_loop(0, 2 * pairs, attend, 0)


    def small(left, right, y_buf, z_buf, stage, ys, yr, zs, zr):
        cols = stage.shape[2]

        def y_copy_(i):
            return remote(stage.at[i], y_buf.at[i], ys.at[i], yr.at[i], to_y)

        def z_copy_(i):
            return remote(stage.at[i], z_buf.at[i], zs.at[i], zr.at[i], target(i))

        def z_local(i):
            return pltpu.make_async_copy(stage.at[i], z_buf.at[i], zs.at[i])

        def y_step(i, carry):
            def put(at_cols, value):
                stage[i, :, at_cols] = value.astype(BF16)

            weight_grad(left, right, target_block(i) + 1 - y, put)
            y_copy_(i).start()
            return carry

        def z_step(i, carry):
            y_copy_(i).wait_recv()
            spot = load_s.at[0, pl.ds(0, bw), pl.ds(0, cols)]
            load = pltpu.make_async_copy(y_buf.at[i], spot, load_sem.at[0])
            load.start()
            y_copy_(i).wait_send()
            load.wait()

            def put(at_cols, value):
                stage[i, :, at_cols] = (value + spot[:, at_cols].astype(F32)).astype(BF16)

            weight_grad(left, right, target_block(i) + y, put)

            @pl.when(i < n - 1)
            def _():
                z_copy_(i).start()

            @pl.when(i == n - 1)
            def _():
                z_local(i).start()

            return carry

        def finish(i, carry):
            @pl.when(i < n - 1)
            def _():
                z_copy_(i).wait_send()
                z_copy_(i).wait_recv()

            @pl.when(i == n - 1)
            def _():
                z_local(i).wait()

            return carry

        return y_step, z_step, finish

    dense_steps = small(
        rows2.at[0], heads1, y_dense, z_dense, dense_stage, yd_send, yd_recv, zd_send, zd_recv
    )
    qkv_steps = small(
        rows2.at[1], heads3, y_qkv, z_qkv, qkv_stage, yq_send, yq_recv, zq_send, zq_recv
    )


    def ring_copy(kind, slot, index, to):
        return remote(
            tile_stage.at[slot], rows_in.at[kind, index], tile_send.at[slot],
            tile_recv.at[kind, index], to,
        )

    def x_slot(kind, t):
        return tile_stage.at[RING + t] if kind else y_stage.at[at(t, tok_rows), :]

    def x_copy(kind, t, index):
        return remote(
            x_slot(kind, t), rows_in.at[kind, index], x_send.at[kind, t], tile_recv.at[kind, index], to_x
        )

    def row_tiles(kind, stage, base, total):
        left, left_w = units2.at[1 - kind], mlp_w.at[1 - kind]
        right, right_w = ((heads3, qkv_w), (heads1, dense_w))[kind]

        def one(t, carry):
            h = lax.rem(t, 2)
            if stage == 0:
                zq, xq = zp ^ (1 - lax.rem(lax.div(t, 2), 2)), x ^ (1 - lax.div(t, 4))
                block, come, to, index = zq * 4 + xq * 2 + 1 - c, (), to_c, zq * 4 + xq * 2 + h
            elif stage == 1:
                zq = zp ^ (1 - lax.div(t, 2))
                block, to, index = zq * 4 + (1 - x) * 2 + c, to_x, 8 + zq * 2 + h
                come = (zq * 4 + (1 - x) * 2 + h,)
            elif stage == 2:
                block, to, index = (1 - zp) * 4 + x * 2 + c, to_zp, 12 + h
                come = ((1 - zp) * 4 + x * 2 + h, 8 + (1 - zp) * 2 + h)
            else:
                block, to, index = zp * 4 + x * 2 + c, None, None
                come = (zp * 4 + x * 2 + h, 8 + zp * 2 + h, 12 + h)
            loads = []
            for slot, (spot, back) in enumerate(zip(come, (to_c, to_x, to_zp))):
                ring_copy(kind, 0, spot, back).wait_recv()
                loads.append(
                    pltpu.make_async_copy(rows_in.at[kind, spot], load_s.at[slot], load_sem.at[slot])
                )
                loads[-1].start()
            for load in loads:
                load.wait()
            rows = at(block, tok_rows)
            if stage in (0, 2):
                slot = lax.rem(base + t, RING)
                spot, copy = tile_stage.at[slot], ring_copy(kind, slot, index, to)

                @pl.when(base + t >= RING)
                def _():
                    copy.wait_send()

            elif stage == 1:
                spot, copy = x_slot(kind, t), x_copy(kind, t, index)
            for j in range(half // CHUNK):
                cols = pl.ds(j * CHUNK, CHUNK)
                model = at(h * (half // CHUNK) + j, CHUNK)
                value = lax.dot_general(left[rows, :], left_w[model, :], NT, preferred_element_type=F32)
                value += lax.dot_general(right[rows, :], right_w[model, :], NT, preferred_element_type=F32)
                for k in range(len(loads)):
                    value += load_s[k, :, cols].astype(F32)
                if stage < 3:
                    spot[:, cols] = value.astype(BF16)
                else:
                    s_s[j] = value
                    if kind == 0:
                        xhat = (tok_s[:, model].astype(F32) - stat_s[0]) * stat_s[1]
                        back = rows2[0, own, model].astype(F32)
                        for row, term in enumerate((value * xhat, value, back)):
                            vec_s[row : row + 1, model] = jnp.sum(term, axis=0, keepdims=True)
            if stage < 3:
                copy.start()
            else:
                out = (grad_out, branch_out)[kind]
                copies = [
                    pltpu.make_async_copy(
                        s_s.at[j], out.at[:, at(h * (half // CHUNK) + j, CHUNK)], wide_sem.at[j]
                    )
                    for j in range(half // CHUNK)
                ]
                for copy in copies:
                    copy.start()
                for copy in copies:
                    copy.wait()
            return carry

        lax.fori_loop(0, total, one, 0)

    def finish_y(k, carry):
        ym_copy(k).wait_send()
        return carry


    hops = [to_zp, to_y]
    bit = 1
    while bit < n_zh:
        hops.append({"zh": zh ^ bit})
        bit *= 2
    dp_hops = len(hops)
    hops += [to_c, to_x]

    def vec_copy(k):
        return remote(vec_s, vec_in.at[k], vec_send.at[k], vec_recv.at[k], hops[k])

    def vec_first():
        for row in (3, 4):
            vec_s[row : row + 1, :] = jnp.zeros((1, width), F32)
        vec_s[3:4, at(zp, units)] = hidden_sum[...]
        for t in range(3):
            vec_s[4:5, at(t * 2 + zp, half_width)] = head_sum[:, pl.ds(t * half_width, half_width)]
        vec_copy(0).start()

    def vec_next(k):
        vec_copy(k).wait()
        vec_s[...] += vec_in[k]
        if k + 1 == dp_hops:
            sums_ref[3:5, :] = vec_s[3:5, :]
        if k + 1 < len(hops):
            vec_copy(k + 1).start()
        else:
            sums_ref[0:3, :] = vec_s[0:3, :]

    per = n // 4
    row_tiles(0, 0, 0, 8)
    lax.fori_loop(0, n, finish_y, 0)
    row_tiles(0, 1, 0, 4)
    lax.fori_loop(n, n + per, zm_step, 0)
    row_tiles(1, 0, 8, 8)
    lax.fori_loop(n + per, n + 2 * per, zm_step, 0)
    row_tiles(1, 1, 0, 4)
    lax.fori_loop(0, n, dense_steps[0], 0)
    lax.fori_loop(0, n, qkv_steps[0], 0)
    row_tiles(0, 2, 16, 2)
    lax.fori_loop(n + 2 * per, 2 * n, zm_step, 0)
    lax.fori_loop(0, n, dense_steps[1], 0)
    lax.fori_loop(0, n // 2, qkv_steps[1], 0)
    row_tiles(1, 2, 18, 2)
    row_tiles(0, 3, 0, 2)
    vec_first()
    lax.fori_loop(n // 2, n // 2 + per, qkv_steps[1], 0)
    vec_next(0)
    vec_next(1)
    lax.fori_loop(n // 2 + per, n, qkv_steps[1], 0)
    for k in range(2, len(hops) - 1):
        vec_next(k)
    row_tiles(1, 3, 0, 2)
    vec_next(len(hops) - 1)


    for copy in started:
        copy.wait_send()

    def finish_z(k, carry):
        i = lax.rem(k, n)

        @pl.when(i < n - 1)
        def _():
            zm_copy(k).wait_recv()

        @pl.when((k >= n) & (i < n - 1))
        def _():
            zm_copy(k).wait_send()

        @pl.when((k >= n) & (i == n - 1))
        def _():
            zm_local(k).wait()

        return carry

    lax.fori_loop(n, 2 * n, finish_y, 0)
    lax.fori_loop(0, 2 * n, finish_z, 0)
    for slot in range(RING):
        ring_copy(0, slot, 0, to_c).wait_send()
    for kind in (0, 1):
        for t in range(4):
            x_copy(kind, t, 0).wait_send()
    lax.fori_loop(0, n, dense_steps[2], 0)
    lax.fori_loop(0, n, qkv_steps[2], 0)


def block(n_zh, tokens, cotangent, halves, outer_params, hidden_bias, head_bias, tables):
    tok_rows, width = tokens.shape
    n = 2 * n_zh
    dp = 2 * n
    bw = width // dp
    units = halves[1].shape[2]
    half_width = halves[2].shape[2]
    triple = 3 * half_width
    seq = 4 * tok_rows
    count = seq // CHUNK
    hops = 4 + (n_zh - 1).bit_length()
    shape = jax.ShapeDtypeStruct
    vmem = pl.BlockSpec(memory_space=pltpu.VMEM)
    dma = pltpu.SemaphoreType.DMA
    outs = [
        shape((2, n, bw, units), BF16),
        shape((n, bw, half_width), BF16),
        shape((n, bw, triple), BF16),
        shape((2, n, bw, units), BF16),
        shape((n, bw, half_width), BF16),
        shape((n, bw, triple), BF16),
        shape((2, 14, tok_rows, width // 2), BF16),
        shape((tok_rows, width), F32),
        shape((tok_rows, width), F32),
        shape((8, width), F32),
    ]
    scratch = [
        pltpu.VMEM((2, 2 * seq, width), BF16),
        pltpu.VMEM((2, width, units), BF16),
        pltpu.VMEM((width, half_width), BF16),
        pltpu.VMEM((width, triple), BF16),
        pltpu.VMEM((2, 2 * seq, units), BF16),
        pltpu.VMEM((2 * seq, triple), BF16),
        pltpu.VMEM((2 * seq, half_width), BF16),
        pltpu.VMEM((seq, 2 * HEAD), F32),
        pltpu.VMEM((2, seq, 2 * HEAD), F32),
        pltpu.VMEM((2, seq, 2 * HEAD), F32),
        pltpu.VMEM((count, CHUNK, CHUNK), F32),
        pltpu.VMEM((count, CHUNK, CHUNK), F32),
        pltpu.VMEM((tok_rows, width), BF16),
        pltpu.VMEM((2, tok_rows, 1), F32),
        pltpu.VMEM((1, units), F32),
        pltpu.VMEM((1, triple), F32),
        pltpu.VMEM((8, width), F32),
        pltpu.VMEM((hops, 8, width), F32),
        pltpu.VMEM((2 * n * bw, units), BF16),
        pltpu.VMEM((n, bw, units), BF16),
        pltpu.VMEM((n, bw, triple), BF16),
        pltpu.VMEM((n, bw, half_width), BF16),
        pltpu.VMEM((RING + 4, tok_rows, width // 2), BF16),
        pltpu.VMEM((3, tok_rows, width // 2), BF16),
        pltpu.VMEM((max(bw, 128), 2 * seq), BF16),
        dma((4, n, 4)), dma((4, n, 4)), dma((4, n, 4)), dma((4, n, 4)), dma((2, 7)), dma((2, 7)), dma((6,)),
        dma((2 * n,)), dma((2 * n,)), dma((n,)), dma((2 * n,)),
        dma((n,)), dma((n,)), dma((n,)), dma((n,)),
        dma((n,)), dma((n,)), dma((n,)), dma((n,)),
        dma((RING,)), dma((2, 14)), dma((2, 4)), dma((3,)), dma((width // 2 // CHUNK,)), dma((hops,)), dma((hops,)),
    ]
    return pl.pallas_call(
        functools.partial(block_kernel, n_zh),
        out_shape=outs,
        in_specs=[ANY] * 6 + [vmem] * 5,
        out_specs=[ANY] * 9 + [vmem],
        scratch_shapes=scratch,
        compiler_params=pltpu.CompilerParams(
            collective_id=0, has_side_effects=True, vmem_limit_bytes=VMEM_LIMIT
        ),
    )(tokens, cotangent, *halves, outer_params, hidden_bias, head_bias, *tables)


def rotation_tables(seq):
    lane = np.arange(2 * HEAD) % HEAD
    exponent = (lane % (ROT // 2)).astype(np.float32) * np.float32(2.0 / ROT)
    inverse = np.exp(np.float32(-math.log(10000.0)) * exponent).astype(np.float32)
    angles = np.arange(seq, dtype=np.float32)[:, None] * inverse[None, :]
    cos = np.cos(angles.astype(np.float64)).astype(np.float32)
    sin = np.sin(angles.astype(np.float64)).astype(np.float32)
    turned, low = lane < ROT, lane < ROT // 2
    zero = np.zeros_like(sin)
    return np.where(turned, cos, zero + 1), np.where(turned, np.where(low, -sin, sin), zero)


def adam_update(weight, moment_one, moment_two, gradient, step_rate, decay_rate):
    first_new = BETA_ONE * moment_one + (1.0 - BETA_ONE) * gradient
    second_new = BETA_TWO * moment_two + (1.0 - BETA_TWO) * gradient * gradient
    normalized = (
        first_new
        / (1.0 - BETA_ONE**STEP)
        / (jnp.sqrt(second_new / (1.0 - BETA_TWO**STEP)) + ADAM_EPS)
    )
    return (weight - step_rate * (normalized + decay_rate * weight), first_new, second_new)


def adam_kernel(rate, turned, zp_ref, parts_ref, w_ref, one_ref, two_ref, *outs):
    parts = parts_ref[...].astype(F32)
    rows, cols = parts.shape[-2:]
    gradient = jnp.sum(parts.reshape(-1, rows, cols), axis=0)
    if turned:
        gradient = gradient.T
    shape = w_ref.shape
    new = adam_update(
        w_ref[...].reshape(gradient.shape), one_ref[...].reshape(gradient.shape),
        two_ref[...].reshape(gradient.shape), gradient, rate, MATRIX_DECAY,
    )
    for out, value in zip(outs, new):
        out[...] = value.reshape(shape)


def adam(zp, parts, state, rate, turned, grid, parts_spec, state_spec):
    shape = jax.ShapeDtypeStruct(state[0].shape, F32)
    spec = pl.BlockSpec(*state_spec)
    return pl.pallas_call(
        functools.partial(adam_kernel, rate, turned),
        out_shape=[shape] * 3,
        grid_spec=pltpu.PrefetchScalarGridSpec(
            num_scalar_prefetch=1,
            grid=grid,
            in_specs=[pl.BlockSpec(*parts_spec)] + [spec] * 3,
            out_specs=[spec] * 3,
        ),
        compiler_params=pltpu.CompilerParams(vmem_limit_bytes=32 * 1024 * 1024),
    )(zp, parts, *state)


def finish_kernel(tok_ref, back_ref, grad_ref, branch_ref, outer_ref, out_ref, in_ref):
    values = tok_ref[...].astype(F32)
    out_ref[...] = (values + branch_ref[...] + outer_ref[2:3, :] + outer_ref[3:4, :]).astype(BF16)
    mean = jnp.mean(values, axis=-1, keepdims=True)
    centred = values - mean
    inverse = lax.rsqrt(jnp.mean(centred * centred, axis=-1, keepdims=True) + 1e-05)
    xhat = centred * inverse
    g = grad_ref[...] * outer_ref[0:1, :]
    inner = g - jnp.mean(g, axis=-1, keepdims=True) - xhat * jnp.mean(g * xhat, axis=-1, keepdims=True)
    in_ref[...] = back_ref[...].astype(F32) + inverse * inner


def finish(tokens, cotangent, grad_normed, branch, outer_params):
    rows, width = tokens.shape
    tile = 64
    spec = pl.BlockSpec((tile, width), lambda i: (i, 0))
    return pl.pallas_call(
        finish_kernel,
        grid=(rows // tile,),
        out_shape=[jax.ShapeDtypeStruct((rows, width), BF16), jax.ShapeDtypeStruct((rows, width), F32)],
        in_specs=[spec] * 4 + [pl.BlockSpec(outer_params.shape, lambda i: (0, 0))],
        out_specs=[spec] * 2,
        compiler_params=pltpu.CompilerParams(vmem_limit_bytes=32 * 1024 * 1024),
    )(tokens, cotangent, grad_normed, branch, outer_params)


def pick(value, index, axis):
    return lax.dynamic_index_in_dim(value, index, axis, keepdims=False)


def local(
    n_zh,
    tokens, cotangent,
    qkv_weight, qkv_first, qkv_second,
    dense_weight, dense_first, dense_second,
    up_weight, up_first, up_second,
    down_weight, down_first, down_second,
    head_bias, head_first, head_second,
    hidden_bias, hidden_first, hidden_second,
    outer_params, outer_first, outer_second,
):
    zp = lax.axis_index("zp")
    tok_rows, width = tokens.shape
    seq_rows = tok_rows * 4
    bw = qkv_weight.shape[1]
    local_width = qkv_weight.shape[2]
    half_width = local_width // 2
    half_units = up_weight.shape[1] // 2

    qkv_rows = qkv_weight.reshape(3, bw, 2, half_width).transpose(2, 1, 0, 3)
    qkv_rows = qkv_rows.reshape(2, bw, 3 * half_width).astype(BF16)
    dense_rows = dense_weight.reshape(2, half_width, bw).swapaxes(1, 2).astype(BF16)
    up_rows = up_weight.reshape(bw, 2, half_units).swapaxes(0, 1).astype(BF16)
    down_rows = down_weight.reshape(2, half_units, bw).swapaxes(1, 2).astype(BF16)
    bias_half = pick(hidden_bias.reshape(2, 1, half_units), zp, 0)
    head_half = pick(head_bias.reshape(3, 2, half_width), zp, 1).reshape(1, 3 * half_width)
    outs = block(
        n_zh, tokens, cotangent, (down_rows, up_rows, dense_rows, qkv_rows), outer_params,
        bias_half, head_half, rotation_tables(seq_rows),
    )
    z_mlp, z_dense, z_qkv = outs[:3]
    grad_normed, branch, sums = outs[7:]
    layer_out, input_grad = finish(tokens, cotangent, grad_normed, branch, outer_params)

    zp_array = jnp.reshape(zp, (1,))
    z_mlp = z_mlp.reshape(2, n_zh, 2, bw, half_units)
    z_dense = z_dense.reshape(n_zh, 2, bw, half_width)
    z_qkv = z_qkv.reshape(n_zh, 2, bw, 3 * half_width)
    tile = min(bw, 128)
    new_up = adam(
        zp_array, z_mlp, (up_weight, up_first, up_second), width ** (-0.5), False,
        (2, bw // tile),
        ((1, n_zh, 1, tile, half_units), lambda h, r, zp_: (1, 0, 1 - (h ^ zp_[0]), r, 0)),
        ((tile, half_units), lambda h, r, zp_: (r, h)),
    )
    new_down = adam(
        zp_array, z_mlp, (down_weight, down_first, down_second), (4 * width) ** (-0.5), True,
        (2, half_units // CHUNK),
        ((1, n_zh, 1, bw, CHUNK), lambda h, r, zp_: (0, 0, 1 - (h ^ zp_[0]), 0, r)),
        ((CHUNK, bw), lambda h, r, zp_: (h * (half_units // CHUNK) + r, 0)),
    )
    new_dense = adam(
        zp_array, z_dense, (dense_weight, dense_first, dense_second), (width // 16) ** (-0.5), True,
        (2,),
        ((n_zh, 1, bw, half_width), lambda h, zp_: (0, 1 - (h ^ zp_[0]), 0, 0)),
        ((half_width, bw), lambda h, zp_: (h, 0)),
    )
    new_qkv = adam(
        zp_array, z_qkv, (qkv_weight, qkv_first, qkv_second), (width // 2) ** (-0.5), False,
        (3, 2),
        ((n_zh, 1, bw, half_width), lambda t, h, zp_: (0, 1 - (h ^ zp_[0]), 0, t)),
        ((1, bw, half_width), lambda t, h, zp_: (t, 0, h)),
    )
    outer_sum = jnp.concatenate([sums[:3], sums[2:3]], axis=0)
    hidden_sum = sums[3]
    head_sum = sums[4, : 3 * local_width].reshape(3, local_width)
    new_head = adam_update(head_bias, head_first, head_second, head_sum, VECTOR_RATE, 0.0)
    new_hidden = adam_update(
        hidden_bias, hidden_first, hidden_second, hidden_sum, VECTOR_RATE, 0.0
    )
    new_outer = adam_update(outer_params, outer_first, outer_second, outer_sum, VECTOR_RATE, 0.0)
    return (
        layer_out,
        input_grad,
        *new_qkv,
        *new_dense,
        *new_up,
        *new_down,
        *new_head,
        *new_hidden,
        *new_outer,
    )


def solution(mesh):
    n_zh = mesh.shape["dp"] // 4
    split = Mesh(mesh.devices.reshape(n_zh, 2, 2, 2, 2), ("zh", "zp", "y", "x", "c"))
    dp, mp = ("zh", "zp", "y"), ("x", "c")
    rows = P(dp + mp, None)
    qkv, dense, up, down = P(None, dp, mp), P(mp, dp), P(dp, mp), P(mp, dp)
    rest = (qkv,) * 3 + (dense,) * 3 + (up,) * 3 + (down,) * 3
    rest += (P(None, mp),) * 3 + (P(mp),) * 3 + (P(),) * 3
    return jax.shard_map(
        functools.partial(local, n_zh),
        mesh=split,
        in_specs=(rows, rows) + rest,
        out_specs=(rows, rows) + rest,
        check_vma=False,
    )
```

```python
import functools
import math

import jax
import jax.numpy as jnp
import numpy as np
from jax import lax
from jax.experimental import pallas as pl
from jax.experimental.pallas import tpu as pltpu
from jax.sharding import Mesh
from jax.sharding import PartitionSpec as P

HEAD = 64
ROT = 32
STEP = 10

BETA_ONE = 0.9
BETA_TWO = 0.999
ADAM_EPS = 1e-08
MATRIX_DECAY = 0.1
VECTOR_RATE = 0.1

F32 = jnp.float32
BF16 = jnp.bfloat16
MESH = pl.DeviceIdType.MESH
ANY = pl.BlockSpec(memory_space=pl.ANY)
VMEM_LIMIT = 63 * 1024 * 1024


RUNS = (
    (
        ("proj", 4), ("f1", 1), ("proj", 3), ("f1", 1), ("proj", 1), ("att", 1), ("f1", 1), ("att", 1),
        ("f0", 2), ("att", 1), ("f0", 1), ("att", 1), ("a1", 1),
    ),
    (
        ("act", 1), ("f0", 1), ("act", 4), ("ysET", 1), ("ysQKV", 1), ("act", 1), ("ysQKV", 1), ("a0", 1),
        ("slope", 1), ("act", 1), ("slope", 2), ("zsQKV", 1), ("ysQKV", 1), ("act", 1), ("slope", 1),
        ("zsQKV", 1), ("ysM", 1), ("slope", 1), ("ysET", 1), ("slope", 1), ("zsET", 1), ("zsQKV", 1),
        ("slope", 1), ("ysM", 1), ("slope", 1), ("ysM", 1),
    ),
    (
        ("zsM", 1), ("r0c", 1), ("zsET", 1), ("r0c", 3), ("zsM", 1), ("r0c", 4), ("r0x", 1), ("zsM", 1),
        ("r0x", 1), ("ysET", 1), ("ysM", 1), ("r0x", 1), ("zsET", 1), ("r0x", 1), ("r0z", 1), ("r1c", 1),
        ("ysM", 1), ("r1c", 2), ("r0z", 1), ("r1c", 1), ("ysM", 1), ("r1c", 1), ("zsM", 2), ("r1c", 3),
        ("r1x", 1), ("zsM", 1), ("r1x", 2), ("ysM", 1), ("r0f", 1), ("r1x", 1), ("r1z", 1), ("ysET", 1),
        ("ysM", 1), ("r0f", 1), ("r1z", 1), ("zsET", 1), ("vec", 1), ("zsM", 1), ("vec", 3), ("ysQKV", 1),
        ("vec", 1), ("zsM", 1), ("r1f", 1), ("vec", 1), ("r1f", 1), ("zsQKV", 1),
    ),
)
ORDER = [[name for name, times in part for _ in range(times)] for part in RUNS]

CHUNK = 256
RING = 2
LATER = 1
GELU = math.sqrt(2.0 / math.pi)
NT = (((1,), (1,)), ((), ()))
TN = (((0,), (0,)), ((), ()))


def at(index, size):
    return pl.ds(pl.multiple_of(index * size, size), size)


def block_kernel(
    n_zh,
    tok_in, c_in, down_in, up_in, dense_in, qkv_in,
    outer_ref, hidden_bias, head_bias, cos_ref, sin_ref,
    z_mlp, z_dense, z_qkv, y_mlp, y_dense, y_qkv, rows_in, grad_out, branch_out, sums_ref,
    rows2, mlp_w, dense_w, qkv_w, units2, heads3, heads1,
    dq_s, dk_s, dv_s, s_s, p_s, tok_s, stat_s, hidden_sum, head_sum, vec_s, vec_in,
    grads_s, qkv_stage, dense_stage, tile_stage, load_s, turned_s,
    w_send, w_recv, fwd_send, fwd_recv, a_send, a_recv, local_sem,
    ym_send, ym_recv, zm_send, zm_recv, yd_send, yd_recv, zd_send, zd_recv,
    yq_send, yq_recv, zq_send, zq_recv, tile_send, tile_recv, x_send, zt_send, load_sem, wide_sem, vec_send, vec_recv,
):
    zh, zp, y = lax.axis_index("zh"), lax.axis_index("zp"), lax.axis_index("y")
    x, c = lax.axis_index("x"), lax.axis_index("c")
    mp = x * 2 + c
    n = 2 * n_zh
    tok_rows, width = tok_in.shape
    _, bw, units = up_in.shape
    half_width = dense_in.shape[2]
    seq = 4 * tok_rows
    half = width // 2
    lanes = 2 * HEAD
    count = seq // CHUNK
    scale = HEAD ** (-0.5)

    def step(i):
        back = n - 1 - i
        if isinstance(back, int):
            return back // 2, back % 2
        return lax.div(back, 2), lax.rem(back, 2)

    def source_block(i):
        s, f = step(i)
        return lax.rem(zh - s + n_zh, n_zh) * 4 + (zp ^ f) * 2 + y

    def target(i):
        s, f = step(i)
        return {"zh": lax.rem(zh + s, n_zh), "zp": zp ^ f}

    def target_block(i):
        s, f = step(i)
        return lax.rem(zh + s, n_zh) * 4 + (zp ^ f) * 2

    to_y, to_x, to_c, to_zp = {"y": 1 - y}, {"x": 1 - x}, {"c": 1 - c}, {"zp": 1 - zp}
    barrier = pltpu.get_barrier_semaphore()
    partners = [target(i) for i in range(n - 1)] + [to_y, to_x, to_c]
    for partner in partners:
        pl.semaphore_signal(barrier, inc=1, device_id=partner, device_id_type=MESH)
    own = at(zp * 4 + mp, tok_rows)
    tok_load = pltpu.make_async_copy(tok_in, tok_s, load_sem.at[0])
    tok_load.start()
    pl.semaphore_wait(barrier, len(partners))

    def remote(src, dst, send, recv, to):
        return pltpu.make_async_remote_copy(
            src_ref=src, dst_ref=dst, send_sem=send, recv_sem=recv, device_id=to, device_id_type=MESH
        )


    me = source_block(n - 1)
    halves = (down_in, up_in, dense_in, qkv_in)

    pieces = (4, 4, 2, 4) if n_zh == 2 else (1, 1, 1, 1)

    def place(w, b, k=0, m=1):
        spot = at(b * m + k, bw // m)
        if w < 2:
            return mlp_w.at[w, spot, :]
        return (dense_w, qkv_w)[w - 2].at[spot, :]

    started = []

    def go(copy):
        copy.start()
        started.append(copy)

    def z_copy(w, i, k):
        m = pieces[w]
        src = halves[w].at[zp ^ step(i)[1], at(k, bw // m), :]
        return remote(src, place(w, me, k, m), w_send.at[w, i, k], w_recv.at[w, i, k], target(i))

    def y_copy(w, i, k=0):
        b = source_block(i)
        if i == n - 1:
            return remote(halves[w].at[zp], place(w, b), fwd_send.at[w, i, 0], fwd_recv.at[w, i, 0], to_y)
        spot = place(w, b, k, pieces[w])
        return remote(spot, spot, fwd_send.at[w, i, k], fwd_recv.at[w, i, k], to_y)

    def y_arrived(w):
        for i in range(n - 1):
            for k in range(pieces[w]):
                y_copy(w, i, k).wait_recv()
        y_copy(w, n - 1).wait_recv()

    own_rows = (c_in, rows2.at[1, own, :])

    def act_copy(k, stage, part):
        if stage == 0:
            slot, to, row, column = 0, to_zp, zp, mp
        else:
            row = zp ^ (part % 2)
            column = mp if part < 2 else (1 - x) * 2 + c
            slot, to = (1 + part, to_x) if stage == 1 else (3 + part, to_c)
        spot = rows2.at[k, at(row * 4 + column, tok_rows), :]
        src = own_rows[k] if stage == 0 or part == 0 else spot
        return remote(src, spot, a_send.at[k, slot], a_recv.at[k, slot], to)

    def locals_():
        return [pltpu.make_async_copy(c_in, rows2.at[0, own, :], local_sem.at[0])] + [
            pltpu.make_async_copy(halves[w].at[zp], place(w, me), local_sem.at[1 + w]) for w in range(4)
        ]

    def pass_on(k, stage, part):
        act_copy(k, stage, part).wait_recv()
        if stage == 0:
            go(act_copy(k, 1, 1))
            go(act_copy(k, 2, 1))
        else:
            go(act_copy(k, 2, 2 + part))

    inner = zh != zp if n_zh == 2 else zh < 0
    outer = jnp.logical_not(inner)

    def send_step(w, i, k):
        if i == 0:
            pl.when(outer)(z_copy(w, i, k).start)
        else:
            z_copy(w, i, k).start()

    def forward(w, i, k):
        z_copy(w, i, k).wait_recv()
        y_copy(w, i, k).start()

    def forward_step(w, i, k):
        if i == 0:
            pl.when(outer)(lambda: forward(w, i, k))
        else:
            forward(w, i, k)

    queue = (3, 2, 1, 0)
    order = [(w, k) for w in queue for k in range(pieces[w])]
    later = list(range(n - 2, -1, -1))
    go(act_copy(0, 0, 0))
    go(act_copy(0, 1, 0))

    @pl.when(inner)
    def _():
        for w, k in order:
            z_copy(w, 0, k).start()

    for w in queue:
        go(y_copy(w, n - 1))
    go(act_copy(0, 2, 0))
    for copy in locals_():
        copy.start()
    tok_load.wait()
    for j in range(tok_rows // 64):
        rows = pl.ds(j * 64, 64)
        values = tok_s[rows, :].astype(F32)
        mean = jnp.mean(values, axis=-1, keepdims=True)
        centred = values - mean
        inverse = lax.rsqrt(jnp.mean(centred * centred, axis=-1, keepdims=True) + 1e-05)
        stat_s[0, rows, :] = mean
        stat_s[1, rows, :] = inverse
        normed = centred * inverse * outer_ref[0:1, :] + outer_ref[1:2, :]
        rows2[1, at((zp * 4 + mp) * (tok_rows // 64) + j, 64), :] = normed.astype(BF16)
    go(act_copy(1, 0, 0))
    go(act_copy(1, 1, 0))
    go(act_copy(1, 2, 0))
    pl.when(inner)(lambda: forward(order[0][0], 0, order[0][1]))
    pass_on(0, 0, 0)
    pass_on(1, 0, 0)
    for w, k in order:
        for i in later:
            send_step(w, i, k)

    @pl.when(inner)
    def _():
        for w, k in order[1:]:
            forward(w, 0, k)

    pass_on(0, 1, 0)
    pass_on(1, 1, 0)
    def forward_pieces(w, start, stop):
        def one(piece, carry):
            for i in later:
                forward_step(w, i, piece)
            return carry

        lax.fori_loop(start, stop, one, 0)

    forward_pieces(3, 0, pieces[3])
    pass_on(0, 1, 1)
    forward_pieces(2, 0, pieces[2])
    pass_on(1, 1, 1)
    forward_pieces(1, 0, pieces[1] // 4)
    for copy in locals_():
        copy.wait()
    for k in (0, 1):
        for part in range(4):
            act_copy(k, 2, part).wait_recv()
    y_arrived(3)
    y_arrived(2)
    tiles = 2 * seq // CHUNK


    def low_rows(r):
        return at(n * bw // CHUNK + r, CHUNK)

    def bent(hidden):
        square = hidden * hidden
        return square, jnp.tanh(GELU * (hidden * (1.0 + 0.044715 * square)))

    def act_tile(r, carry):
        rows = at(r, CHUNK)
        for j in range(units // CHUNK):
            cols = pl.ds(j * CHUNK, CHUNK)
            hidden = jnp.dot(rows2[1, rows, :], mlp_w[1, :, cols], preferred_element_type=F32)
            hidden = hidden + hidden_bias[:, cols]
            high = hidden.astype(BF16)
            units2[1, rows, cols] = high
            grads_s[low_rows(r), cols] = (hidden - high.astype(F32)).astype(BF16)
            _, tanh = bent(hidden)
            units2[0, rows, cols] = (0.5 * hidden * (1.0 + tanh)).astype(BF16)
        return carry

    def slope_tile(r, carry):
        rows = at(r, CHUNK)
        for j in range(units // CHUNK):
            cols = pl.ds(j * CHUNK, CHUNK)
            hidden = units2[1, rows, cols].astype(F32) + grads_s[low_rows(r), cols].astype(F32)
            square, tanh = bent(hidden)
            grad = jnp.dot(rows2[0, rows, :], mlp_w[0, :, cols], preferred_element_type=F32)
            slope = 0.5 * (1.0 + tanh) + 0.5 * hidden * (1.0 - tanh * tanh) * (
                GELU * (1.0 + 3.0 * 0.044715 * square)
            )
            low = (grad * slope).astype(BF16)
            units2[1, rows, cols] = low
            hidden_sum[:, cols] += jnp.sum(low.astype(F32), axis=0, keepdims=True)
        return carry

    for w in range(4):
        for i in range(n - 1):
            for k in range(pieces[w]):
                started.extend([z_copy(w, i, k), y_copy(w, i, k)])


    low_lane = lax.broadcasted_iota(jnp.int32, (1, lanes), 1) % HEAD < ROT // 2

    def turn(values, rows, sign):
        after = pltpu.roll(values, lanes - ROT // 2, 1)
        before = pltpu.roll(values, ROT // 2, 1)
        return values * cos_ref[rows, :] + jnp.where(low_lane, after, before) * (sign * sin_ref[rows, :])

    def proj_tile(r, carry):
        rows = at(r, CHUNK)
        where = at(lax.rem(r, count), CHUNK)
        for t in range(3):
            cols = pl.ds(t * half_width, half_width)
            proj = jnp.dot(rows2[1, rows, :], qkv_w[:, cols], preferred_element_type=F32) + head_bias[:, cols]
            for g in range(half_width // lanes):
                part = proj[:, g * lanes : (g + 1) * lanes]
                if t < 2:
                    part = turn(part, where, 1.0)
                heads3[rows, pl.ds(t * half_width + g * lanes, lanes)] = part.astype(BF16)
        heads1[rows, :] = jnp.dot(rows2[0, rows, :], dense_w[...], preferred_element_type=F32).astype(BF16)
        return carry


    first = lax.broadcasted_iota(jnp.int32, (1, lanes), 1) < HEAD
    pairs = half_width // lanes

    def attend(it, carry):
        base = lax.div(it, pairs) * count
        hp = lax.rem(it, pairs)

        def cols(t):
            return at(t * pairs + hp, lanes)

        here = at(hp, lanes)
        dk_s[...] = jnp.zeros_like(dk_s)
        dv_s[...] = jnp.zeros_like(dv_s)
        diagonal = lax.broadcasted_iota(jnp.int32, (CHUNK, CHUNK), 0) <= lax.broadcasted_iota(
            jnp.int32, (CHUNK, CHUNK), 1
        )
        for qb in range(count):
            rows = at(base + qb, CHUNK)
            q_rows = heads3[rows, cols(0)] * jnp.asarray(scale, BF16)
            g_rows = heads1[rows, here]
            mixed_halves, dq_halves = [], []
            for h in (0, 1):
                mine = first if h == 0 else jnp.logical_not(first)
                q_one = jnp.where(mine, q_rows, jnp.zeros_like(q_rows))
                g_one = jnp.where(mine, g_rows, jnp.zeros_like(g_rows))
                top = None
                for j in range(qb + 1):
                    keys = heads3[at(base + j, CHUNK), cols(1)]
                    scores = lax.dot_general(keys, q_one, NT, preferred_element_type=F32)
                    if j == qb:
                        scores = jnp.where(diagonal, scores, -1e30)
                    s_s[j] = scores
                    peak = jnp.max(scores, axis=0, keepdims=True)
                    top = peak if top is None else jnp.maximum(top, peak)
                total = None
                for j in range(qb + 1):
                    e = jnp.exp(s_s[j] - top)
                    s_s[j] = e
                    part = jnp.sum(e, axis=0, keepdims=True)
                    total = part if total is None else total + part
                inverse = 1.0 / total
                mixed, inner = None, None
                for j in range(qb + 1):
                    values = heads3[at(base + j, CHUNK), cols(2)]
                    probs = s_s[j] * inverse
                    low = probs.astype(BF16)
                    part = lax.dot_general(low, values, TN, preferred_element_type=F32)
                    mixed = part if mixed is None else mixed + part
                    dv_s[h, pl.ds(j * CHUNK, CHUNK), :] += jnp.dot(low, g_rows, preferred_element_type=F32)
                    grad_probs = lax.dot_general(values, g_one, NT, preferred_element_type=F32)
                    s_s[j] = probs
                    p_s[j] = grad_probs
                    part = jnp.sum(probs * grad_probs, axis=0, keepdims=True)
                    inner = part if inner is None else inner + part
                dq = None
                for j in range(qb + 1):
                    keys = heads3[at(base + j, CHUNK), cols(1)]
                    grad_scores = (s_s[j] * (p_s[j] - inner)).astype(BF16)
                    part = lax.dot_general(grad_scores, keys, TN, preferred_element_type=F32)
                    dq = part if dq is None else dq + part
                    dk_s[h, pl.ds(j * CHUNK, CHUNK), :] += jnp.dot(
                        grad_scores, q_rows, preferred_element_type=F32
                    )
                mixed_halves.append(mixed)
                dq_halves.append(dq)
            heads1[rows, here] = jnp.where(first, *mixed_halves).astype(BF16)
            dq_s[pl.ds(qb * CHUNK, CHUNK), :] = jnp.where(first, *dq_halves) * scale
        for qb in range(count):
            rows = pl.ds(qb * CHUNK, CHUNK)
            gq = turn(dq_s[rows, :], rows, -1.0)
            gk = turn(jnp.where(first, dk_s[0, rows, :], dk_s[1, rows, :]), rows, -1.0)
            gv = jnp.where(first, dv_s[0, rows, :], dv_s[1, rows, :])
            for t, g in enumerate((gq, gk, gv)):
                low = g.astype(BF16)
                heads3[at(base + qb, CHUNK), cols(t)] = low
                head_sum[:, cols(t)] += jnp.sum(low.astype(F32), axis=0, keepdims=True)
        return carry


    def weight_grad(left, right, b, put):
        wide = max(bw, 128)
        turned = turned_s.at[pl.ds(0, wide), :]
        if bw == wide:
            turned[...] = left[:, at(b, bw)].T
        else:
            turned[...] = left[:, at(lax.div(b, wide // bw), wide)].T
        for j in range(right.shape[1] // CHUNK):
            cols = pl.ds(j * CHUNK, CHUNK)
            value = jnp.dot(turned[...], right[:, cols], preferred_element_type=F32)
            if bw < wide:
                spot = lax.rem(b, wide // bw)
                value = sum(
                    jnp.where(spot == k, value[k * bw : (k + 1) * bw], 0.0) for k in range(wide // bw)
                )
            put(cols, value)

    def mlp_grad(w, b, put):
        weight_grad(rows2.at[w], units2.at[w], b, put)

    def ym_copy(k):
        w, i = lax.div(k, n), lax.rem(k, n)
        return remote(grads_s.at[at(k, bw), :], y_mlp.at[w, i], ym_send.at[k], ym_recv.at[k], to_y)

    def ym_step(k, carry):
        w, i = lax.div(k, n), lax.rem(k, n)

        def put(cols, value):
            grads_s[at(k, bw), cols] = value.astype(BF16)

        mlp_grad(w, target_block(i) + 1 - y, put)
        ym_copy(k).start()
        return carry


    def zm_copy(k):
        w, i = lax.div(k, n), lax.rem(k, n)
        return remote(grads_s.at[at(2 * n + i, bw), :], z_mlp.at[w, i], zm_send.at[i], zm_recv.at[k], target(i))

    def zm_local(k):
        w, i = lax.div(k, n), lax.rem(k, n)
        return pltpu.make_async_copy(grads_s.at[at(2 * n + i, bw), :], z_mlp.at[w, i], zm_send.at[i])

    def zm_step(k, carry):
        w, i = lax.div(k, n), lax.rem(k, n)
        ym_copy(k).wait_recv()
        load = pltpu.make_async_copy(y_mlp.at[w, i], load_s.at[0, pl.ds(0, bw), :], load_sem.at[0])
        load.start()

        @pl.when((k >= n) & (i < n - 1))
        def _():
            zm_copy(k - n).wait_send()

        @pl.when((k >= n) & (i == n - 1))
        def _():
            zm_local(k - n).wait()

        load.wait()

        def put(cols, value):
            grads_s[at(2 * n + i, bw), cols] = (value + load_s[0, pl.ds(0, bw), cols].astype(F32)).astype(BF16)

        mlp_grad(w, target_block(i) + y, put)

        @pl.when(i < n - 1)
        def _():
            zm_copy(k).start()

        @pl.when(i == n - 1)
        def _():
            zm_local(k).start()

        return carry


    def small(left, right, y_buf, z_buf, held, ys, yr, zs, zr):
        cols = held.shape[2]

        def y_copy_(i):
            return remote(held.at[i], y_buf.at[i], ys.at[i], yr.at[i], to_y)

        def z_copy_(i):
            return remote(held.at[i], z_buf.at[i], zs.at[i], zr.at[i], target(i))

        def z_local(i):
            return pltpu.make_async_copy(held.at[i], z_buf.at[i], zs.at[i])

        def y_step(i, carry):
            def put(at_cols, value):
                held[i, :, at_cols] = value.astype(BF16)

            weight_grad(left, right, target_block(i) + 1 - y, put)
            y_copy_(i).start()
            return carry

        def z_step(i, carry):
            y_copy_(i).wait_recv()
            spot = load_s.at[0, pl.ds(0, bw), pl.ds(0, cols)]
            load = pltpu.make_async_copy(y_buf.at[i], spot, load_sem.at[0])
            load.start()
            y_copy_(i).wait_send()
            load.wait()

            def put(at_cols, value):
                held[i, :, at_cols] = (value + spot[:, at_cols].astype(F32)).astype(BF16)

            weight_grad(left, right, target_block(i) + y, put)

            @pl.when(i < n - 1)
            def _():
                z_copy_(i).start()

            @pl.when(i == n - 1)
            def _():
                z_local(i).start()

            return carry

        def finish(i, carry):
            @pl.when(i < n - 1)
            def _():
                z_copy_(i).wait_send()
                z_copy_(i).wait_recv()

            @pl.when(i == n - 1)
            def _():
                z_local(i).wait()

            return carry

        return y_step, z_step, finish

    dense_steps = small(
        rows2.at[0], heads1, y_dense, z_dense, dense_stage, yd_send, yd_recv, zd_send, zd_recv
    )
    qkv_steps = small(
        rows2.at[1], heads3, y_qkv, z_qkv, qkv_stage, yq_send, yq_recv, zq_send, zq_recv
    )


    def tile_copy(kind, slot, sem, index, to):
        return remote(
            tile_stage.at[slot], rows_in.at[kind, index], sem, tile_recv.at[kind, index], to
        )

    def c_copy(kind, t, index):
        slot = lax.rem(t, RING)
        return tile_copy(kind, slot, tile_send.at[slot], index, to_c)

    def x_copy(kind, t, index):
        return tile_copy(kind, RING + t, x_send.at[t], index, to_x)

    def zt_copy(kind, h, index):
        return tile_copy(kind, RING + h, zt_send.at[h], index, to_zp)

    def row_tiles(kind, stage):
        left, left_w = units2.at[1 - kind], mlp_w.at[1 - kind]
        right, right_w = ((heads3, qkv_w), (heads1, dense_w))[kind]

        def one(t):
            h = lax.rem(t, 2)
            if stage == 0:
                zq, xq = zp ^ (1 - lax.rem(lax.div(t, 2), 2)), x ^ (1 - lax.div(t, 4))
                block, come, to, index = zq * 4 + xq * 2 + 1 - c, (), to_c, zq * 4 + xq * 2 + h
            elif stage == 1:
                zq = zp ^ (1 - lax.div(t, 2))
                block, to, index = zq * 4 + (1 - x) * 2 + c, to_x, 8 + zq * 2 + h
                come = (zq * 4 + (1 - x) * 2 + h,)
            elif stage == 2:
                block, to, index = (1 - zp) * 4 + x * 2 + c, to_zp, 12 + h
                come = ((1 - zp) * 4 + x * 2 + h, 8 + (1 - zp) * 2 + h)
            else:
                block, to, index = zp * 4 + x * 2 + c, None, None
                come = (zp * 4 + x * 2 + h, 8 + zp * 2 + h, 12 + h)
            loads = []
            for slot, (spot, back) in enumerate(zip(come, (to_c, to_x, to_zp))):
                tile_copy(kind, 0, tile_send.at[0], spot, back).wait_recv()
                loads.append(
                    pltpu.make_async_copy(rows_in.at[kind, spot], load_s.at[slot], load_sem.at[slot])
                )
                loads[-1].start()
            for load in loads:
                load.wait()
            rows = at(block, tok_rows)
            if stage == 0:
                spot, copy = tile_stage.at[lax.rem(t, RING)], c_copy(kind, t, index)
                if kind == LATER:
                    copy.wait_send()
                else:
                    pl.when(t >= RING)(copy.wait_send)
            elif stage == 1:
                spot, copy = tile_stage.at[RING + t], x_copy(kind, t, index)
                if kind == LATER:
                    pl.when(t < 2)(zt_copy(kind, lax.rem(t, 2), index).wait_send)
                    pl.when(t >= 2)(copy.wait_send)
            elif stage == 2:
                spot, copy = tile_stage.at[RING + h], zt_copy(kind, h, index)
                x_copy(kind, h, index).wait_send()
            for j in range(half // CHUNK):
                cols = pl.ds(j * CHUNK, CHUNK)
                model = at(h * (half // CHUNK) + j, CHUNK)
                value = lax.dot_general(left[rows, :], left_w[model, :], NT, preferred_element_type=F32)
                value += lax.dot_general(right[rows, :], right_w[model, :], NT, preferred_element_type=F32)
                for k in range(len(loads)):
                    value += load_s[k, :, cols].astype(F32)
                if stage < 3:
                    spot[:, cols] = value.astype(BF16)
                else:
                    s_s[j] = value
                    if kind == 0:
                        xhat = (tok_s[:, model].astype(F32) - stat_s[0]) * stat_s[1]
                        back = rows2[0, own, model].astype(F32)
                        for row, term in enumerate((value * xhat, value, back)):
                            vec_s[row : row + 1, model] = jnp.sum(term, axis=0, keepdims=True)
            if stage < 3:
                copy.start()
            else:
                out = (grad_out, branch_out)[kind]
                copies = [
                    pltpu.make_async_copy(
                        s_s.at[j], out.at[:, at(h * (half // CHUNK) + j, CHUNK)], wide_sem.at[j]
                    )
                    for j in range(half // CHUNK)
                ]
                for copy in copies:
                    copy.start()
                for copy in copies:
                    copy.wait()

        return one


    hops = [to_zp, to_y]
    bit = 1
    while bit < n_zh:
        hops.append({"zh": zh ^ bit})
        bit *= 2
    dp_hops = len(hops)
    hops += [to_c, to_x]

    def vec_copy(k):
        return remote(vec_s, vec_in.at[k], vec_send.at[k], vec_recv.at[k], hops[k])

    def vec_first():
        for row in (3, 4):
            vec_s[row : row + 1, :] = jnp.zeros((1, width), F32)
        vec_s[3:4, at(zp, units)] = hidden_sum[...]
        for t in range(3):
            vec_s[4:5, at(t * 2 + zp, half_width)] = head_sum[:, pl.ds(t * half_width, half_width)]
        vec_copy(0).start()

    def vec_next(k):
        vec_copy(k).wait()
        vec_s[...] += vec_in[k]
        if k + 1 == dp_hops:
            sums_ref[3:5, :] = vec_s[3:5, :]
        if k + 1 < len(hops):
            vec_copy(k + 1).start()
        else:
            sums_ref[0:3, :] = vec_s[0:3, :]


    def steps(step_, total, parts):
        def share(q):
            if total == parts:
                step_(q, 0)
            else:
                lax.fori_loop(q * total // parts, (q + 1) * total // parts, step_, 0)

        return share

    def pieces_of(w):
        m = pieces[w]
        return lambda q: forward_pieces(w, lax.div(q * m, 4), lax.div((q + 1) * m, 4))

    def vector_hop(q):
        pl.when(q == 0)(vec_first)
        for k in range(5):
            @pl.when(q == k + 1)
            def _():
                for hop in range(k, len(hops) if k == 4 else k + 1):
                    vec_next(hop)

    tasks = {
        "f1": pieces_of(1),
        "f0": pieces_of(0),
        "a1": lambda q: y_arrived(1),
        "a0": lambda q: y_arrived(0),
        "proj": steps(proj_tile, tiles, 8),
        "att": steps(attend, 2 * pairs, 4),
        "act": steps(act_tile, tiles, 8),
        "slope": steps(slope_tile, tiles, 8),
        "ysET": steps(dense_steps[0], n, 4),
        "zsET": steps(dense_steps[1], n, 4),
        "ysQKV": steps(qkv_steps[0], n, 4),
        "zsQKV": steps(qkv_steps[1], n, 4),
        "ysM": steps(ym_step, 2 * n, 8),
        "zsM": steps(zm_step, 2 * n, 8),
        "vec": vector_hop,
    }
    for kind in (0, 1):
        for stage, letter in enumerate("cxzf"):
            tasks[f"r{kind}{letter}"] = row_tiles(kind, stage)

    def dispatch(part, seen):
        names = list(dict.fromkeys(part))

        def one(now, carry):
            for name in names:
                spots = [k for k, other in enumerate(part) if other == name]
                mine = functools.reduce(jnp.logical_or, [now == k for k in spots])
                q = seen[name] + sum((now >= k).astype(jnp.int32) for k in spots[1:])
                pl.when(mine)(functools.partial(tasks[name], q))
            return carry

        lax.fori_loop(0, len(part), one, 0)

    hidden_sum[...] = jnp.zeros_like(hidden_sum)
    head_sum[...] = jnp.zeros_like(head_sum)
    seen = dict.fromkeys(tasks, 0)
    seen["f1"] = 1
    for part in ORDER:
        dispatch(part, dict(seen))
        for name in part:
            seen[name] += 1

    def finish_y(k, carry):
        ym_copy(k).wait_send()
        return carry


    for copy in started:
        copy.wait_send()

    def finish_z(k, carry):
        i = lax.rem(k, n)

        @pl.when(i < n - 1)
        def _():
            zm_copy(k).wait_recv()

        @pl.when((k >= n) & (i < n - 1))
        def _():
            zm_copy(k).wait_send()

        @pl.when((k >= n) & (i == n - 1))
        def _():
            zm_local(k).wait()

        return carry

    lax.fori_loop(0, 2 * n, finish_y, 0)
    lax.fori_loop(0, 2 * n, finish_z, 0)
    for slot in range(RING):
        c_copy(0, slot, 0).wait_send()
    for t in (0, 1):
        zt_copy(0, t, 0).wait_send()
        x_copy(0, 2 + t, 0).wait_send()
    lax.fori_loop(0, n, dense_steps[2], 0)
    lax.fori_loop(0, n, qkv_steps[2], 0)


def block(n_zh, tokens, cotangent, halves, outer_params, hidden_bias, head_bias, tables):
    tok_rows, width = tokens.shape
    n = 2 * n_zh
    dp = 2 * n
    bw = width // dp
    units = halves[1].shape[2]
    half_width = halves[2].shape[2]
    triple = 3 * half_width
    seq = 4 * tok_rows
    count = seq // CHUNK
    hops = 4 + (n_zh - 1).bit_length()
    shape = jax.ShapeDtypeStruct
    vmem = pl.BlockSpec(memory_space=pltpu.VMEM)
    dma = pltpu.SemaphoreType.DMA
    outs = [
        shape((2, n, bw, units), BF16),
        shape((n, bw, half_width), BF16),
        shape((n, bw, triple), BF16),
        shape((2, n, bw, units), BF16),
        shape((n, bw, half_width), BF16),
        shape((n, bw, triple), BF16),
        shape((2, 14, tok_rows, width // 2), BF16),
        shape((tok_rows, width), F32),
        shape((tok_rows, width), F32),
        shape((8, width), F32),
    ]
    scratch = [
        pltpu.VMEM((2, 2 * seq, width), BF16),
        pltpu.VMEM((2, width, units), BF16),
        pltpu.VMEM((width, half_width), BF16),
        pltpu.VMEM((width, triple), BF16),
        pltpu.VMEM((2, 2 * seq, units), BF16),
        pltpu.VMEM((2 * seq, triple), BF16),
        pltpu.VMEM((2 * seq, half_width), BF16),
        pltpu.VMEM((seq, 2 * HEAD), F32),
        pltpu.VMEM((2, seq, 2 * HEAD), F32),
        pltpu.VMEM((2, seq, 2 * HEAD), F32),
        pltpu.VMEM((count, CHUNK, CHUNK), F32),
        pltpu.VMEM((count, CHUNK, CHUNK), F32),
        pltpu.VMEM((tok_rows, width), BF16),
        pltpu.VMEM((2, tok_rows, 1), F32),
        pltpu.VMEM((1, units), F32),
        pltpu.VMEM((1, triple), F32),
        pltpu.VMEM((8, width), F32),
        pltpu.VMEM((hops, 8, width), F32),
        pltpu.VMEM((3 * n * bw, units), BF16),
        pltpu.VMEM((n, bw, triple), BF16),
        pltpu.VMEM((n, bw, half_width), BF16),
        pltpu.VMEM((RING + 4, tok_rows, width // 2), BF16),
        pltpu.VMEM((3, tok_rows, width // 2), BF16),
        pltpu.VMEM((max(bw, 128), 2 * seq), BF16),
        dma((4, n, 4)), dma((4, n, 4)), dma((4, n, 4)), dma((4, n, 4)), dma((2, 7)), dma((2, 7)), dma((6,)),
        dma((2 * n,)), dma((2 * n,)), dma((n,)), dma((2 * n,)),
        dma((n,)), dma((n,)), dma((n,)), dma((n,)),
        dma((n,)), dma((n,)), dma((n,)), dma((n,)),
        dma((RING,)), dma((2, 14)), dma((4,)), dma((2,)), dma((3,)), dma((width // 2 // CHUNK,)), dma((hops,)), dma((hops,)),
    ]
    return pl.pallas_call(
        functools.partial(block_kernel, n_zh),
        out_shape=outs,
        in_specs=[ANY] * 6 + [vmem] * 5,
        out_specs=[ANY] * 9 + [vmem],
        scratch_shapes=scratch,
        compiler_params=pltpu.CompilerParams(
            collective_id=0, has_side_effects=True, vmem_limit_bytes=VMEM_LIMIT
        ),
    )(tokens, cotangent, *halves, outer_params, hidden_bias, head_bias, *tables)


def rotation_tables(seq):
    lane = np.arange(2 * HEAD) % HEAD
    exponent = (lane % (ROT // 2)).astype(np.float32) * np.float32(2.0 / ROT)
    inverse = np.exp(np.float32(-math.log(10000.0)) * exponent).astype(np.float32)
    angles = np.arange(seq, dtype=np.float32)[:, None] * inverse[None, :]
    cos = np.cos(angles.astype(np.float64)).astype(np.float32)
    sin = np.sin(angles.astype(np.float64)).astype(np.float32)
    turned, low = lane < ROT, lane < ROT // 2
    zero = np.zeros_like(sin)
    return np.where(turned, cos, zero + 1), np.where(turned, np.where(low, -sin, sin), zero)


def adam_update(weight, moment_one, moment_two, gradient, step_rate, decay_rate):
    first_new = BETA_ONE * moment_one + (1.0 - BETA_ONE) * gradient
    second_new = BETA_TWO * moment_two + (1.0 - BETA_TWO) * gradient * gradient
    normalized = (
        first_new
        / (1.0 - BETA_ONE**STEP)
        / (jnp.sqrt(second_new / (1.0 - BETA_TWO**STEP)) + ADAM_EPS)
    )
    return (weight - step_rate * (normalized + decay_rate * weight), first_new, second_new)


def adam_kernel(rate, turned, zp_ref, parts_ref, w_ref, one_ref, two_ref, *outs):
    parts = parts_ref[...].astype(F32)
    rows, cols = parts.shape[-2:]
    gradient = jnp.sum(parts.reshape(-1, rows, cols), axis=0)
    if turned:
        gradient = gradient.T
    shape = w_ref.shape
    new = adam_update(
        w_ref[...].reshape(gradient.shape), one_ref[...].reshape(gradient.shape),
        two_ref[...].reshape(gradient.shape), gradient, rate, MATRIX_DECAY,
    )
    for out, value in zip(outs, new):
        out[...] = value.reshape(shape)


def adam(zp, parts, state, rate, turned, grid, parts_spec, state_spec):
    shape = jax.ShapeDtypeStruct(state[0].shape, F32)
    spec = pl.BlockSpec(*state_spec)
    return pl.pallas_call(
        functools.partial(adam_kernel, rate, turned),
        out_shape=[shape] * 3,
        grid_spec=pltpu.PrefetchScalarGridSpec(
            num_scalar_prefetch=1,
            grid=grid,
            in_specs=[pl.BlockSpec(*parts_spec)] + [spec] * 3,
            out_specs=[spec] * 3,
        ),
        compiler_params=pltpu.CompilerParams(vmem_limit_bytes=VMEM_LIMIT),
    )(zp, parts, *state)


def finish_kernel(tok_ref, back_ref, grad_ref, branch_ref, outer_ref, out_ref, in_ref):
    values = tok_ref[...].astype(F32)
    out_ref[...] = (values + branch_ref[...] + outer_ref[2:3, :] + outer_ref[3:4, :]).astype(BF16)
    mean = jnp.mean(values, axis=-1, keepdims=True)
    centred = values - mean
    inverse = lax.rsqrt(jnp.mean(centred * centred, axis=-1, keepdims=True) + 1e-05)
    xhat = centred * inverse
    g = grad_ref[...] * outer_ref[0:1, :]
    inner = g - jnp.mean(g, axis=-1, keepdims=True) - xhat * jnp.mean(g * xhat, axis=-1, keepdims=True)
    in_ref[...] = back_ref[...].astype(F32) + inverse * inner


def finish(tokens, cotangent, grad_normed, branch, outer_params):
    rows, width = tokens.shape
    tile = 64
    spec = pl.BlockSpec((tile, width), lambda i: (i, 0))
    return pl.pallas_call(
        finish_kernel,
        grid=(rows // tile,),
        out_shape=[jax.ShapeDtypeStruct((rows, width), BF16), jax.ShapeDtypeStruct((rows, width), F32)],
        in_specs=[spec] * 4 + [pl.BlockSpec(outer_params.shape, lambda i: (0, 0))],
        out_specs=[spec] * 2,
        compiler_params=pltpu.CompilerParams(vmem_limit_bytes=VMEM_LIMIT),
    )(tokens, cotangent, grad_normed, branch, outer_params)


def pick(value, index, axis):
    return lax.dynamic_index_in_dim(value, index, axis, keepdims=False)


def local(
    n_zh,
    tokens, cotangent,
    qkv_weight, qkv_first, qkv_second,
    dense_weight, dense_first, dense_second,
    up_weight, up_first, up_second,
    down_weight, down_first, down_second,
    head_bias, head_first, head_second,
    hidden_bias, hidden_first, hidden_second,
    outer_params, outer_first, outer_second,
):
    zp = lax.axis_index("zp")
    tok_rows, width = tokens.shape
    seq_rows = tok_rows * 4
    bw = qkv_weight.shape[1]
    local_width = qkv_weight.shape[2]
    half_width = local_width // 2
    half_units = up_weight.shape[1] // 2

    qkv_rows = qkv_weight.reshape(3, bw, 2, half_width).transpose(2, 1, 0, 3)
    qkv_rows = qkv_rows.reshape(2, bw, 3 * half_width).astype(BF16)
    dense_rows = dense_weight.reshape(2, half_width, bw).swapaxes(1, 2).astype(BF16)
    up_rows = up_weight.reshape(bw, 2, half_units).swapaxes(0, 1).astype(BF16)
    down_rows = down_weight.reshape(2, half_units, bw).swapaxes(1, 2).astype(BF16)
    bias_half = pick(hidden_bias.reshape(2, 1, half_units), zp, 0)
    head_half = pick(head_bias.reshape(3, 2, half_width), zp, 1).reshape(1, 3 * half_width)
    outs = block(
        n_zh, tokens, cotangent, (down_rows, up_rows, dense_rows, qkv_rows), outer_params,
        bias_half, head_half, rotation_tables(seq_rows),
    )
    z_mlp, z_dense, z_qkv = outs[:3]
    grad_normed, branch, sums = outs[7:]
    layer_out, input_grad = finish(tokens, cotangent, grad_normed, branch, outer_params)

    zp_array = jnp.reshape(zp, (1,))
    z_mlp = z_mlp.reshape(2, n_zh, 2, bw, half_units)
    z_dense = z_dense.reshape(n_zh, 2, bw, half_width)
    z_qkv = z_qkv.reshape(n_zh, 2, bw, 3 * half_width)
    tile = min(bw, 128)
    new_up = adam(
        zp_array, z_mlp, (up_weight, up_first, up_second), width ** (-0.5), False,
        (2, bw // tile),
        ((1, n_zh, 1, tile, half_units), lambda h, r, zp_: (1, 0, 1 - (h ^ zp_[0]), r, 0)),
        ((tile, half_units), lambda h, r, zp_: (r, h)),
    )
    new_down = adam(
        zp_array, z_mlp, (down_weight, down_first, down_second), (4 * width) ** (-0.5), True,
        (2, half_units // CHUNK),
        ((1, n_zh, 1, bw, CHUNK), lambda h, r, zp_: (0, 0, 1 - (h ^ zp_[0]), 0, r)),
        ((CHUNK, bw), lambda h, r, zp_: (h * (half_units // CHUNK) + r, 0)),
    )
    new_dense = adam(
        zp_array, z_dense, (dense_weight, dense_first, dense_second), (width // 16) ** (-0.5), True,
        (2,),
        ((n_zh, 1, bw, half_width), lambda h, zp_: (0, 1 - (h ^ zp_[0]), 0, 0)),
        ((half_width, bw), lambda h, zp_: (h, 0)),
    )
    new_qkv = adam(
        zp_array, z_qkv, (qkv_weight, qkv_first, qkv_second), (width // 2) ** (-0.5), False,
        (3, 2),
        ((n_zh, 1, bw, half_width), lambda t, h, zp_: (0, 1 - (h ^ zp_[0]), 0, t)),
        ((1, bw, half_width), lambda t, h, zp_: (t, 0, h)),
    )
    outer_sum = jnp.concatenate([sums[:3], sums[2:3]], axis=0)
    hidden_sum = sums[3]
    head_sum = sums[4, : 3 * local_width].reshape(3, local_width)
    new_head = adam_update(head_bias, head_first, head_second, head_sum, VECTOR_RATE, 0.0)
    new_hidden = adam_update(
        hidden_bias, hidden_first, hidden_second, hidden_sum, VECTOR_RATE, 0.0
    )
    new_outer = adam_update(outer_params, outer_first, outer_second, outer_sum, VECTOR_RATE, 0.0)
    return (
        layer_out,
        input_grad,
        *new_qkv,
        *new_dense,
        *new_up,
        *new_down,
        *new_head,
        *new_hidden,
        *new_outer,
    )


def solution(mesh):
    n_zh = mesh.shape["dp"] // 4
    split = Mesh(mesh.devices.reshape(n_zh, 2, 2, 2, 2), ("zh", "zp", "y", "x", "c"))
    dp, mp = ("zh", "zp", "y"), ("x", "c")
    rows = P(dp + mp, None)
    qkv, dense, up, down = P(None, dp, mp), P(mp, dp), P(dp, mp), P(mp, dp)
    rest = (qkv,) * 3 + (dense,) * 3 + (up,) * 3 + (down,) * 3
    rest += (P(None, mp),) * 3 + (P(mp),) * 3 + (P(),) * 3
    return jax.shard_map(
        functools.partial(local, n_zh),
        mesh=split,
        in_specs=(rows, rows) + rest,
        out_specs=(rows, rows) + rest,
        check_vma=False,
    )
```

```python
import functools
import math

import jax
import jax.numpy as jnp
import numpy as np
from jax import lax
from jax.experimental import pallas as pl
from jax.experimental.pallas import tpu as pltpu
from jax.sharding import Mesh
from jax.sharding import PartitionSpec as P

HEAD = 64
ROT = 32
STEP = 10

BETA_ONE = 0.9
BETA_TWO = 0.999
ADAM_EPS = 1e-08
MATRIX_DECAY = 0.1
VECTOR_RATE = 0.1

F32 = jnp.float32
BF16 = jnp.bfloat16
MESH = pl.DeviceIdType.MESH
ANY = pl.BlockSpec(memory_space=pl.ANY)
VMEM_LIMIT = 63 * 1024 * 1024


RUNS = (
    (
        ("proj", 4), ("n1", 1), ("f1", 1), ("att", 1), ("n2", 1), ("proj", 2), ("f1", 1), ("proj", 2),
        ("f1", 1), ("att", 1), ("f0", 1), ("att", 1), ("f0", 1), ("att", 1), ("f0", 1), ("a1", 1),
    ),
    (
        ("act", 1), ("f0", 1), ("act", 2), ("ysQKV", 1), ("act", 1), ("ysET", 1), ("ysQKV", 1), ("act", 3),
        ("a0", 1), ("slope", 2), ("zsQKV", 1), ("act", 1), ("slope", 1), ("ysM", 1), ("slope", 2),
        ("zsQKV", 1), ("slope", 1), ("zsET", 1), ("ysM", 1), ("slope", 2),
    ),
    (
        ("zsM", 1), ("ysET", 1), ("ysQKV", 1), ("ysM", 1), ("ysET", 1), ("zsM", 1), ("r0c", 5),
        ("zsQKV", 1), ("r0c", 2), ("zsET", 1), ("r0c", 1), ("r0x", 1), ("zsET", 1), ("zsM", 1), ("ysM", 1),
        ("r0x", 3), ("r0z", 1), ("r1c", 1), ("ysM", 2), ("r1c", 1), ("r0z", 1), ("zsM", 1), ("r1c", 3),
        ("zsM", 1), ("r1c", 3), ("r1x", 1), ("zsM", 1), ("r1x", 1), ("r0f", 1), ("ysM", 1), ("r1x", 2),
        ("r1z", 1), ("r0f", 1), ("vec", 1), ("ysM", 1), ("vec", 1), ("r1z", 1), ("zsM", 1), ("ysET", 1),
        ("ysQKV", 1), ("vec", 3), ("zsET", 1), ("r1f", 1), ("zsM", 1), ("zsQKV", 1), ("r1f", 1),
        ("vec", 1),
    ),
)
ORDER = [[name for name, times in part for _ in range(times)] for part in RUNS]

CHUNK = 256
RING = 2
LATER = 1
GELU = math.sqrt(2.0 / math.pi)
NT = (((1,), (1,)), ((), ()))
TN = (((0,), (0,)), ((), ()))


def at(index, size):
    return pl.ds(pl.multiple_of(index * size, size), size)


def block_kernel(
    n_zh,
    tok_in, c_in, down_in, up_in, dense_in, qkv_in,
    outer_ref, hidden_bias, head_bias, cos_ref, sin_ref,
    z_mlp, z_dense, z_qkv, y_mlp, y_dense, y_qkv, rows_in, grad_out, branch_out, sums_ref,
    rows2, mlp_w, dense_w, qkv_w, units2, heads3, heads1,
    dq_s, dk_s, dv_s, s_s, p_s, tok_s, stat_s, hidden_sum, head_sum, vec_s, vec_in,
    grads_s, qkv_stage, dense_stage, tile_stage, load_s, turned_s,
    w_send, w_recv, fwd_send, fwd_recv, a_send, a_recv, local_sem,
    ym_send, ym_recv, zm_send, zm_recv, yd_send, yd_recv, zd_send, zd_recv,
    yq_send, yq_recv, zq_send, zq_recv, tile_send, tile_recv, x_send, zt_send, load_sem, wide_sem, vec_send, vec_recv,
):
    zh, zp, y = lax.axis_index("zh"), lax.axis_index("zp"), lax.axis_index("y")
    x, c = lax.axis_index("x"), lax.axis_index("c")
    mp = x * 2 + c
    n = 2 * n_zh
    tok_rows, width = tok_in.shape
    _, bw, units = up_in.shape
    half_width = dense_in.shape[2]
    seq = 4 * tok_rows
    half = width // 2
    lanes = 2 * HEAD
    count = seq // CHUNK
    scale = HEAD ** (-0.5)

    def step(i):
        back = n - 1 - i
        if isinstance(back, int):
            return back // 2, back % 2
        return lax.div(back, 2), lax.rem(back, 2)

    def source_block(i):
        s, f = step(i)
        return lax.rem(zh - s + n_zh, n_zh) * 4 + (zp ^ f) * 2 + y

    def target(i):
        s, f = step(i)
        return {"zh": lax.rem(zh + s, n_zh), "zp": zp ^ f}

    def target_block(i):
        s, f = step(i)
        return lax.rem(zh + s, n_zh) * 4 + (zp ^ f) * 2

    to_y, to_x, to_c, to_zp = {"y": 1 - y}, {"x": 1 - x}, {"c": 1 - c}, {"zp": 1 - zp}
    barrier = pltpu.get_barrier_semaphore()
    partners = [target(i) for i in range(n - 1)] + [to_y, to_x, to_c]
    for partner in partners:
        pl.semaphore_signal(barrier, inc=1, device_id=partner, device_id_type=MESH)
    own = at(zp * 4 + mp, tok_rows)
    tok_load = pltpu.make_async_copy(tok_in, tok_s, load_sem.at[0])
    tok_load.start()
    pl.semaphore_wait(barrier, len(partners))

    def remote(src, dst, send, recv, to):
        return pltpu.make_async_remote_copy(
            src_ref=src, dst_ref=dst, send_sem=send, recv_sem=recv, device_id=to, device_id_type=MESH
        )


    me = source_block(n - 1)
    halves = (down_in, up_in, dense_in, qkv_in)

    pieces = (4, 4, 2, 4) if n_zh == 2 else (1, 1, 1, 1)

    def place(w, b, k=0, m=1):
        spot = at(b * m + k, bw // m)
        if w < 2:
            return mlp_w.at[w, spot, :]
        return (dense_w, qkv_w)[w - 2].at[spot, :]

    started = []

    def go(copy):
        copy.start()
        started.append(copy)

    def z_copy(w, i, k):
        m = pieces[w]
        src = halves[w].at[zp ^ step(i)[1], at(k, bw // m), :]
        return remote(src, place(w, me, k, m), w_send.at[w, i, k], w_recv.at[w, i, k], target(i))

    def y_copy(w, i, k=0):
        b = source_block(i)
        if i == n - 1:
            return remote(halves[w].at[zp], place(w, b), fwd_send.at[w, i, 0], fwd_recv.at[w, i, 0], to_y)
        spot = place(w, b, k, pieces[w])
        return remote(spot, spot, fwd_send.at[w, i, k], fwd_recv.at[w, i, k], to_y)

    def y_arrived(w):
        for i in range(n - 1):
            for k in range(pieces[w]):
                y_copy(w, i, k).wait_recv()
        y_copy(w, n - 1).wait_recv()

    own_rows = (c_in, rows2.at[1, own, :])

    def act_copy(k, stage, part):
        if stage == 0:
            slot, to, row, column = 0, to_zp, zp, mp
        else:
            row = zp ^ (part % 2)
            column = mp if part < 2 else (1 - x) * 2 + c
            slot, to = (1 + part, to_x) if stage == 1 else (3 + part, to_c)
        spot = rows2.at[k, at(row * 4 + column, tok_rows), :]
        src = own_rows[k] if stage == 0 or part == 0 else spot
        return remote(src, spot, a_send.at[k, slot], a_recv.at[k, slot], to)

    def locals_():
        return [pltpu.make_async_copy(c_in, rows2.at[0, own, :], local_sem.at[0])] + [
            pltpu.make_async_copy(halves[w].at[zp], place(w, me), local_sem.at[1 + w]) for w in range(4)
        ]

    def pass_on(k, stage, part):
        act_copy(k, stage, part).wait_recv()
        if stage == 0:
            go(act_copy(k, 1, 1))
            go(act_copy(k, 2, 1))
        else:
            go(act_copy(k, 2, 2 + part))

    inner = zh != zp if n_zh == 2 else zh < 0
    outer = jnp.logical_not(inner)

    def send_step(w, i, k):
        if i == 0:
            pl.when(outer)(z_copy(w, i, k).start)
        else:
            z_copy(w, i, k).start()

    def forward(w, i, k):
        z_copy(w, i, k).wait_recv()
        y_copy(w, i, k).start()

    def forward_step(w, i, k):
        if i == 0:
            pl.when(outer)(lambda: forward(w, i, k))
        else:
            forward(w, i, k)

    queue = (3, 2, 1, 0)
    order = [(w, k) for w in queue for k in range(pieces[w])]
    later = list(range(n - 2, -1, -1))
    go(act_copy(0, 0, 0))
    go(act_copy(0, 1, 0))

    @pl.when(inner)
    def _():
        for w, k in order:
            z_copy(w, 0, k).start()

    for w in queue:
        go(y_copy(w, n - 1))
    go(act_copy(0, 2, 0))
    for copy in locals_():
        copy.start()
    tok_load.wait()
    for j in range(tok_rows // 64):
        rows = pl.ds(j * 64, 64)
        values = tok_s[rows, :].astype(F32)
        mean = jnp.mean(values, axis=-1, keepdims=True)
        centred = values - mean
        inverse = lax.rsqrt(jnp.mean(centred * centred, axis=-1, keepdims=True) + 1e-05)
        stat_s[0, rows, :] = mean
        stat_s[1, rows, :] = inverse
        normed = centred * inverse * outer_ref[0:1, :] + outer_ref[1:2, :]
        rows2[1, at((zp * 4 + mp) * (tok_rows // 64) + j, 64), :] = normed.astype(BF16)
    go(act_copy(1, 0, 0))
    go(act_copy(1, 1, 0))
    go(act_copy(1, 2, 0))
    pl.when(inner)(lambda: forward(order[0][0], 0, order[0][1]))
    pass_on(0, 0, 0)
    pass_on(1, 0, 0)
    for w, k in order:
        for i in later:
            send_step(w, i, k)

    @pl.when(inner)
    def _():
        for w, k in order[1:]:
            forward(w, 0, k)

    pass_on(0, 1, 0)
    pass_on(1, 1, 0)
    def forward_pieces(w, start, stop):
        def one(piece, carry):
            for i in later:
                forward_step(w, i, piece)
            return carry

        lax.fori_loop(start, stop, one, 0)

    forward_pieces(3, 0, pieces[3])
    pass_on(0, 1, 1)
    forward_pieces(2, 0, pieces[2])
    forward_pieces(1, 0, pieces[1] // 4)
    started.append(act_copy(1, 2, 3))
    for copy in locals_():
        copy.wait()
    for k in (0, 1):
        for part in (0, 2):
            act_copy(k, 2, part).wait_recv()
    y_arrived(3)
    y_arrived(2)
    tiles = 2 * seq // CHUNK


    def low_rows(r):
        return at(n * bw // CHUNK + r, CHUNK)

    def bent(hidden):
        square = hidden * hidden
        return square, jnp.tanh(GELU * (hidden * (1.0 + 0.044715 * square)))

    def act_tile(r, carry):
        rows = at(r, CHUNK)
        for j in range(units // CHUNK):
            cols = pl.ds(j * CHUNK, CHUNK)
            hidden = jnp.dot(rows2[1, rows, :], mlp_w[1, :, cols], preferred_element_type=F32)
            hidden = hidden + hidden_bias[:, cols]
            high = hidden.astype(BF16)
            units2[1, rows, cols] = high
            grads_s[low_rows(r), cols] = (hidden - high.astype(F32)).astype(BF16)
            _, tanh = bent(hidden)
            units2[0, rows, cols] = (0.5 * hidden * (1.0 + tanh)).astype(BF16)
        return carry

    def slope_tile(r, carry):
        rows = at(r, CHUNK)
        for j in range(units // CHUNK):
            cols = pl.ds(j * CHUNK, CHUNK)
            hidden = units2[1, rows, cols].astype(F32) + grads_s[low_rows(r), cols].astype(F32)
            square, tanh = bent(hidden)
            grad = jnp.dot(rows2[0, rows, :], mlp_w[0, :, cols], preferred_element_type=F32)
            slope = 0.5 * (1.0 + tanh) + 0.5 * hidden * (1.0 - tanh * tanh) * (
                GELU * (1.0 + 3.0 * 0.044715 * square)
            )
            low = (grad * slope).astype(BF16)
            units2[1, rows, cols] = low
            hidden_sum[:, cols] += jnp.sum(low.astype(F32), axis=0, keepdims=True)
        return carry

    for w in range(4):
        for i in range(n - 1):
            for k in range(pieces[w]):
                started.extend([z_copy(w, i, k), y_copy(w, i, k)])


    low_lane = lax.broadcasted_iota(jnp.int32, (1, lanes), 1) % HEAD < ROT // 2

    def turn(values, rows, sign):
        after = pltpu.roll(values, lanes - ROT // 2, 1)
        before = pltpu.roll(values, ROT // 2, 1)
        return values * cos_ref[rows, :] + jnp.where(low_lane, after, before) * (sign * sin_ref[rows, :])

    def proj_tile(r, carry):
        rows = at((lax.div(r, count) ^ zp) * count + lax.rem(r, count), CHUNK)
        where = at(lax.rem(r, count), CHUNK)
        for t in range(3):
            cols = pl.ds(t * half_width, half_width)
            proj = jnp.dot(rows2[1, rows, :], qkv_w[:, cols], preferred_element_type=F32) + head_bias[:, cols]
            for g in range(half_width // lanes):
                part = proj[:, g * lanes : (g + 1) * lanes]
                if t < 2:
                    part = turn(part, where, 1.0)
                heads3[rows, pl.ds(t * half_width + g * lanes, lanes)] = part.astype(BF16)
        heads1[rows, :] = jnp.dot(rows2[0, rows, :], dense_w[...], preferred_element_type=F32).astype(BF16)
        return carry


    first = lax.broadcasted_iota(jnp.int32, (1, lanes), 1) < HEAD
    pairs = half_width // lanes

    def attend(it, carry):
        base = (lax.div(it, pairs) ^ zp) * count
        hp = lax.rem(it, pairs)

        def cols(t):
            return at(t * pairs + hp, lanes)

        here = at(hp, lanes)
        dk_s[...] = jnp.zeros_like(dk_s)
        dv_s[...] = jnp.zeros_like(dv_s)
        diagonal = lax.broadcasted_iota(jnp.int32, (CHUNK, CHUNK), 0) <= lax.broadcasted_iota(
            jnp.int32, (CHUNK, CHUNK), 1
        )
        for qb in range(count):
            rows = at(base + qb, CHUNK)
            q_rows = heads3[rows, cols(0)] * jnp.asarray(scale, BF16)
            g_rows = heads1[rows, here]
            mixed_halves, dq_halves = [], []
            for h in (0, 1):
                mine = first if h == 0 else jnp.logical_not(first)
                q_one = jnp.where(mine, q_rows, jnp.zeros_like(q_rows))
                g_one = jnp.where(mine, g_rows, jnp.zeros_like(g_rows))
                top = None
                for j in range(qb + 1):
                    keys = heads3[at(base + j, CHUNK), cols(1)]
                    scores = lax.dot_general(keys, q_one, NT, preferred_element_type=F32)
                    if j == qb:
                        scores = jnp.where(diagonal, scores, -1e30)
                    s_s[j] = scores
                    peak = jnp.max(scores, axis=0, keepdims=True)
                    top = peak if top is None else jnp.maximum(top, peak)
                total = None
                for j in range(qb + 1):
                    e = jnp.exp(s_s[j] - top)
                    s_s[j] = e
                    part = jnp.sum(e, axis=0, keepdims=True)
                    total = part if total is None else total + part
                inverse = 1.0 / total
                mixed, inner = None, None
                for j in range(qb + 1):
                    values = heads3[at(base + j, CHUNK), cols(2)]
                    probs = s_s[j] * inverse
                    low = probs.astype(BF16)
                    part = lax.dot_general(low, values, TN, preferred_element_type=F32)
                    mixed = part if mixed is None else mixed + part
                    dv_s[h, pl.ds(j * CHUNK, CHUNK), :] += jnp.dot(low, g_rows, preferred_element_type=F32)
                    grad_probs = lax.dot_general(values, g_one, NT, preferred_element_type=F32)
                    s_s[j] = probs
                    p_s[j] = grad_probs
                    part = jnp.sum(probs * grad_probs, axis=0, keepdims=True)
                    inner = part if inner is None else inner + part
                dq = None
                for j in range(qb + 1):
                    keys = heads3[at(base + j, CHUNK), cols(1)]
                    grad_scores = (s_s[j] * (p_s[j] - inner)).astype(BF16)
                    part = lax.dot_general(grad_scores, keys, TN, preferred_element_type=F32)
                    dq = part if dq is None else dq + part
                    dk_s[h, pl.ds(j * CHUNK, CHUNK), :] += jnp.dot(
                        grad_scores, q_rows, preferred_element_type=F32
                    )
                mixed_halves.append(mixed)
                dq_halves.append(dq)
            heads1[rows, here] = jnp.where(first, *mixed_halves).astype(BF16)
            dq_s[pl.ds(qb * CHUNK, CHUNK), :] = jnp.where(first, *dq_halves) * scale
        for qb in range(count):
            rows = pl.ds(qb * CHUNK, CHUNK)
            gq = turn(dq_s[rows, :], rows, -1.0)
            gk = turn(jnp.where(first, dk_s[0, rows, :], dk_s[1, rows, :]), rows, -1.0)
            gv = jnp.where(first, dv_s[0, rows, :], dv_s[1, rows, :])
            for t, g in enumerate((gq, gk, gv)):
                low = g.astype(BF16)
                heads3[at(base + qb, CHUNK), cols(t)] = low
                head_sum[:, cols(t)] += jnp.sum(low.astype(F32), axis=0, keepdims=True)
        return carry


    def weight_grad(left, right, b, put):
        wide = max(bw, 128)
        turned = turned_s.at[pl.ds(0, wide), :]
        if bw == wide:
            turned[...] = left[:, at(b, bw)].T
        else:
            turned[...] = left[:, at(lax.div(b, wide // bw), wide)].T
        for j in range(right.shape[1] // CHUNK):
            cols = pl.ds(j * CHUNK, CHUNK)
            value = jnp.dot(turned[...], right[:, cols], preferred_element_type=F32)
            if bw < wide:
                spot = lax.rem(b, wide // bw)
                value = sum(
                    jnp.where(spot == k, value[k * bw : (k + 1) * bw], 0.0) for k in range(wide // bw)
                )
            put(cols, value)

    def mlp_grad(w, b, put):
        weight_grad(rows2.at[w], units2.at[w], b, put)

    def ym_copy(k):
        w, i = lax.div(k, n), lax.rem(k, n)
        return remote(grads_s.at[at(k, bw), :], y_mlp.at[w, i], ym_send.at[k], ym_recv.at[k], to_y)

    def ym_step(k, carry):
        w, i = lax.div(k, n), lax.rem(k, n)

        def put(cols, value):
            grads_s[at(k, bw), cols] = value.astype(BF16)

        mlp_grad(w, target_block(i) + 1 - y, put)
        ym_copy(k).start()
        return carry


    def zm_copy(k):
        w, i = lax.div(k, n), lax.rem(k, n)
        return remote(grads_s.at[at(2 * n + i, bw), :], z_mlp.at[w, i], zm_send.at[i], zm_recv.at[k], target(i))

    def zm_local(k):
        w, i = lax.div(k, n), lax.rem(k, n)
        return pltpu.make_async_copy(grads_s.at[at(2 * n + i, bw), :], z_mlp.at[w, i], zm_send.at[i])

    def zm_step(k, carry):
        w, i = lax.div(k, n), lax.rem(k, n)
        ym_copy(k).wait_recv()
        load = pltpu.make_async_copy(y_mlp.at[w, i], load_s.at[0, pl.ds(0, bw), :], load_sem.at[0])
        load.start()

        @pl.when((k >= n) & (i < n - 1))
        def _():
            zm_copy(k - n).wait_send()

        @pl.when((k >= n) & (i == n - 1))
        def _():
            zm_local(k - n).wait()

        load.wait()

        def put(cols, value):
            grads_s[at(2 * n + i, bw), cols] = (value + load_s[0, pl.ds(0, bw), cols].astype(F32)).astype(BF16)

        mlp_grad(w, target_block(i) + y, put)

        @pl.when(i < n - 1)
        def _():
            zm_copy(k).start()

        @pl.when(i == n - 1)
        def _():
            zm_local(k).start()

        return carry


    def small(left, right, y_buf, z_buf, held, ys, yr, zs, zr):
        cols = held.shape[2]

        def y_copy_(i):
            return remote(held.at[i], y_buf.at[i], ys.at[i], yr.at[i], to_y)

        def z_copy_(i):
            return remote(held.at[i], z_buf.at[i], zs.at[i], zr.at[i], target(i))

        def z_local(i):
            return pltpu.make_async_copy(held.at[i], z_buf.at[i], zs.at[i])

        def y_step(i, carry):
            def put(at_cols, value):
                held[i, :, at_cols] = value.astype(BF16)

            weight_grad(left, right, target_block(i) + 1 - y, put)
            y_copy_(i).start()
            return carry

        def z_step(i, carry):
            y_copy_(i).wait_recv()
            spot = load_s.at[0, pl.ds(0, bw), pl.ds(0, cols)]
            load = pltpu.make_async_copy(y_buf.at[i], spot, load_sem.at[0])
            load.start()
            y_copy_(i).wait_send()
            load.wait()

            def put(at_cols, value):
                held[i, :, at_cols] = (value + spot[:, at_cols].astype(F32)).astype(BF16)

            weight_grad(left, right, target_block(i) + y, put)

            @pl.when(i < n - 1)
            def _():
                z_copy_(i).start()

            @pl.when(i == n - 1)
            def _():
                z_local(i).start()

            return carry

        def finish(i, carry):
            @pl.when(i < n - 1)
            def _():
                z_copy_(i).wait_send()
                z_copy_(i).wait_recv()

            @pl.when(i == n - 1)
            def _():
                z_local(i).wait()

            return carry

        return y_step, z_step, finish

    dense_steps = small(
        rows2.at[0], heads1, y_dense, z_dense, dense_stage, yd_send, yd_recv, zd_send, zd_recv
    )
    qkv_steps = small(
        rows2.at[1], heads3, y_qkv, z_qkv, qkv_stage, yq_send, yq_recv, zq_send, zq_recv
    )


    def tile_copy(kind, slot, sem, index, to):
        return remote(
            tile_stage.at[slot], rows_in.at[kind, index], sem, tile_recv.at[kind, index], to
        )

    def c_copy(kind, t, index):
        slot = lax.rem(t, RING)
        return tile_copy(kind, slot, tile_send.at[slot], index, to_c)

    def x_copy(kind, t, index):
        return tile_copy(kind, RING + t, x_send.at[t], index, to_x)

    def zt_copy(kind, h, index):
        return tile_copy(kind, RING + h, zt_send.at[h], index, to_zp)

    def row_tiles(kind, stage):
        left, left_w = units2.at[1 - kind], mlp_w.at[1 - kind]
        right, right_w = ((heads3, qkv_w), (heads1, dense_w))[kind]

        def one(t):
            h = lax.rem(t, 2)
            if stage == 0:
                zq, xq = zp ^ (1 - lax.rem(lax.div(t, 2), 2)), x ^ (1 - lax.div(t, 4))
                block, come, to, index = zq * 4 + xq * 2 + 1 - c, (), to_c, zq * 4 + xq * 2 + h
            elif stage == 1:
                zq = zp ^ (1 - lax.div(t, 2))
                block, to, index = zq * 4 + (1 - x) * 2 + c, to_x, 8 + zq * 2 + h
                come = (zq * 4 + (1 - x) * 2 + h,)
            elif stage == 2:
                block, to, index = (1 - zp) * 4 + x * 2 + c, to_zp, 12 + h
                come = ((1 - zp) * 4 + x * 2 + h, 8 + (1 - zp) * 2 + h)
            else:
                block, to, index = zp * 4 + x * 2 + c, None, None
                come = (zp * 4 + x * 2 + h, 8 + zp * 2 + h, 12 + h)
            loads = []
            for slot, (spot, back) in enumerate(zip(come, (to_c, to_x, to_zp))):
                tile_copy(kind, 0, tile_send.at[0], spot, back).wait_recv()
                loads.append(
                    pltpu.make_async_copy(rows_in.at[kind, spot], load_s.at[slot], load_sem.at[slot])
                )
                loads[-1].start()
            for load in loads:
                load.wait()
            rows = at(block, tok_rows)
            if stage == 0:
                spot, copy = tile_stage.at[lax.rem(t, RING)], c_copy(kind, t, index)
                if kind == LATER:
                    copy.wait_send()
                else:
                    pl.when(t >= RING)(copy.wait_send)
            elif stage == 1:
                spot, copy = tile_stage.at[RING + t], x_copy(kind, t, index)
                if kind == LATER:
                    pl.when(t < 2)(zt_copy(kind, lax.rem(t, 2), index).wait_send)
                    pl.when(t >= 2)(copy.wait_send)
            elif stage == 2:
                spot, copy = tile_stage.at[RING + h], zt_copy(kind, h, index)
                x_copy(kind, h, index).wait_send()
            for j in range(half // CHUNK):
                cols = pl.ds(j * CHUNK, CHUNK)
                model = at(h * (half // CHUNK) + j, CHUNK)
                value = lax.dot_general(left[rows, :], left_w[model, :], NT, preferred_element_type=F32)
                value += lax.dot_general(right[rows, :], right_w[model, :], NT, preferred_element_type=F32)
                for k in range(len(loads)):
                    value += load_s[k, :, cols].astype(F32)
                if stage < 3:
                    spot[:, cols] = value.astype(BF16)
                else:
                    s_s[j] = value
                    if kind == 0:
                        xhat = (tok_s[:, model].astype(F32) - stat_s[0]) * stat_s[1]
                        back = rows2[0, own, model].astype(F32)
                        for row, term in enumerate((value * xhat, value, back)):
                            vec_s[row : row + 1, model] = jnp.sum(term, axis=0, keepdims=True)
            if stage < 3:
                copy.start()
            else:
                out = (grad_out, branch_out)[kind]
                copies = [
                    pltpu.make_async_copy(
                        s_s.at[j], out.at[:, at(h * (half // CHUNK) + j, CHUNK)], wide_sem.at[j]
                    )
                    for j in range(half // CHUNK)
                ]
                for copy in copies:
                    copy.start()
                for copy in copies:
                    copy.wait()

        return one


    hops = [to_zp, to_y]
    bit = 1
    while bit < n_zh:
        hops.append({"zh": zh ^ bit})
        bit *= 2
    dp_hops = len(hops)
    hops += [to_c, to_x]

    def vec_copy(k):
        return remote(vec_s, vec_in.at[k], vec_send.at[k], vec_recv.at[k], hops[k])

    def vec_first():
        for row in (3, 4):
            vec_s[row : row + 1, :] = jnp.zeros((1, width), F32)
        vec_s[3:4, at(zp, units)] = hidden_sum[...]
        for t in range(3):
            vec_s[4:5, at(t * 2 + zp, half_width)] = head_sum[:, pl.ds(t * half_width, half_width)]
        vec_copy(0).start()

    def vec_next(k):
        vec_copy(k).wait()
        vec_s[...] += vec_in[k]
        if k + 1 == dp_hops:
            sums_ref[3:5, :] = vec_s[3:5, :]
        if k + 1 < len(hops):
            vec_copy(k + 1).start()
        else:
            sums_ref[0:3, :] = vec_s[0:3, :]


    def steps(step_, total, parts):
        def share(q):
            if total == parts:
                step_(q, 0)
            else:
                lax.fori_loop(q * total // parts, (q + 1) * total // parts, step_, 0)

        return share

    def pieces_of(w):
        m = pieces[w]
        return lambda q: forward_pieces(w, lax.div(q * m, 4), lax.div((q + 1) * m, 4))

    def vector_hop(q):
        pl.when(q == 0)(vec_first)
        for k in range(5):
            @pl.when(q == k + 1)
            def _():
                for hop in range(k, len(hops) if k == 4 else k + 1):
                    vec_next(hop)

    def pass_last(q):
        act_copy(1, 1, 1).wait_recv()
        act_copy(1, 2, 3).start()

    def rows_arrived(q):
        for k in (0, 1):
            for part in (1, 3):
                act_copy(k, 2, part).wait_recv()

    tasks = {
        "n1": pass_last,
        "n2": rows_arrived,
        "f1": pieces_of(1),
        "f0": pieces_of(0),
        "a1": lambda q: y_arrived(1),
        "a0": lambda q: y_arrived(0),
        "proj": steps(proj_tile, tiles, 8),
        "att": steps(attend, 2 * pairs, 4),
        "act": steps(act_tile, tiles, 8),
        "slope": steps(slope_tile, tiles, 8),
        "ysET": steps(dense_steps[0], n, 4),
        "zsET": steps(dense_steps[1], n, 4),
        "ysQKV": steps(qkv_steps[0], n, 4),
        "zsQKV": steps(qkv_steps[1], n, 4),
        "ysM": steps(ym_step, 2 * n, 8),
        "zsM": steps(zm_step, 2 * n, 8),
        "vec": vector_hop,
    }
    for kind in (0, 1):
        for stage, letter in enumerate("cxzf"):
            tasks[f"r{kind}{letter}"] = row_tiles(kind, stage)

    def dispatch(part, seen):
        names = list(dict.fromkeys(part))

        def one(now, carry):
            for name in names:
                spots = [k for k, other in enumerate(part) if other == name]
                mine = functools.reduce(jnp.logical_or, [now == k for k in spots])
                q = seen[name] + sum((now >= k).astype(jnp.int32) for k in spots[1:])
                pl.when(mine)(functools.partial(tasks[name], q))
            return carry

        lax.fori_loop(0, len(part), one, 0)

    hidden_sum[...] = jnp.zeros_like(hidden_sum)
    head_sum[...] = jnp.zeros_like(head_sum)
    seen = dict.fromkeys(tasks, 0)
    seen["f1"] = 1
    for part in ORDER:
        dispatch(part, dict(seen))
        for name in part:
            seen[name] += 1

    def finish_y(k, carry):
        ym_copy(k).wait_send()
        return carry


    for copy in started:
        copy.wait_send()

    def finish_z(k, carry):
        i = lax.rem(k, n)

        @pl.when(i < n - 1)
        def _():
            zm_copy(k).wait_recv()

        @pl.when((k >= n) & (i < n - 1))
        def _():
            zm_copy(k).wait_send()

        @pl.when((k >= n) & (i == n - 1))
        def _():
            zm_local(k).wait()

        return carry

    lax.fori_loop(0, 2 * n, finish_y, 0)
    lax.fori_loop(0, 2 * n, finish_z, 0)
    for slot in range(RING):
        c_copy(0, slot, 0).wait_send()
    for t in (0, 1):
        zt_copy(0, t, 0).wait_send()
        x_copy(0, 2 + t, 0).wait_send()
    lax.fori_loop(0, n, dense_steps[2], 0)
    lax.fori_loop(0, n, qkv_steps[2], 0)


def block(n_zh, tokens, cotangent, halves, outer_params, hidden_bias, head_bias, tables):
    tok_rows, width = tokens.shape
    n = 2 * n_zh
    dp = 2 * n
    bw = width // dp
    units = halves[1].shape[2]
    half_width = halves[2].shape[2]
    triple = 3 * half_width
    seq = 4 * tok_rows
    count = seq // CHUNK
    hops = 4 + (n_zh - 1).bit_length()
    shape = jax.ShapeDtypeStruct
    vmem = pl.BlockSpec(memory_space=pltpu.VMEM)
    dma = pltpu.SemaphoreType.DMA
    outs = [
        shape((2, n, bw, units), BF16),
        shape((n, bw, half_width), BF16),
        shape((n, bw, triple), BF16),
        shape((2, n, bw, units), BF16),
        shape((n, bw, half_width), BF16),
        shape((n, bw, triple), BF16),
        shape((2, 14, tok_rows, width // 2), BF16),
        shape((tok_rows, width), F32),
        shape((tok_rows, width), F32),
        shape((8, width), F32),
    ]
    scratch = [
        pltpu.VMEM((2, 2 * seq, width), BF16),
        pltpu.VMEM((2, width, units), BF16),
        pltpu.VMEM((width, half_width), BF16),
        pltpu.VMEM((width, triple), BF16),
        pltpu.VMEM((2, 2 * seq, units), BF16),
        pltpu.VMEM((2 * seq, triple), BF16),
        pltpu.VMEM((2 * seq, half_width), BF16),
        pltpu.VMEM((seq, 2 * HEAD), F32),
        pltpu.VMEM((2, seq, 2 * HEAD), F32),
        pltpu.VMEM((2, seq, 2 * HEAD), F32),
        pltpu.VMEM((count, CHUNK, CHUNK), F32),
        pltpu.VMEM((count, CHUNK, CHUNK), F32),
        pltpu.VMEM((tok_rows, width), BF16),
        pltpu.VMEM((2, tok_rows, 1), F32),
        pltpu.VMEM((1, units), F32),
        pltpu.VMEM((1, triple), F32),
        pltpu.VMEM((8, width), F32),
        pltpu.VMEM((hops, 8, width), F32),
        pltpu.VMEM((3 * n * bw, units), BF16),
        pltpu.VMEM((n, bw, triple), BF16),
        pltpu.VMEM((n, bw, half_width), BF16),
        pltpu.VMEM((RING + 4, tok_rows, width // 2), BF16),
        pltpu.VMEM((3, tok_rows, width // 2), BF16),
        pltpu.VMEM((max(bw, 128), 2 * seq), BF16),
        dma((4, n, 4)), dma((4, n, 4)), dma((4, n, 4)), dma((4, n, 4)), dma((2, 7)), dma((2, 7)), dma((6,)),
        dma((2 * n,)), dma((2 * n,)), dma((n,)), dma((2 * n,)),
        dma((n,)), dma((n,)), dma((n,)), dma((n,)),
        dma((n,)), dma((n,)), dma((n,)), dma((n,)),
        dma((RING,)), dma((2, 14)), dma((4,)), dma((2,)), dma((3,)), dma((width // 2 // CHUNK,)), dma((hops,)), dma((hops,)),
    ]
    return pl.pallas_call(
        functools.partial(block_kernel, n_zh),
        out_shape=outs,
        in_specs=[ANY] * 6 + [vmem] * 5,
        out_specs=[ANY] * 9 + [vmem],
        scratch_shapes=scratch,
        compiler_params=pltpu.CompilerParams(
            collective_id=0, has_side_effects=True, vmem_limit_bytes=VMEM_LIMIT
        ),
    )(tokens, cotangent, *halves, outer_params, hidden_bias, head_bias, *tables)


def rotation_tables(seq):
    lane = np.arange(2 * HEAD) % HEAD
    exponent = (lane % (ROT // 2)).astype(np.float32) * np.float32(2.0 / ROT)
    inverse = np.exp(np.float32(-math.log(10000.0)) * exponent).astype(np.float32)
    angles = np.arange(seq, dtype=np.float32)[:, None] * inverse[None, :]
    cos = np.cos(angles.astype(np.float64)).astype(np.float32)
    sin = np.sin(angles.astype(np.float64)).astype(np.float32)
    turned, low = lane < ROT, lane < ROT // 2
    zero = np.zeros_like(sin)
    return np.where(turned, cos, zero + 1), np.where(turned, np.where(low, -sin, sin), zero)


def adam_update(weight, moment_one, moment_two, gradient, step_rate, decay_rate):
    first_new = BETA_ONE * moment_one + (1.0 - BETA_ONE) * gradient
    second_new = BETA_TWO * moment_two + (1.0 - BETA_TWO) * gradient * gradient
    normalized = (
        first_new
        / (1.0 - BETA_ONE**STEP)
        / (jnp.sqrt(second_new / (1.0 - BETA_TWO**STEP)) + ADAM_EPS)
    )
    return (weight - step_rate * (normalized + decay_rate * weight), first_new, second_new)


def adam_kernel(rate, turned, zp_ref, parts_ref, w_ref, one_ref, two_ref, *outs):
    parts = parts_ref[...].astype(F32)
    rows, cols = parts.shape[-2:]
    gradient = jnp.sum(parts.reshape(-1, rows, cols), axis=0)
    if turned:
        gradient = gradient.T
    shape = w_ref.shape
    new = adam_update(
        w_ref[...].reshape(gradient.shape), one_ref[...].reshape(gradient.shape),
        two_ref[...].reshape(gradient.shape), gradient, rate, MATRIX_DECAY,
    )
    for out, value in zip(outs, new):
        out[...] = value.reshape(shape)


def adam(zp, parts, state, rate, turned, grid, parts_spec, state_spec):
    shape = jax.ShapeDtypeStruct(state[0].shape, F32)
    spec = pl.BlockSpec(*state_spec)
    return pl.pallas_call(
        functools.partial(adam_kernel, rate, turned),
        out_shape=[shape] * 3,
        grid_spec=pltpu.PrefetchScalarGridSpec(
            num_scalar_prefetch=1,
            grid=grid,
            in_specs=[pl.BlockSpec(*parts_spec)] + [spec] * 3,
            out_specs=[spec] * 3,
        ),
        compiler_params=pltpu.CompilerParams(vmem_limit_bytes=VMEM_LIMIT),
    )(zp, parts, *state)


def finish_kernel(tok_ref, back_ref, grad_ref, branch_ref, outer_ref, out_ref, in_ref):
    values = tok_ref[...].astype(F32)
    out_ref[...] = (values + branch_ref[...] + outer_ref[2:3, :] + outer_ref[3:4, :]).astype(BF16)
    mean = jnp.mean(values, axis=-1, keepdims=True)
    centred = values - mean
    inverse = lax.rsqrt(jnp.mean(centred * centred, axis=-1, keepdims=True) + 1e-05)
    xhat = centred * inverse
    g = grad_ref[...] * outer_ref[0:1, :]
    inner = g - jnp.mean(g, axis=-1, keepdims=True) - xhat * jnp.mean(g * xhat, axis=-1, keepdims=True)
    in_ref[...] = back_ref[...].astype(F32) + inverse * inner


def finish(tokens, cotangent, grad_normed, branch, outer_params):
    rows, width = tokens.shape
    tile = 32
    spec = pl.BlockSpec((tile, width), lambda i: (i, 0))
    return pl.pallas_call(
        finish_kernel,
        grid=(rows // tile,),
        out_shape=[jax.ShapeDtypeStruct((rows, width), BF16), jax.ShapeDtypeStruct((rows, width), F32)],
        in_specs=[spec] * 4 + [pl.BlockSpec(outer_params.shape, lambda i: (0, 0))],
        out_specs=[spec] * 2,
        compiler_params=pltpu.CompilerParams(vmem_limit_bytes=VMEM_LIMIT),
    )(tokens, cotangent, grad_normed, branch, outer_params)


def pick(value, index, axis):
    return lax.dynamic_index_in_dim(value, index, axis, keepdims=False)


def local(
    n_zh,
    tokens, cotangent,
    qkv_weight, qkv_first, qkv_second,
    dense_weight, dense_first, dense_second,
    up_weight, up_first, up_second,
    down_weight, down_first, down_second,
    head_bias, head_first, head_second,
    hidden_bias, hidden_first, hidden_second,
    outer_params, outer_first, outer_second,
):
    zp = lax.axis_index("zp")
    tok_rows, width = tokens.shape
    seq_rows = tok_rows * 4
    bw = qkv_weight.shape[1]
    local_width = qkv_weight.shape[2]
    half_width = local_width // 2
    half_units = up_weight.shape[1] // 2

    qkv_rows = qkv_weight.reshape(3, bw, 2, half_width).transpose(2, 1, 0, 3)
    qkv_rows = qkv_rows.reshape(2, bw, 3 * half_width).astype(BF16)
    dense_rows = dense_weight.reshape(2, half_width, bw).swapaxes(1, 2).astype(BF16)
    up_rows = up_weight.reshape(bw, 2, half_units).swapaxes(0, 1).astype(BF16)
    down_rows = down_weight.reshape(2, half_units, bw).swapaxes(1, 2).astype(BF16)
    bias_half = pick(hidden_bias.reshape(2, 1, half_units), zp, 0)
    head_half = pick(head_bias.reshape(3, 2, half_width), zp, 1).reshape(1, 3 * half_width)
    outs = block(
        n_zh, tokens, cotangent, (down_rows, up_rows, dense_rows, qkv_rows), outer_params,
        bias_half, head_half, rotation_tables(seq_rows),
    )
    z_mlp, z_dense, z_qkv = outs[:3]
    grad_normed, branch, sums = outs[7:]
    layer_out, input_grad = finish(tokens, cotangent, grad_normed, branch, outer_params)

    zp_array = jnp.reshape(zp, (1,))
    z_mlp = z_mlp.reshape(2, n_zh, 2, bw, half_units)
    z_dense = z_dense.reshape(n_zh, 2, bw, half_width)
    z_qkv = z_qkv.reshape(n_zh, 2, bw, 3 * half_width)
    tile = min(bw, 32)
    new_up = adam(
        zp_array, z_mlp, (up_weight, up_first, up_second), width ** (-0.5), False,
        (2, bw // tile),
        ((1, n_zh, 1, tile, half_units), lambda h, r, zp_: (1, 0, 1 - (h ^ zp_[0]), r, 0)),
        ((tile, half_units), lambda h, r, zp_: (r, h)),
    )
    new_down = adam(
        zp_array, z_mlp, (down_weight, down_first, down_second), (4 * width) ** (-0.5), True,
        (2, half_units // CHUNK),
        ((1, n_zh, 1, bw, CHUNK), lambda h, r, zp_: (0, 0, 1 - (h ^ zp_[0]), 0, r)),
        ((CHUNK, bw), lambda h, r, zp_: (h * (half_units // CHUNK) + r, 0)),
    )
    new_dense = adam(
        zp_array, z_dense, (dense_weight, dense_first, dense_second), (width // 16) ** (-0.5), True,
        (2,),
        ((n_zh, 1, bw, half_width), lambda h, zp_: (0, 1 - (h ^ zp_[0]), 0, 0)),
        ((half_width, bw), lambda h, zp_: (h, 0)),
    )
    new_qkv = adam(
        zp_array, z_qkv, (qkv_weight, qkv_first, qkv_second), (width // 2) ** (-0.5), False,
        (3, 2),
        ((n_zh, 1, bw, half_width), lambda t, h, zp_: (0, 1 - (h ^ zp_[0]), 0, t)),
        ((1, bw, half_width), lambda t, h, zp_: (t, 0, h)),
    )
    outer_sum = jnp.concatenate([sums[:3], sums[2:3]], axis=0)
    hidden_sum = sums[3]
    head_sum = sums[4, : 3 * local_width].reshape(3, local_width)
    new_head = adam_update(head_bias, head_first, head_second, head_sum, VECTOR_RATE, 0.0)
    new_hidden = adam_update(
        hidden_bias, hidden_first, hidden_second, hidden_sum, VECTOR_RATE, 0.0
    )
    new_outer = adam_update(outer_params, outer_first, outer_second, outer_sum, VECTOR_RATE, 0.0)
    return (
        layer_out,
        input_grad,
        *new_qkv,
        *new_dense,
        *new_up,
        *new_down,
        *new_head,
        *new_hidden,
        *new_outer,
    )


def solution(mesh):
    n_zh = mesh.shape["dp"] // 4
    split = Mesh(mesh.devices.reshape(n_zh, 2, 2, 2, 2), ("zh", "zp", "y", "x", "c"))
    dp, mp = ("zh", "zp", "y"), ("x", "c")
    rows = P(dp + mp, None)
    qkv, dense, up, down = P(None, dp, mp), P(mp, dp), P(dp, mp), P(mp, dp)
    rest = (qkv,) * 3 + (dense,) * 3 + (up,) * 3 + (down,) * 3
    rest += (P(None, mp),) * 3 + (P(mp),) * 3 + (P(),) * 3
    return jax.shard_map(
        functools.partial(local, n_zh),
        mesh=split,
        in_specs=(rows, rows) + rest,
        out_specs=(rows, rows) + rest,
        check_vma=False,
    )
```

```python
import functools
import math

import jax
import jax.numpy as jnp
import numpy as np
from jax import lax
from jax.experimental import pallas as pl
from jax.experimental.pallas import tpu as pltpu
from jax.sharding import Mesh
from jax.sharding import PartitionSpec as P

HEAD = 64
ROT = 32
STEP = 10

BETA_ONE = 0.9
BETA_TWO = 0.999
ADAM_EPS = 1e-08
MATRIX_DECAY = 0.1
VECTOR_RATE = 0.1

F32 = jnp.float32
BF16 = jnp.bfloat16
MESH = pl.DeviceIdType.MESH
ANY = pl.BlockSpec(memory_space=pl.ANY)
VMEM_LIMIT = 63 * 1024 * 1024


RUNS = (
    (
        ("proj", 4), ("f1", 1), ("proj", 3), ("f1", 1), ("proj", 1), ("att", 1), ("f1", 1), ("att", 1),
        ("f0", 2), ("att", 1), ("f0", 1), ("att", 1), ("a1", 1),
    ),
    (
        ("act", 1), ("f0", 1), ("act", 4), ("ysET", 1), ("ysQKV", 1), ("act", 1), ("ysQKV", 1), ("a0", 1),
        ("slope", 1), ("act", 1), ("slope", 2), ("zsQKV", 1), ("ysQKV", 1), ("act", 1), ("slope", 1),
        ("zsQKV", 1), ("ysM", 1), ("slope", 1), ("ysET", 1), ("slope", 1), ("zsET", 1), ("zsQKV", 1),
        ("slope", 1), ("ysM", 1), ("slope", 1), ("ysM", 1),
    ),
    (
        ("zsM", 1), ("r0c", 1), ("zsET", 1), ("r0c", 3), ("zsM", 1), ("r0c", 4), ("r0x", 1), ("zsM", 1),
        ("r0x", 1), ("ysET", 1), ("ysM", 1), ("r0x", 1), ("zsET", 1), ("r0x", 1), ("r0z", 1), ("r1c", 1),
        ("ysM", 1), ("r1c", 2), ("r0z", 1), ("r1c", 1), ("ysM", 1), ("r1c", 1), ("zsM", 2), ("r1c", 3),
        ("r1x", 1), ("zsM", 1), ("r1x", 2), ("ysM", 1), ("r0f", 1), ("r1x", 1), ("r1z", 1), ("ysET", 1),
        ("ysM", 1), ("r0f", 1), ("r1z", 1), ("zsET", 1), ("vec", 1), ("zsM", 1), ("vec", 3), ("ysQKV", 1),
        ("vec", 1), ("zsM", 1), ("r1f", 1), ("vec", 1), ("r1f", 1), ("zsQKV", 1),
    ),
)
ORDER = [[name for name, times in part for _ in range(times)] for part in RUNS]

CHUNK = 256
RING = 2
LATER = 1
GELU = math.sqrt(2.0 / math.pi)
NT = (((1,), (1,)), ((), ()))
TN = (((0,), (0,)), ((), ()))


def at(index, size):
    return pl.ds(pl.multiple_of(index * size, size), size)


def block_kernel(
    n_zh,
    tok_in, c_in, down_in, up_in, dense_in, qkv_in,
    outer_ref, hidden_bias, head_bias, cos_ref, sin_ref,
    z_mlp, z_dense, z_qkv, y_mlp, y_dense, y_qkv, rows_in, grad_out, branch_out, sums_ref,
    rows2, mlp_w, dense_w, qkv_w, units2, heads3, heads1,
    dq_s, dk_s, dv_s, s_s, p_s, tok_s, stat_s, hidden_sum, head_sum, vec_s, vec_in,
    grads_s, qkv_stage, dense_stage, tile_stage, load_s, turned_s,
    w_send, w_recv, fwd_send, fwd_recv, a_send, a_recv, local_sem,
    ym_send, ym_recv, zm_send, zm_recv, yd_send, yd_recv, zd_send, zd_recv,
    yq_send, yq_recv, zq_send, zq_recv, tile_send, tile_recv, x_send, zt_send, load_sem, wide_sem, vec_send, vec_recv,
):
    zh, zp, y = lax.axis_index("zh"), lax.axis_index("zp"), lax.axis_index("y")
    x, c = lax.axis_index("x"), lax.axis_index("c")
    mp = x * 2 + c
    n = 2 * n_zh
    tok_rows, width = tok_in.shape
    _, bw, units = up_in.shape
    half_width = dense_in.shape[2]
    seq = 4 * tok_rows
    half = width // 2
    lanes = 2 * HEAD
    count = seq // CHUNK
    scale = HEAD ** (-0.5)

    def step(i):
        back = n - 1 - i
        if isinstance(back, int):
            return back // 2, back % 2
        return lax.div(back, 2), lax.rem(back, 2)

    def source_block(i):
        s, f = step(i)
        return lax.rem(zh - s + n_zh, n_zh) * 4 + (zp ^ f) * 2 + y

    def target(i):
        s, f = step(i)
        return {"zh": lax.rem(zh + s, n_zh), "zp": zp ^ f}

    def target_block(i):
        s, f = step(i)
        return lax.rem(zh + s, n_zh) * 4 + (zp ^ f) * 2

    to_y, to_x, to_c, to_zp = {"y": 1 - y}, {"x": 1 - x}, {"c": 1 - c}, {"zp": 1 - zp}
    barrier = pltpu.get_barrier_semaphore()
    partners = [target(i) for i in range(n - 1)] + [to_y, to_x, to_c]
    for partner in partners:
        pl.semaphore_signal(barrier, inc=1, device_id=partner, device_id_type=MESH)
    own = at(zp * 4 + mp, tok_rows)
    tok_load = pltpu.make_async_copy(tok_in, tok_s, load_sem.at[0])
    tok_load.start()
    pl.semaphore_wait(barrier, len(partners))

    def remote(src, dst, send, recv, to):
        return pltpu.make_async_remote_copy(
            src_ref=src, dst_ref=dst, send_sem=send, recv_sem=recv, device_id=to, device_id_type=MESH
        )


    me = source_block(n - 1)
    halves = (down_in, up_in, dense_in, qkv_in)

    pieces = (4, 4, 2, 4) if n_zh == 2 else (1, 1, 1, 1)

    def place(w, b, k=0, m=1):
        spot = at(b * m + k, bw // m)
        if w < 2:
            return mlp_w.at[w, spot, :]
        return (dense_w, qkv_w)[w - 2].at[spot, :]

    started = []

    def go(copy):
        copy.start()
        started.append(copy)

    def z_copy(w, i, k):
        m = pieces[w]
        src = halves[w].at[zp ^ step(i)[1], at(k, bw // m), :]
        return remote(src, place(w, me, k, m), w_send.at[w, i, k], w_recv.at[w, i, k], target(i))

    def y_copy(w, i, k=0):
        b = source_block(i)
        if i == n - 1:
            return remote(halves[w].at[zp], place(w, b), fwd_send.at[w, i, 0], fwd_recv.at[w, i, 0], to_y)
        spot = place(w, b, k, pieces[w])
        return remote(spot, spot, fwd_send.at[w, i, k], fwd_recv.at[w, i, k], to_y)

    def y_arrived(w):
        for i in range(n - 1):
            for k in range(pieces[w]):
                y_copy(w, i, k).wait_recv()
        y_copy(w, n - 1).wait_recv()

    own_rows = (c_in, rows2.at[1, own, :])

    def act_copy(k, stage, part):
        if stage == 0:
            slot, to, row, column = 0, to_zp, zp, mp
        else:
            row = zp ^ (part % 2)
            column = mp if part < 2 else (1 - x) * 2 + c
            slot, to = (1 + part, to_x) if stage == 1 else (3 + part, to_c)
        spot = rows2.at[k, at(row * 4 + column, tok_rows), :]
        src = own_rows[k] if stage == 0 or part == 0 else spot
        return remote(src, spot, a_send.at[k, slot], a_recv.at[k, slot], to)

    def locals_():
        return [pltpu.make_async_copy(c_in, rows2.at[0, own, :], local_sem.at[0])] + [
            pltpu.make_async_copy(halves[w].at[zp], place(w, me), local_sem.at[1 + w]) for w in range(4)
        ]

    def pass_on(k, stage, part):
        act_copy(k, stage, part).wait_recv()
        if stage == 0:
            go(act_copy(k, 1, 1))
            go(act_copy(k, 2, 1))
        else:
            go(act_copy(k, 2, 2 + part))

    inner = zh != zp if n_zh == 2 else zh < 0
    outer = jnp.logical_not(inner)

    def send_step(w, i, k):
        if i == 0:
            pl.when(outer)(z_copy(w, i, k).start)
        else:
            z_copy(w, i, k).start()

    def forward(w, i, k):
        z_copy(w, i, k).wait_recv()
        y_copy(w, i, k).start()

    def forward_step(w, i, k):
        if i == 0:
            pl.when(outer)(lambda: forward(w, i, k))
        else:
            forward(w, i, k)

    queue = (3, 2, 1, 0)
    order = [(w, k) for w in queue for k in range(pieces[w])]
    later = list(range(n - 2, -1, -1))
    go(act_copy(0, 0, 0))
    go(act_copy(0, 1, 0))

    @pl.when(inner)
    def _():
        for w, k in order:
            z_copy(w, 0, k).start()

    for w in queue:
        go(y_copy(w, n - 1))
    go(act_copy(0, 2, 0))
    for copy in locals_():
        copy.start()
    tok_load.wait()
    for j in range(tok_rows // 64):
        rows = pl.ds(j * 64, 64)
        values = tok_s[rows, :].astype(F32)
        mean = jnp.mean(values, axis=-1, keepdims=True)
        centred = values - mean
        inverse = lax.rsqrt(jnp.mean(centred * centred, axis=-1, keepdims=True) + 1e-05)
        stat_s[0, rows, :] = mean
        stat_s[1, rows, :] = inverse
        normed = centred * inverse * outer_ref[0:1, :] + outer_ref[1:2, :]
        rows2[1, at((zp * 4 + mp) * (tok_rows // 64) + j, 64), :] = normed.astype(BF16)
    go(act_copy(1, 0, 0))
    go(act_copy(1, 1, 0))
    go(act_copy(1, 2, 0))
    pl.when(inner)(lambda: forward(order[0][0], 0, order[0][1]))
    pass_on(0, 0, 0)
    pass_on(1, 0, 0)
    for w, k in order:
        for i in later:
            send_step(w, i, k)

    @pl.when(inner)
    def _():
        for w, k in order[1:]:
            forward(w, 0, k)

    pass_on(0, 1, 0)
    pass_on(1, 1, 0)
    def forward_pieces(w, start, stop):
        def one(piece, carry):
            for i in later:
                forward_step(w, i, piece)
            return carry

        lax.fori_loop(start, stop, one, 0)

    forward_pieces(3, 0, pieces[3])
    pass_on(0, 1, 1)
    forward_pieces(2, 0, pieces[2])
    pass_on(1, 1, 1)
    forward_pieces(1, 0, pieces[1] // 4)
    for copy in locals_():
        copy.wait()
    for k in (0, 1):
        for part in range(4):
            act_copy(k, 2, part).wait_recv()
    y_arrived(3)
    y_arrived(2)
    tiles = 2 * seq // CHUNK


    def low_rows(r):
        return at(n * bw // CHUNK + r, CHUNK)

    def bent(hidden):
        square = hidden * hidden
        return square, jnp.tanh(GELU * (hidden * (1.0 + 0.044715 * square)))

    def act_tile(r, carry):
        rows = at(r, CHUNK)
        for j in range(units // CHUNK):
            cols = pl.ds(j * CHUNK, CHUNK)
            hidden = jnp.dot(rows2[1, rows, :], mlp_w[1, :, cols], preferred_element_type=F32)
            hidden = hidden + hidden_bias[:, cols]
            high = hidden.astype(BF16)
            units2[1, rows, cols] = high
            grads_s[low_rows(r), cols] = (hidden - high.astype(F32)).astype(BF16)
            _, tanh = bent(hidden)
            units2[0, rows, cols] = (0.5 * hidden * (1.0 + tanh)).astype(BF16)
        return carry

    def slope_tile(r, carry):
        rows = at(r, CHUNK)
        for j in range(units // CHUNK):
            cols = pl.ds(j * CHUNK, CHUNK)
            hidden = units2[1, rows, cols].astype(F32) + grads_s[low_rows(r), cols].astype(F32)
            square, tanh = bent(hidden)
            grad = jnp.dot(rows2[0, rows, :], mlp_w[0, :, cols], preferred_element_type=F32)
            slope = 0.5 * (1.0 + tanh) + 0.5 * hidden * (1.0 - tanh * tanh) * (
                GELU * (1.0 + 3.0 * 0.044715 * square)
            )
            low = (grad * slope).astype(BF16)
            units2[1, rows, cols] = low
            hidden_sum[:, cols] += jnp.sum(low.astype(F32), axis=0, keepdims=True)
        return carry

    for w in range(4):
        for i in range(n - 1):
            for k in range(pieces[w]):
                started.extend([z_copy(w, i, k), y_copy(w, i, k)])


    low_lane = lax.broadcasted_iota(jnp.int32, (1, lanes), 1) % HEAD < ROT // 2

    def turn(values, rows, sign):
        after = pltpu.roll(values, lanes - ROT // 2, 1)
        before = pltpu.roll(values, ROT // 2, 1)
        return values * cos_ref[rows, :] + jnp.where(low_lane, after, before) * (sign * sin_ref[rows, :])

    def proj_tile(r, carry):
        rows = at(r, CHUNK)
        where = at(lax.rem(r, count), CHUNK)
        for t in range(3):
            cols = pl.ds(t * half_width, half_width)
            proj = jnp.dot(rows2[1, rows, :], qkv_w[:, cols], preferred_element_type=F32) + head_bias[:, cols]
            for g in range(half_width // lanes):
                part = proj[:, g * lanes : (g + 1) * lanes]
                if t < 2:
                    part = turn(part, where, 1.0)
                heads3[rows, pl.ds(t * half_width + g * lanes, lanes)] = part.astype(BF16)
        heads1[rows, :] = jnp.dot(rows2[0, rows, :], dense_w[...], preferred_element_type=F32).astype(BF16)
        return carry


    first = lax.broadcasted_iota(jnp.int32, (1, lanes), 1) < HEAD
    pairs = half_width // lanes

    def attend(it, carry):
        base = lax.div(it, pairs) * count
        hp = lax.rem(it, pairs)

        def cols(t):
            return at(t * pairs + hp, lanes)

        here = at(hp, lanes)
        dk_s[...] = jnp.zeros_like(dk_s)
        dv_s[...] = jnp.zeros_like(dv_s)
        diagonal = lax.broadcasted_iota(jnp.int32, (CHUNK, CHUNK), 0) <= lax.broadcasted_iota(
            jnp.int32, (CHUNK, CHUNK), 1
        )
        for qb in range(count):
            rows = at(base + qb, CHUNK)
            q_rows = heads3[rows, cols(0)] * jnp.asarray(scale, BF16)
            g_rows = heads1[rows, here]
            mixed_halves, dq_halves = [], []
            for h in (0, 1):
                mine = first if h == 0 else jnp.logical_not(first)
                q_one = jnp.where(mine, q_rows, jnp.zeros_like(q_rows))
                g_one = jnp.where(mine, g_rows, jnp.zeros_like(g_rows))
                top = None
                for j in range(qb + 1):
                    keys = heads3[at(base + j, CHUNK), cols(1)]
                    scores = lax.dot_general(keys, q_one, NT, preferred_element_type=F32)
                    if j == qb:
                        scores = jnp.where(diagonal, scores, -1e30)
                    s_s[j] = scores
                    peak = jnp.max(scores, axis=0, keepdims=True)
                    top = peak if top is None else jnp.maximum(top, peak)
                total = None
                for j in range(qb + 1):
                    e = jnp.exp(s_s[j] - top)
                    s_s[j] = e
                    part = jnp.sum(e, axis=0, keepdims=True)
                    total = part if total is None else total + part
                inverse = 1.0 / total
                mixed, inner = None, None
                for j in range(qb + 1):
                    values = heads3[at(base + j, CHUNK), cols(2)]
                    probs = s_s[j] * inverse
                    low = probs.astype(BF16)
                    part = lax.dot_general(low, values, TN, preferred_element_type=F32)
                    mixed = part if mixed is None else mixed + part
                    dv_s[h, pl.ds(j * CHUNK, CHUNK), :] += jnp.dot(low, g_rows, preferred_element_type=F32)
                    grad_probs = lax.dot_general(values, g_one, NT, preferred_element_type=F32)
                    s_s[j] = probs
                    p_s[j] = grad_probs
                    part = jnp.sum(probs * grad_probs, axis=0, keepdims=True)
                    inner = part if inner is None else inner + part
                dq = None
                for j in range(qb + 1):
                    keys = heads3[at(base + j, CHUNK), cols(1)]
                    grad_scores = (s_s[j] * (p_s[j] - inner)).astype(BF16)
                    part = lax.dot_general(grad_scores, keys, TN, preferred_element_type=F32)
                    dq = part if dq is None else dq + part
                    dk_s[h, pl.ds(j * CHUNK, CHUNK), :] += jnp.dot(
                        grad_scores, q_rows, preferred_element_type=F32
                    )
                mixed_halves.append(mixed)
                dq_halves.append(dq)
            heads1[rows, here] = jnp.where(first, *mixed_halves).astype(BF16)
            dq_s[pl.ds(qb * CHUNK, CHUNK), :] = jnp.where(first, *dq_halves) * scale
        for qb in range(count):
            rows = pl.ds(qb * CHUNK, CHUNK)
            gq = turn(dq_s[rows, :], rows, -1.0)
            gk = turn(jnp.where(first, dk_s[0, rows, :], dk_s[1, rows, :]), rows, -1.0)
            gv = jnp.where(first, dv_s[0, rows, :], dv_s[1, rows, :])
            for t, g in enumerate((gq, gk, gv)):
                low = g.astype(BF16)
                heads3[at(base + qb, CHUNK), cols(t)] = low
                head_sum[:, cols(t)] += jnp.sum(low.astype(F32), axis=0, keepdims=True)
        return carry


    def weight_grad(left, right, b, put):
        wide = max(bw, 128)
        turned = turned_s.at[pl.ds(0, wide), :]
        if bw == wide:
            turned[...] = left[:, at(b, bw)].T
        else:
            turned[...] = left[:, at(lax.div(b, wide // bw), wide)].T
        for j in range(right.shape[1] // CHUNK):
            cols = pl.ds(j * CHUNK, CHUNK)
            value = jnp.dot(turned[...], right[:, cols], preferred_element_type=F32)
            if bw < wide:
                spot = lax.rem(b, wide // bw)
                value = sum(
                    jnp.where(spot == k, value[k * bw : (k + 1) * bw], 0.0) for k in range(wide // bw)
                )
            put(cols, value)

    def mlp_grad(w, b, put):
        weight_grad(rows2.at[w], units2.at[w], b, put)

    def ym_copy(k):
        w, i = lax.div(k, n), lax.rem(k, n)
        return remote(grads_s.at[at(k, bw), :], y_mlp.at[w, i], ym_send.at[k], ym_recv.at[k], to_y)

    def ym_step(k, carry):
        w, i = lax.div(k, n), lax.rem(k, n)

        def put(cols, value):
            grads_s[at(k, bw), cols] = value.astype(BF16)

        mlp_grad(w, target_block(i) + 1 - y, put)
        ym_copy(k).start()
        return carry


    def zm_copy(k):
        w, i = lax.div(k, n), lax.rem(k, n)
        return remote(grads_s.at[at(2 * n + i, bw), :], z_mlp.at[w, i], zm_send.at[i], zm_recv.at[k], target(i))

    def zm_local(k):
        w, i = lax.div(k, n), lax.rem(k, n)
        return pltpu.make_async_copy(grads_s.at[at(2 * n + i, bw), :], z_mlp.at[w, i], zm_send.at[i])

    def zm_step(k, carry):
        w, i = lax.div(k, n), lax.rem(k, n)
        ym_copy(k).wait_recv()
        load = pltpu.make_async_copy(y_mlp.at[w, i], load_s.at[0, pl.ds(0, bw), :], load_sem.at[0])
        load.start()

        @pl.when((k >= n) & (i < n - 1))
        def _():
            zm_copy(k - n).wait_send()

        @pl.when((k >= n) & (i == n - 1))
        def _():
            zm_local(k - n).wait()

        load.wait()

        def put(cols, value):
            grads_s[at(2 * n + i, bw), cols] = (value + load_s[0, pl.ds(0, bw), cols].astype(F32)).astype(BF16)

        mlp_grad(w, target_block(i) + y, put)

        @pl.when(i < n - 1)
        def _():
            zm_copy(k).start()

        @pl.when(i == n - 1)
        def _():
            zm_local(k).start()

        return carry


    def small(left, right, y_buf, z_buf, held, ys, yr, zs, zr):
        cols = held.shape[2]

        def y_copy_(i):
            return remote(held.at[i], y_buf.at[i], ys.at[i], yr.at[i], to_y)

        def z_copy_(i):
            return remote(held.at[i], z_buf.at[i], zs.at[i], zr.at[i], target(i))

        def z_local(i):
            return pltpu.make_async_copy(held.at[i], z_buf.at[i], zs.at[i])

        def y_step(i, carry):
            def put(at_cols, value):
                held[i, :, at_cols] = value.astype(BF16)

            weight_grad(left, right, target_block(i) + 1 - y, put)
            y_copy_(i).start()
            return carry

        def z_step(i, carry):
            y_copy_(i).wait_recv()
            spot = load_s.at[0, pl.ds(0, bw), pl.ds(0, cols)]
            load = pltpu.make_async_copy(y_buf.at[i], spot, load_sem.at[0])
            load.start()
            y_copy_(i).wait_send()
            load.wait()

            def put(at_cols, value):
                held[i, :, at_cols] = (value + spot[:, at_cols].astype(F32)).astype(BF16)

            weight_grad(left, right, target_block(i) + y, put)

            @pl.when(i < n - 1)
            def _():
                z_copy_(i).start()

            @pl.when(i == n - 1)
            def _():
                z_local(i).start()

            return carry

        def finish(i, carry):
            @pl.when(i < n - 1)
            def _():
                z_copy_(i).wait_send()
                z_copy_(i).wait_recv()

            @pl.when(i == n - 1)
            def _():
                z_local(i).wait()

            return carry

        return y_step, z_step, finish

    dense_steps = small(
        rows2.at[0], heads1, y_dense, z_dense, dense_stage, yd_send, yd_recv, zd_send, zd_recv
    )
    qkv_steps = small(
        rows2.at[1], heads3, y_qkv, z_qkv, qkv_stage, yq_send, yq_recv, zq_send, zq_recv
    )


    def tile_copy(kind, slot, sem, index, to):
        return remote(
            tile_stage.at[slot], rows_in.at[kind, index], sem, tile_recv.at[kind, index], to
        )

    def c_copy(kind, t, index):
        slot = lax.rem(t, RING)
        return tile_copy(kind, slot, tile_send.at[slot], index, to_c)

    def x_copy(kind, t, index):
        return tile_copy(kind, RING + t, x_send.at[t], index, to_x)

    def zt_copy(kind, h, index):
        return tile_copy(kind, RING + h, zt_send.at[h], index, to_zp)

    def row_tiles(kind, stage):
        left, left_w = units2.at[1 - kind], mlp_w.at[1 - kind]
        right, right_w = ((heads3, qkv_w), (heads1, dense_w))[kind]

        def one(t):
            h = lax.rem(t, 2)
            if stage == 0:
                zq, xq = zp ^ (1 - lax.rem(lax.div(t, 2), 2)), x ^ (1 - lax.div(t, 4))
                block, come, to, index = zq * 4 + xq * 2 + 1 - c, (), to_c, zq * 4 + xq * 2 + h
            elif stage == 1:
                zq = zp ^ (1 - lax.div(t, 2))
                block, to, index = zq * 4 + (1 - x) * 2 + c, to_x, 8 + zq * 2 + h
                come = (zq * 4 + (1 - x) * 2 + h,)
            elif stage == 2:
                block, to, index = (1 - zp) * 4 + x * 2 + c, to_zp, 12 + h
                come = ((1 - zp) * 4 + x * 2 + h, 8 + (1 - zp) * 2 + h)
            else:
                block, to, index = zp * 4 + x * 2 + c, None, None
                come = (zp * 4 + x * 2 + h, 8 + zp * 2 + h, 12 + h)
            loads = []
            for slot, (spot, back) in enumerate(zip(come, (to_c, to_x, to_zp))):
                tile_copy(kind, 0, tile_send.at[0], spot, back).wait_recv()
                loads.append(
                    pltpu.make_async_copy(rows_in.at[kind, spot], load_s.at[slot], load_sem.at[slot])
                )
                loads[-1].start()
            for load in loads:
                load.wait()
            rows = at(block, tok_rows)
            if stage == 0:
                spot, copy = tile_stage.at[lax.rem(t, RING)], c_copy(kind, t, index)
                if kind == LATER:
                    copy.wait_send()
                else:
                    pl.when(t >= RING)(copy.wait_send)
            elif stage == 1:
                spot, copy = tile_stage.at[RING + t], x_copy(kind, t, index)
                if kind == LATER:
                    pl.when(t < 2)(zt_copy(kind, lax.rem(t, 2), index).wait_send)
                    pl.when(t >= 2)(copy.wait_send)
            elif stage == 2:
                spot, copy = tile_stage.at[RING + h], zt_copy(kind, h, index)
                x_copy(kind, h, index).wait_send()
            for j in range(half // CHUNK):
                cols = pl.ds(j * CHUNK, CHUNK)
                model = at(h * (half // CHUNK) + j, CHUNK)
                value = lax.dot_general(left[rows, :], left_w[model, :], NT, preferred_element_type=F32)
                value += lax.dot_general(right[rows, :], right_w[model, :], NT, preferred_element_type=F32)
                for k in range(len(loads)):
                    value += load_s[k, :, cols].astype(F32)
                if stage < 3:
                    spot[:, cols] = value.astype(BF16)
                else:
                    s_s[j] = value
                    if kind == 0:
                        xhat = (tok_s[:, model].astype(F32) - stat_s[0]) * stat_s[1]
                        back = rows2[0, own, model].astype(F32)
                        for row, term in enumerate((value * xhat, value, back)):
                            vec_s[row : row + 1, model] = jnp.sum(term, axis=0, keepdims=True)
            if stage < 3:
                copy.start()
            else:
                out = (grad_out, branch_out)[kind]
                copies = [
                    pltpu.make_async_copy(
                        s_s.at[j], out.at[:, at(h * (half // CHUNK) + j, CHUNK)], wide_sem.at[j]
                    )
                    for j in range(half // CHUNK)
                ]
                for copy in copies:
                    copy.start()
                for copy in copies:
                    copy.wait()

        return one


    hops = [to_zp, to_y]
    bit = 1
    while bit < n_zh:
        hops.append({"zh": zh ^ bit})
        bit *= 2
    dp_hops = len(hops)
    hops += [to_c, to_x]

    def vec_copy(k):
        return remote(vec_s, vec_in.at[k], vec_send.at[k], vec_recv.at[k], hops[k])

    def vec_first():
        for row in (3, 4):
            vec_s[row : row + 1, :] = jnp.zeros((1, width), F32)
        vec_s[3:4, at(zp, units)] = hidden_sum[...]
        for t in range(3):
            vec_s[4:5, at(t * 2 + zp, half_width)] = head_sum[:, pl.ds(t * half_width, half_width)]
        vec_copy(0).start()

    def vec_next(k):
        vec_copy(k).wait()
        vec_s[...] += vec_in[k]
        if k + 1 == dp_hops:
            sums_ref[3:5, :] = vec_s[3:5, :]
        if k + 1 < len(hops):
            vec_copy(k + 1).start()
        else:
            sums_ref[0:3, :] = vec_s[0:3, :]


    def steps(step_, total, parts):
        def share(q):
            if total == parts:
                step_(q, 0)
            else:
                lax.fori_loop(q * total // parts, (q + 1) * total // parts, step_, 0)

        return share

    def pieces_of(w):
        m = pieces[w]
        return lambda q: forward_pieces(w, lax.div(q * m, 4), lax.div((q + 1) * m, 4))

    def vector_hop(q):
        pl.when(q == 0)(vec_first)
        for k in range(5):
            @pl.when(q == k + 1)
            def _():
                for hop in range(k, len(hops) if k == 4 else k + 1):
                    vec_next(hop)

    tasks = {
        "f1": pieces_of(1),
        "f0": pieces_of(0),
        "a1": lambda q: y_arrived(1),
        "a0": lambda q: y_arrived(0),
        "proj": steps(proj_tile, tiles, 8),
        "att": steps(attend, 2 * pairs, 4),
        "act": steps(act_tile, tiles, 8),
        "slope": steps(slope_tile, tiles, 8),
        "ysET": steps(dense_steps[0], n, 4),
        "zsET": steps(dense_steps[1], n, 4),
        "ysQKV": steps(qkv_steps[0], n, 4),
        "zsQKV": steps(qkv_steps[1], n, 4),
        "ysM": steps(ym_step, 2 * n, 8),
        "zsM": steps(zm_step, 2 * n, 8),
        "vec": vector_hop,
    }
    for kind in (0, 1):
        for stage, letter in enumerate("cxzf"):
            tasks[f"r{kind}{letter}"] = row_tiles(kind, stage)

    def dispatch(part, seen):
        names = list(dict.fromkeys(part))

        def one(now, carry):
            for name in names:
                spots = [k for k, other in enumerate(part) if other == name]
                mine = functools.reduce(jnp.logical_or, [now == k for k in spots])
                q = seen[name] + sum((now >= k).astype(jnp.int32) for k in spots[1:])
                pl.when(mine)(functools.partial(tasks[name], q))
            return carry

        lax.fori_loop(0, len(part), one, 0)

    hidden_sum[...] = jnp.zeros_like(hidden_sum)
    head_sum[...] = jnp.zeros_like(head_sum)
    seen = dict.fromkeys(tasks, 0)
    seen["f1"] = 1
    for part in ORDER:
        dispatch(part, dict(seen))
        for name in part:
            seen[name] += 1

    def finish_y(k, carry):
        ym_copy(k).wait_send()
        return carry


    for copy in started:
        copy.wait_send()

    def finish_z(k, carry):
        i = lax.rem(k, n)

        @pl.when(i < n - 1)
        def _():
            zm_copy(k).wait_recv()

        @pl.when((k >= n) & (i < n - 1))
        def _():
            zm_copy(k).wait_send()

        @pl.when((k >= n) & (i == n - 1))
        def _():
            zm_local(k).wait()

        return carry

    lax.fori_loop(0, 2 * n, finish_y, 0)
    lax.fori_loop(0, 2 * n, finish_z, 0)
    for slot in range(RING):
        c_copy(0, slot, 0).wait_send()
    for t in (0, 1):
        zt_copy(0, t, 0).wait_send()
        x_copy(0, 2 + t, 0).wait_send()
    lax.fori_loop(0, n, dense_steps[2], 0)
    lax.fori_loop(0, n, qkv_steps[2], 0)


def block(n_zh, tokens, cotangent, halves, outer_params, hidden_bias, head_bias, tables):
    tok_rows, width = tokens.shape
    n = 2 * n_zh
    dp = 2 * n
    bw = width // dp
    units = halves[1].shape[2]
    half_width = halves[2].shape[2]
    triple = 3 * half_width
    seq = 4 * tok_rows
    count = seq // CHUNK
    hops = 4 + (n_zh - 1).bit_length()
    shape = jax.ShapeDtypeStruct
    vmem = pl.BlockSpec(memory_space=pltpu.VMEM)
    dma = pltpu.SemaphoreType.DMA
    outs = [
        shape((2, n, bw, units), BF16),
        shape((n, bw, half_width), BF16),
        shape((n, bw, triple), BF16),
        shape((2, n, bw, units), BF16),
        shape((n, bw, half_width), BF16),
        shape((n, bw, triple), BF16),
        shape((2, 14, tok_rows, width // 2), BF16),
        shape((tok_rows, width), F32),
        shape((tok_rows, width), F32),
        shape((8, width), F32),
    ]
    scratch = [
        pltpu.VMEM((2, 2 * seq, width), BF16),
        pltpu.VMEM((2, width, units), BF16),
        pltpu.VMEM((width, half_width), BF16),
        pltpu.VMEM((width, triple), BF16),
        pltpu.VMEM((2, 2 * seq, units), BF16),
        pltpu.VMEM((2 * seq, triple), BF16),
        pltpu.VMEM((2 * seq, half_width), BF16),
        pltpu.VMEM((seq, 2 * HEAD), F32),
        pltpu.VMEM((2, seq, 2 * HEAD), F32),
        pltpu.VMEM((2, seq, 2 * HEAD), F32),
        pltpu.VMEM((count, CHUNK, CHUNK), F32),
        pltpu.VMEM((count, CHUNK, CHUNK), F32),
        pltpu.VMEM((tok_rows, width), BF16),
        pltpu.VMEM((2, tok_rows, 1), F32),
        pltpu.VMEM((1, units), F32),
        pltpu.VMEM((1, triple), F32),
        pltpu.VMEM((8, width), F32),
        pltpu.VMEM((hops, 8, width), F32),
        pltpu.VMEM((3 * n * bw, units), BF16),
        pltpu.VMEM((n, bw, triple), BF16),
        pltpu.VMEM((n, bw, half_width), BF16),
        pltpu.VMEM((RING + 4, tok_rows, width // 2), BF16),
        pltpu.VMEM((3, tok_rows, width // 2), BF16),
        pltpu.VMEM((max(bw, 128), 2 * seq), BF16),
        dma((4, n, 4)), dma((4, n, 4)), dma((4, n, 4)), dma((4, n, 4)), dma((2, 7)), dma((2, 7)), dma((6,)),
        dma((2 * n,)), dma((2 * n,)), dma((n,)), dma((2 * n,)),
        dma((n,)), dma((n,)), dma((n,)), dma((n,)),
        dma((n,)), dma((n,)), dma((n,)), dma((n,)),
        dma((RING,)), dma((2, 14)), dma((4,)), dma((2,)), dma((3,)), dma((width // 2 // CHUNK,)), dma((hops,)), dma((hops,)),
    ]
    return pl.pallas_call(
        functools.partial(block_kernel, n_zh),
        out_shape=outs,
        in_specs=[ANY] * 6 + [vmem] * 5,
        out_specs=[ANY] * 9 + [vmem],
        scratch_shapes=scratch,
        compiler_params=pltpu.CompilerParams(
            collective_id=0, has_side_effects=True, vmem_limit_bytes=VMEM_LIMIT
        ),
    )(tokens, cotangent, *halves, outer_params, hidden_bias, head_bias, *tables)


def rotation_tables(seq):
    lane = np.arange(2 * HEAD) % HEAD
    exponent = (lane % (ROT // 2)).astype(np.float32) * np.float32(2.0 / ROT)
    inverse = np.exp(np.float32(-math.log(10000.0)) * exponent).astype(np.float32)
    angles = np.arange(seq, dtype=np.float32)[:, None] * inverse[None, :]
    cos = np.cos(angles.astype(np.float64)).astype(np.float32)
    sin = np.sin(angles.astype(np.float64)).astype(np.float32)
    turned, low = lane < ROT, lane < ROT // 2
    zero = np.zeros_like(sin)
    return np.where(turned, cos, zero + 1), np.where(turned, np.where(low, -sin, sin), zero)


def adam_update(weight, moment_one, moment_two, gradient, step_rate, decay_rate):
    first_new = BETA_ONE * moment_one + (1.0 - BETA_ONE) * gradient
    second_new = BETA_TWO * moment_two + (1.0 - BETA_TWO) * gradient * gradient
    normalized = (
        first_new
        / (1.0 - BETA_ONE**STEP)
        / (jnp.sqrt(second_new / (1.0 - BETA_TWO**STEP)) + ADAM_EPS)
    )
    return (weight - step_rate * (normalized + decay_rate * weight), first_new, second_new)


def adam_kernel(rate, turned, zp_ref, parts_ref, w_ref, one_ref, two_ref, *outs):
    parts = parts_ref[...].astype(F32)
    rows, cols = parts.shape[-2:]
    gradient = jnp.sum(parts.reshape(-1, rows, cols), axis=0)
    if turned:
        gradient = gradient.T
    shape = w_ref.shape
    new = adam_update(
        w_ref[...].reshape(gradient.shape), one_ref[...].reshape(gradient.shape),
        two_ref[...].reshape(gradient.shape), gradient, rate, MATRIX_DECAY,
    )
    for out, value in zip(outs, new):
        out[...] = value.reshape(shape)


def adam(zp, parts, state, rate, turned, grid, parts_spec, state_spec):
    shape = jax.ShapeDtypeStruct(state[0].shape, F32)
    spec = pl.BlockSpec(*state_spec)
    return pl.pallas_call(
        functools.partial(adam_kernel, rate, turned),
        out_shape=[shape] * 3,
        grid_spec=pltpu.PrefetchScalarGridSpec(
            num_scalar_prefetch=1,
            grid=grid,
            in_specs=[pl.BlockSpec(*parts_spec)] + [spec] * 3,
            out_specs=[spec] * 3,
        ),
        compiler_params=pltpu.CompilerParams(vmem_limit_bytes=VMEM_LIMIT),
    )(zp, parts, *state)


def finish_kernel(tok_ref, back_ref, grad_ref, branch_ref, outer_ref, out_ref, in_ref):
    values = tok_ref[...].astype(F32)
    out_ref[...] = (values + branch_ref[...] + outer_ref[2:3, :] + outer_ref[3:4, :]).astype(BF16)
    mean = jnp.mean(values, axis=-1, keepdims=True)
    centred = values - mean
    inverse = lax.rsqrt(jnp.mean(centred * centred, axis=-1, keepdims=True) + 1e-05)
    xhat = centred * inverse
    g = grad_ref[...] * outer_ref[0:1, :]
    inner = g - jnp.mean(g, axis=-1, keepdims=True) - xhat * jnp.mean(g * xhat, axis=-1, keepdims=True)
    in_ref[...] = back_ref[...].astype(F32) + inverse * inner


def finish(tokens, cotangent, grad_normed, branch, outer_params):
    rows, width = tokens.shape
    tile = rows // 2
    spec = pl.BlockSpec((tile, width), lambda i: (i, 0))
    return pl.pallas_call(
        finish_kernel,
        grid=(rows // tile,),
        out_shape=[jax.ShapeDtypeStruct((rows, width), BF16), jax.ShapeDtypeStruct((rows, width), F32)],
        in_specs=[spec] * 4 + [pl.BlockSpec(outer_params.shape, lambda i: (0, 0))],
        out_specs=[spec] * 2,
        compiler_params=pltpu.CompilerParams(vmem_limit_bytes=VMEM_LIMIT),
    )(tokens, cotangent, grad_normed, branch, outer_params)


def pick(value, index, axis):
    return lax.dynamic_index_in_dim(value, index, axis, keepdims=False)


def local(
    n_zh,
    tokens, cotangent,
    qkv_weight, qkv_first, qkv_second,
    dense_weight, dense_first, dense_second,
    up_weight, up_first, up_second,
    down_weight, down_first, down_second,
    head_bias, head_first, head_second,
    hidden_bias, hidden_first, hidden_second,
    outer_params, outer_first, outer_second,
):
    zp = lax.axis_index("zp")
    tok_rows, width = tokens.shape
    seq_rows = tok_rows * 4
    bw = qkv_weight.shape[1]
    local_width = qkv_weight.shape[2]
    half_width = local_width // 2
    half_units = up_weight.shape[1] // 2

    qkv_rows = qkv_weight.reshape(3, bw, 2, half_width).transpose(2, 1, 0, 3)
    qkv_rows = qkv_rows.reshape(2, bw, 3 * half_width).astype(BF16)
    dense_rows = dense_weight.reshape(2, half_width, bw).swapaxes(1, 2).astype(BF16)
    up_rows = up_weight.reshape(bw, 2, half_units).swapaxes(0, 1).astype(BF16)
    down_rows = down_weight.reshape(2, half_units, bw).swapaxes(1, 2).astype(BF16)
    bias_half = pick(hidden_bias.reshape(2, 1, half_units), zp, 0)
    head_half = pick(head_bias.reshape(3, 2, half_width), zp, 1).reshape(1, 3 * half_width)
    outs = block(
        n_zh, tokens, cotangent, (down_rows, up_rows, dense_rows, qkv_rows), outer_params,
        bias_half, head_half, rotation_tables(seq_rows),
    )
    z_mlp, z_dense, z_qkv = outs[:3]
    grad_normed, branch, sums = outs[7:]
    layer_out, input_grad = finish(tokens, cotangent, grad_normed, branch, outer_params)

    zp_array = jnp.reshape(zp, (1,))
    z_mlp = z_mlp.reshape(2, n_zh, 2, bw, half_units)
    z_dense = z_dense.reshape(n_zh, 2, bw, half_width)
    z_qkv = z_qkv.reshape(n_zh, 2, bw, 3 * half_width)
    tile = bw
    new_up = adam(
        zp_array, z_mlp, (up_weight, up_first, up_second), width ** (-0.5), False,
        (2, bw // tile),
        ((1, n_zh, 1, tile, half_units), lambda h, r, zp_: (1, 0, 1 - (h ^ zp_[0]), r, 0)),
        ((tile, half_units), lambda h, r, zp_: (r, h)),
    )
    new_down = adam(
        zp_array, z_mlp, (down_weight, down_first, down_second), (4 * width) ** (-0.5), True,
        (2, half_units // (2 * CHUNK)),
        ((1, n_zh, 1, bw, 2 * CHUNK), lambda h, r, zp_: (0, 0, 1 - (h ^ zp_[0]), 0, r)),
        ((2 * CHUNK, bw), lambda h, r, zp_: (h * (half_units // (2 * CHUNK)) + r, 0)),
    )
    new_dense = adam(
        zp_array, z_dense, (dense_weight, dense_first, dense_second), (width // 16) ** (-0.5), True,
        (2,),
        ((n_zh, 1, bw, half_width), lambda h, zp_: (0, 1 - (h ^ zp_[0]), 0, 0)),
        ((half_width, bw), lambda h, zp_: (h, 0)),
    )
    new_qkv = adam(
        zp_array, z_qkv, (qkv_weight, qkv_first, qkv_second), (width // 2) ** (-0.5), False,
        (3, 2),
        ((n_zh, 1, bw, half_width), lambda t, h, zp_: (0, 1 - (h ^ zp_[0]), 0, t)),
        ((1, bw, half_width), lambda t, h, zp_: (t, 0, h)),
    )
    outer_sum = jnp.concatenate([sums[:3], sums[2:3]], axis=0)
    hidden_sum = sums[3]
    head_sum = sums[4, : 3 * local_width].reshape(3, local_width)
    new_head = adam_update(head_bias, head_first, head_second, head_sum, VECTOR_RATE, 0.0)
    new_hidden = adam_update(
        hidden_bias, hidden_first, hidden_second, hidden_sum, VECTOR_RATE, 0.0
    )
    new_outer = adam_update(outer_params, outer_first, outer_second, outer_sum, VECTOR_RATE, 0.0)
    return (
        layer_out,
        input_grad,
        *new_qkv,
        *new_dense,
        *new_up,
        *new_down,
        *new_head,
        *new_hidden,
        *new_outer,
    )


def solution(mesh):
    n_zh = mesh.shape["dp"] // 4
    split = Mesh(mesh.devices.reshape(n_zh, 2, 2, 2, 2), ("zh", "zp", "y", "x", "c"))
    dp, mp = ("zh", "zp", "y"), ("x", "c")
    rows = P(dp + mp, None)
    qkv, dense, up, down = P(None, dp, mp), P(mp, dp), P(dp, mp), P(mp, dp)
    rest = (qkv,) * 3 + (dense,) * 3 + (up,) * 3 + (down,) * 3
    rest += (P(None, mp),) * 3 + (P(mp),) * 3 + (P(),) * 3
    return jax.shard_map(
        functools.partial(local, n_zh),
        mesh=split,
        in_specs=(rows, rows) + rest,
        out_specs=(rows, rows) + rest,
        check_vma=False,
    )
```
